32 devices in a mesh: dp: 8 (over z, x), mp: 4 (over y, core).
Axes of the slice: x: 2, y: 2, z: 4, core: 2. Of those that a mesh axis runs over, the one named last changes fastest.
Arguments:
- features: bfloat16 [256, 32, 512], P(('dp', 'mp')), may hold values from -6 to 6
- lengths: int32 [256], P(('dp', 'mp')), may hold values from 1 to 7, as said below
- dests: int32 [256], P(('dp', 'mp')), may hold values from 0 to 7, as said below
- offsets: int32 [256], P(('dp', 'mp')), may hold values from 0 to 127, as said below
- conv_weight: bfloat16 [2, 1024, 512], replicated, may hold values from -0.1875 to 0.1875
- norm_gain: float32 [2, 512], replicated, may hold values from 0.1 to 1.9
- norm_shift: float32 [2, 512], replicated, may hold values from -3 to 3
- proj_weight: bfloat16 [512, 1280], P(None, 'mp'), may hold values from -0.25 to 0.25
- grad_packed: bfloat16 [1024, 1280], P('dp', 'mp'), may hold values from -6 to 6
Outputs:
- packed: bfloat16 [1024, 1280], P('dp', 'mp')
- grad_features: bfloat16 [256, 32, 512], P(('dp', 'mp'))
- grad_conv: float32 [2, 1024, 512], P(None, ('dp', 'mp'))
- grad_norm: float32 [2, 1024], P(None, ('dp', 'mp'))
- grad_proj: float32 [512, 1280], P('dp', 'mp')
The draws below stay inside these ranges and needn't reach their ends.
Inputs may be any that keep to these rules, and one draw needn't show every extreme that they name: Utterances 2k and 2k+1 of each device form a pair whose lengths sum to 8. `dests`: both utterances of a pair name the same shard; the 4 pairs of one device name different shards, and every shard is named by exactly 16 pairs. A pair fills one aligned block of 8 rows of its shard that no other pair uses: the first utterance starts at offsets[2k], a multiple of 8, and the second at offsets[2k] + lengths[2k].
All inputs are finite; a program needn't handle non-finite values.
Results may differ from the reference program's by a relative error of at most 0.015.
Values may be sent and summed in bfloat16 or wider, within the bound.
No kernel may reach another device: no remote copies, remote signals or barrier semaphores. Data moves between devices by JAX's collectives and lax.ppermute only.
A program may use at most 64 MiB of HBM per device.

```python
import jax
import jax.numpy as jnp
from jax import lax

C = 512
HID = 1280
LAYERS = 2
FU = 8
GROUPS = 4
UTT_DEV = 8
BLOCKS = 16
ROWS = 128
UTTS = 256
SEQ_ROWS = 1024


def pair_plan(key):
    dp_total = 2 * GROUPS
    device_total = UTTS // UTT_DEV
    mp_total = device_total // dp_total
    shuffled = jax.random.permutation(jax.random.fold_in(key, 101), device_total).astype(jnp.int32)
    base_shard = shuffled // mp_total
    within = shuffled % mp_total
    rotations = jax.random.permutation(jax.random.fold_in(key, 102), dp_total)[:GROUPS].astype(jnp.int32)
    pair_dest = (base_shard[:, None] + rotations[None, :]) % dp_total
    natural = jnp.arange(GROUPS, dtype=jnp.int32)[None, :] * mp_total + within[:, None]
    shard_keys = jax.random.split(jax.random.fold_in(key, 103), dp_total)
    shuffles = jax.vmap(lambda one_key: jax.random.permutation(one_key, BLOCKS))(shard_keys).astype(jnp.int32)
    pair_block = shuffles[pair_dest, natural]
    first_len = jax.random.randint(jax.random.fold_in(key, 104), (device_total, GROUPS), 1, FU, dtype=jnp.int32)
    last_pair = jnp.logical_and(pair_dest == 0, pair_block == BLOCKS - 1)
    first_len = jnp.where(last_pair, FU - 1, first_len).astype(jnp.int32)
    lengths = jnp.stack([first_len, FU - first_len], axis=-1).reshape(UTTS).astype(jnp.int32)
    dests = jnp.stack([pair_dest, pair_dest], axis=-1).reshape(UTTS).astype(jnp.int32)
    block_start = pair_block * FU
    offsets = jnp.stack([block_start, block_start + first_len], axis=-1).reshape(UTTS).astype(jnp.int32)
    return (lengths, dests, offsets)


def draw_lengths(key, part):
    return pair_plan(key)[0]


def draw_dests(key, part):
    return pair_plan(key)[1]


def draw_offsets(key, part):
    return pair_plan(key)[2]


def level_of(rng, dims, cuts, smallest, largest):
    gain = 1.0
    for axis_at, shards_of in cuts:
        draws = jax.random.uniform(jax.random.fold_in(jax.random.fold_in(rng, 6), axis_at), (shards_of,), jnp.float32, smallest / len(cuts), largest / len(cuts))
        gain = gain * jnp.repeat(jnp.exp(draws), dims[axis_at] // shards_of).reshape((-1,) + (1,) * (len(dims) - 1 - axis_at))
    return gain


def normal_values(rng, shape, scale, limit, cuts=(), kind=jnp.bfloat16):
    entries = scale * jax.random.normal(rng, shape, jnp.float32)
    if cuts:
        entries = entries * level_of(rng, shape, cuts, -0.22, 0.18)
    return jnp.clip(entries, -limit, limit).astype(kind)


def setup_inputs(seed: int = 0) -> dict:
    splits = jax.random.split(jax.random.key(seed), 10)
    features = normal_values(splits[0], (UTTS, 4 * FU, C), 1.0, 6.0, ((0, 32),))
    lengths = draw_lengths(jax.random.fold_in(splits[9], 71), 0)
    dests = draw_dests(jax.random.fold_in(splits[9], 71), 0)
    offsets = draw_offsets(jax.random.fold_in(splits[9], 71), 0)
    conv_weight = normal_values(splits[4], (LAYERS, 2 * C, C), (2 * C) ** -0.5, 0.1875)
    norm_gain = jnp.clip(1.0 + 0.18 * jax.random.normal(splits[5], (LAYERS, C), jnp.float32), 0.1, 1.9)
    norm_shift = normal_values(splits[6], (LAYERS, C), 0.5, 3.0, (), jnp.float32)
    proj_weight = normal_values(splits[7], (C, HID), C ** -0.5, 0.25, ((1, 4),))
    grad_packed = normal_values(splits[8], (SEQ_ROWS, HID), 1.0, 6.0, ((0, 8), (1, 4)))
    return {"features": features, "lengths": lengths, "dests": dests, "offsets": offsets, "conv_weight": conv_weight, "norm_gain": norm_gain, "norm_shift": norm_shift, "proj_weight": proj_weight, "grad_packed": grad_packed}


epsilon = 1e-05

def norm_gelu(pre_norm, gain_row, shift_row):
    average = lax.optimization_barrier(jnp.mean(pre_norm, axis=-1, keepdims=True))
    centred = pre_norm - average
    spread = lax.optimization_barrier(jnp.mean(centred * centred, axis=-1, keepdims=True))
    return jax.nn.gelu(centred * lax.rsqrt(spread + epsilon) * gain_row + shift_row, approximate=False)

def encode_block(inputs, conv_weight, norm_gain, norm_shift):
    channels = inputs.shape[-1]
    first_in = inputs.reshape(-1, 2 * channels)
    first_out = jnp.dot(first_in, conv_weight[0], preferred_element_type=jnp.float32)
    hidden = norm_gelu(first_out, norm_gain[0], norm_shift[0]).astype(jnp.bfloat16)
    second_in = hidden.reshape(-1, 2 * channels)
    second = jnp.dot(second_in, conv_weight[1], preferred_element_type=jnp.float32)
    frames = norm_gelu(second, norm_gain[1], norm_shift[1]).astype(jnp.bfloat16)
    return (first_in, first_out, second_in, second, frames)

def back_block(inputs, grad_frames, conv_weight, norm_gain, norm_shift):
    channels = inputs.shape[-1]
    first_in, first_out, second_in, second, frames = encode_block(inputs, conv_weight, norm_gain, norm_shift)
    unused_second, pull_second = jax.vjp(norm_gelu, second, norm_gain[1], norm_shift[1])
    grad_second, gain_second, shift_second = pull_second(lax.optimization_barrier(grad_frames).astype(jnp.float32))
    grad_second = grad_second.astype(jnp.bfloat16)
    grad_hidden = jnp.dot(grad_second, conv_weight[1].T, preferred_element_type=jnp.float32).astype(jnp.bfloat16)
    grad_hidden = lax.optimization_barrier(grad_hidden).reshape(-1, channels).astype(jnp.float32)
    unused_first, pull_first = jax.vjp(norm_gelu, first_out, norm_gain[0], norm_shift[0])
    grad_first, gain_first, shift_first = pull_first(grad_hidden)
    grad_first = grad_first.astype(jnp.bfloat16)
    grad_inputs = jnp.dot(grad_first, conv_weight[0].T, preferred_element_type=jnp.float32).astype(jnp.bfloat16)
    grad_weight = jnp.stack([jnp.dot(first_in.T, grad_first, preferred_element_type=jnp.float32), jnp.dot(second_in.T, grad_second, preferred_element_type=jnp.float32)])
    grad_norms = jnp.stack([jnp.concatenate([gain_first, shift_first]), jnp.concatenate([gain_second, shift_second])])
    return (grad_inputs.reshape(inputs.shape), grad_weight, grad_norms)

def reference(features, lengths, dests, offsets, conv_weight, norm_gain, norm_shift, proj_weight, grad_packed):
    device_total = UTTS // UTT_DEV
    blocks_in = features.reshape(device_total, UTT_DEV * 4 * FU, C)

    def forward_one(device_block):
        return encode_block(device_block, conv_weight, norm_gain, norm_shift)[4]
    frames = lax.map(forward_one, blocks_in).reshape(UTTS, FU, C)
    frame_index = jnp.arange(FU, dtype=jnp.int32)
    is_live = frame_index[None, :] < lengths[:, None]
    row_index = jnp.where(is_live, dests[:, None] * ROWS + offsets[:, None] + frame_index[None, :], SEQ_ROWS)
    row_index = row_index.astype(jnp.int32).reshape(-1)
    packed_in = jnp.zeros((SEQ_ROWS, C), jnp.bfloat16).at[row_index].set(frames.reshape(-1, C), mode='drop')
    packed = jnp.dot(packed_in, proj_weight, preferred_element_type=jnp.float32).astype(jnp.bfloat16)
    grad_proj = jnp.dot(packed_in.T, grad_packed, preferred_element_type=jnp.float32)
    grad_rows = jnp.dot(grad_packed, proj_weight.T, preferred_element_type=jnp.float32).astype(jnp.bfloat16)
    padded_rows = jnp.concatenate([grad_rows, jnp.zeros((1, C), jnp.bfloat16)], axis=0)
    grad_frames = padded_rows[row_index].reshape(device_total, UTT_DEV * FU, C)

    def back_one(totals, pieces):
        device_block, grad_block = pieces
        grad_inputs, grad_weight, grad_norms = back_block(device_block, grad_block, conv_weight, norm_gain, norm_shift)
        return ((totals[0] + grad_weight, totals[1] + grad_norms), grad_inputs)
    zero_sums = (jnp.zeros((LAYERS, 2 * C, C), jnp.float32), jnp.zeros((LAYERS, 2 * C), jnp.float32))
    sums, grad_features = lax.scan(back_one, zero_sums, (blocks_in, grad_frames))
    grad_features = grad_features.reshape(UTTS, 4 * FU, C)
    return (packed, grad_features, sums[0], sums[1], grad_proj)
```

```python
import functools
import math

import jax
import jax.numpy as jnp
from jax import lax
from jax.experimental import pallas as pl
from jax.experimental.pallas import tpu as pltpu
from jax.sharding import PartitionSpec as P

epsilon = 1e-05
BF = jnp.bfloat16
F32 = jnp.float32
VMEM = pltpu.VMEM
SMEM = pltpu.SMEM


def call(body, out, args, scalars=0, flops=0, scratch=()):
    specs = [
        pl.BlockSpec(memory_space=SMEM if i < scalars else VMEM) for i in range(len(args))
    ]
    many = isinstance(out, (list, tuple))
    moved = sum(a.size * a.dtype.itemsize for a in args)
    return pl.pallas_call(
        body,
        out_shape=out,
        in_specs=specs,
        out_specs=[pl.BlockSpec(memory_space=VMEM)] * len(out)
        if many
        else pl.BlockSpec(memory_space=VMEM),
        scratch_shapes=list(scratch),
        compiler_params=pltpu.CompilerParams(vmem_limit_bytes=40 * 2**20),
        cost_estimate=pl.CostEstimate(flops=flops, bytes_accessed=moved, transcendentals=0),
    )(*args)


def shape(*dims, kind=BF):
    return jax.ShapeDtypeStruct(dims, kind)


def dot(a, b):
    return jnp.dot(a, b, preferred_element_type=F32)


def dot_nt(a, b):
    return lax.dot_general(a, b, (((1,), (1,)), ((), ())), preferred_element_type=F32)


def norm_parts(pre):
    average = jnp.mean(pre, axis=-1, keepdims=True)
    centred = pre - average
    spread = jnp.mean(centred * centred, axis=-1, keepdims=True)
    scale = lax.rsqrt(spread + epsilon)
    return centred * scale, scale


def gelu_parts(value):
    half = 0.5 * (1.0 + lax.erf(value * math.sqrt(0.5)))
    density = jnp.exp(-0.5 * value * value) * (1.0 / math.sqrt(2.0 * math.pi))
    return value * half, half + value * density


def source_of(row, lengths_ref, pairs, frames):
    part = lax.div(row, pairs * frames)
    inner = lax.rem(row, pairs * frames)
    pair = lax.div(inner, frames)
    t = lax.rem(inner, frames)
    first = jnp.zeros_like(row)
    for p in range(pairs):
        first = jnp.where(pair == p, lengths_ref[2 * p], first)
    off = jnp.where(part == 1, 2, jnp.where(part == 2, 1, part))
    t_from = jnp.where(t < first, t, t + frames - first)
    return pair * (8 * frames) + 4 * t_from + off


def index_kernel(dests_ref, offsets_ref, out_ref, *, pairs, frames):
    row = lax.broadcasted_iota(jnp.int32, out_ref.shape, 0)
    value = jnp.full(out_ref.shape, -1, jnp.int32)
    for p in range(pairs):
        value = jnp.where(row == dests_ref[2 * p], lax.div(offsets_ref[2 * p], frames), value)
    out_ref[...] = value


def forward_kernel(
    lengths_ref, me_ref, feat_ref, weight_ref, gain_ref, shift_ref, *rest, pairs, frames, groups, owned
):
    mp_count = me_ref.shape[0] - 1
    frames_ref, slope1_ref, slope2_ref, hat1_ref, hat2_ref, scale1_ref, scale2_ref = rest[:7]
    turned_refs, in_turned = rest[7:-1], rest[-1]
    channels = feat_ref.shape[1]
    n2 = pairs * frames
    row = lax.broadcasted_iota(jnp.int32, (4 * n2, 1), 0)
    source = source_of(row, lengths_ref, pairs, frames)
    place = lax.broadcasted_iota(jnp.int32, (4 * n2, feat_ref.shape[0]), 1)
    pick = jnp.where(place == source, 1.0, 0.0).astype(BF)
    chosen32 = dot(pick, feat_ref[...])
    chosen = chosen32.astype(BF)
    even, odd = chosen[: 2 * n2], chosen[2 * n2 :]
    first = dot(even, weight_ref[0, :channels, :]) + dot(odd, weight_ref[0, channels:, :])
    hat, scale = norm_parts(first)
    hidden, slope = gelu_parts(hat * gain_ref[0:1, :] + shift_ref[0:1, :])
    slope1_ref[...] = slope
    hat1_ref[...] = hat
    scale1_ref[...] = jnp.broadcast_to(scale, scale1_ref.shape)
    hidden = hidden.astype(BF)
    hidden32 = hidden.astype(F32)
    second = dot(hidden[:n2], weight_ref[1, :channels, :]) + dot(
        hidden[n2:], weight_ref[1, channels:, :]
    )
    hat, scale = norm_parts(second)
    made, slope = gelu_parts(hat * gain_ref[1:2, :] + shift_ref[1:2, :])
    slope2_ref[...] = slope
    hat2_ref[...] = hat
    scale2_ref[...] = jnp.broadcast_to(scale, scale2_ref.shape)
    frames_ref[...] = made.astype(BF)
    wide = in_turned.shape[1]
    fill = [jnp.zeros((wide - 3 * n2, channels), F32)] if wide > 3 * n2 else []
    for tap in range(2):
        stacked = jnp.concatenate(
            [chosen32[2 * n2 * tap : 2 * n2 * (tap + 1)], hidden32[n2 * tap : n2 * (tap + 1)]] + fill,
            axis=0,
        )
        in_turned[channels * tap : channels * (tap + 1), :] = stacked.T
    for k, turned_ref in enumerate(turned_refs):
        start = me_ref[1 + k] * owned
        turned_ref[...] = jnp.concatenate(
            [
                in_turned[pl.ds(pl.multiple_of(d * mp_count * owned + start, owned), owned), :]
                for d in range(groups)
            ],
            axis=0,
        ).astype(BF)


def send_kernel(got_ref, dests_ref, mine_ref, other_ref, frames_ref, out_ref, rows32, *, pairs, frames):
    rows32[...] = mine_ref[...].astype(F32) + other_ref[...].astype(F32)
    blocks = rows32.shape[0] // frames
    made = frames_ref[...].astype(F32)
    none = jnp.zeros((frames, made.shape[1]), F32)
    for d in range(out_ref.shape[0]):
        block = got_ref[d, 0]
        safe = jnp.clip(block, 0, blocks - 1)
        grads = rows32[pl.ds(pl.multiple_of(safe * frames, frames), frames), :]
        grads = jnp.where(block >= 0, grads, none)
        sent = none
        for p in range(pairs):
            sent = jnp.where(dests_ref[2 * p] == d, made[p * frames : (p + 1) * frames], sent)
        out_ref[d] = jnp.concatenate([grads, sent], axis=0).astype(BF)


def place_kernel(got_ref, slots_ref, out_ref, rows32, *, frames):
    rows32[...] = jnp.zeros_like(rows32)
    for d in range(slots_ref.shape[0]):
        block = got_ref[d, 0]

        @pl.when(block >= 0)
        def _():
            safe = jnp.clip(block, 0, rows32.shape[0] // frames - 1)
            rows32[pl.ds(pl.multiple_of(safe * frames, frames), frames), :] = slots_ref[d].astype(F32)[
                frames:
            ]

    out_ref[...] = rows32[...].astype(BF)


def project_kernel(mine_ref, other_ref, weight_ref, packed_ref, turned_ref):
    rows32 = mine_ref[...].astype(F32) + other_ref[...].astype(F32)
    packed_ref[...] = dot(rows32.astype(BF), weight_ref[...]).astype(BF)
    turned_ref[...] = rows32.T.astype(BF)


def norm_back(grad, slope_ref, hat_ref, scale_ref, gain):
    pre = grad * slope_ref[...]
    hat = hat_ref[...]
    by_hat = pre * hat
    inner = pre * gain
    average = jnp.mean(inner, axis=-1, keepdims=True)
    along = jnp.mean(inner * hat, axis=-1, keepdims=True)
    back = (inner - average - hat * along) * scale_ref[:, 0:1]
    return (
        back.astype(BF),
        jnp.sum(by_hat, axis=0, keepdims=True),
        jnp.sum(pre, axis=0, keepdims=True),
    )


def back_kernel(
    dests_ref, slots_ref, slope1_ref, slope2_ref, hat1_ref, hat2_ref, scale1_ref, scale2_ref,
    weight_ref, gain_ref, out_ref, grads32, *, pairs, frames
):
    channels = weight_ref.shape[2]
    for p in range(pairs):
        slot = jnp.clip(dests_ref[2 * p], 0, slots_ref.shape[0] - 1)
        grads32[p * frames : (p + 1) * frames, :] = slots_ref[slot].astype(F32)[:frames]
    second, gain2, shift2 = norm_back(grads32[...], slope2_ref, hat2_ref, scale2_ref, gain_ref[1:2, :])
    hidden = jnp.concatenate(
        [
            dot_nt(second, weight_ref[1, :channels, :]),
            dot_nt(second, weight_ref[1, channels:, :]),
        ],
        axis=0,
    )
    hidden = hidden.astype(BF).astype(F32)
    first, gain1, shift1 = norm_back(hidden, slope1_ref, hat1_ref, scale1_ref, gain_ref[0:1, :])
    sums = jnp.concatenate([gain1, shift1, gain2, shift2], axis=0)
    high = sums.astype(BF).astype(F32)
    rows = [high, sums - high, jnp.zeros((8, channels), F32)]
    n1, n2 = first.shape[0], second.shape[0]
    out_ref[:n1, :] = first
    out_ref[n1 : n1 + n2, :] = second
    out_ref[n1 + n2 :, :] = jnp.concatenate(rows, axis=0).astype(BF)


def input_kernel(lengths_ref, grad_ref, weight_ref, out_ref, *, pairs, frames):
    channels = weight_ref.shape[2]
    n1 = 2 * pairs * frames
    first = grad_ref[:n1, :]
    rows = jnp.concatenate(
        [dot_nt(first, weight_ref[0, :channels, :]), dot_nt(first, weight_ref[0, channels:, :])],
        axis=0,
    ).astype(BF)
    row = lax.broadcasted_iota(jnp.int32, (1, 2 * n1), 1)
    source = source_of(row, lengths_ref, pairs, frames)
    place = lax.broadcasted_iota(jnp.int32, (out_ref.shape[0], 2 * n1), 0)
    pick = jnp.where(place == source, 1.0, 0.0).astype(BF)
    out_ref[...] = dot(pick, rows).astype(BF)


def kernel_grad_kernel(*refs, n1, n2, owned, count):
    grad_refs, in_refs, turned_ref, out_ref = refs[:count], refs[count : 2 * count], refs[-2], refs[-1]
    channels = out_ref.shape[2]
    groups = out_ref.shape[0]
    first, second, sums = 0.0, 0.0, 0.0
    for grad_ref, in_ref in zip(grad_refs, in_refs):
        side = in_ref[...]
        first += dot(side[:, :n1], grad_ref[:n1, :])
        second += dot(side[:, n1 : n1 + n2], grad_ref[n1 : n1 + n2, :])
        tail = grad_ref[n1 + n2 :, :].astype(F32)
        sums += tail[0:4] + tail[4:8]
    high = sums.astype(BF).astype(F32)
    low = sums - high
    width = 2 * channels // groups
    per_slot = channels // groups
    across = channels // turned_ref.shape[1]
    each = per_slot // across
    for d in range(groups):
        at = (d * width) % channels
        which = (d * width) // channels
        pieces = [
            part[2 * layer + which : 2 * layer + which + 1, at : at + width]
            for part in (high, low)
            for layer in range(2)
        ]
        if 4 * width < channels:
            pieces.append(jnp.zeros((1, channels - 4 * width), F32))
        norm_row = jnp.concatenate(pieces, axis=1)
        turned = turned_ref[d * per_slot : (d + 1) * per_slot, :].astype(F32)
        turned = jnp.concatenate([turned[g * each : (g + 1) * each] for g in range(across)], axis=1)
        out_ref[d] = jnp.concatenate(
            [
                first[d * owned : (d + 1) * owned],
                second[d * owned : (d + 1) * owned],
                turned,
                norm_row,
                jnp.zeros((7, channels), F32),
            ],
            axis=0,
        ).astype(BF)


def last_kernel(me_ref, slots_ref, cotangent_ref, conv_ref, norm_ref, proj_ref, *, owned, mp_count):
    groups, _, channels = slots_ref.shape
    seq = cotangent_ref.shape[0] // groups
    across = channels // seq
    each = channels // groups // across
    total, norms, proj = 0.0, 0.0, 0.0
    for d in range(groups):
        slot = slots_ref[d].astype(F32)
        total += slot[: 2 * owned]
        turned = slot[2 * owned : 2 * owned + each]
        turned = jnp.concatenate([turned[:, g * seq : (g + 1) * seq] for g in range(across)], axis=0)
        norms += slot[2 * owned + each : 2 * owned + each + 1]
        proj += dot(turned.astype(BF), cotangent_ref[d * seq : (d + 1) * seq, :])
    conv_ref[0] = total[:owned]
    conv_ref[1] = total[owned:]
    proj_ref[...] = proj
    width = mp_count * owned
    rows = []
    for layer in range(2):
        line = norms[:, layer * width : (layer + 1) * width]
        line = line + norms[:, (2 + layer) * width : (3 + layer) * width]
        mine = jnp.zeros((1, owned), F32)
        for m in range(mp_count):
            mine = jnp.where(me_ref[0] == m, line[:, m * owned : (m + 1) * owned], mine)
        rows.append(mine)
    norm_ref[...] = jnp.concatenate(rows, axis=0)


def local(
    features, lengths, dests, offsets, conv_weight, norm_gain, norm_shift, proj_weight, grad_packed
):
    utt_count, positions, channels = features.shape
    frames = positions // 4
    pairs = utt_count // 2
    dp_count = lax.axis_size("dp")
    mp_count = lax.axis_size("mp")
    seq = grad_packed.shape[0]
    width = grad_packed.shape[1]
    owned = 2 * channels // (dp_count * mp_count)
    n1, n2 = 2 * pairs * frames, pairs * frames
    bits = [1 << b for b in range(mp_count.bit_length() - 1)][::-1]

    def swap(x, mask):
        return lax.ppermute(x, "mp", [(i, i ^ mask) for i in range(mp_count)])

    me = lax.axis_index("mp").astype(jnp.int32)
    me_all = jnp.stack([me] + [me ^ k for k in range(mp_count)])

    index = call(
        functools.partial(index_kernel, pairs=pairs, frames=frames),
        shape(dp_count, 128, kind=jnp.int32),
        (dests, offsets),
        scalars=2,
    )
    got_index = lax.all_to_all(index, "dp", split_axis=0, concat_axis=0, tiled=True)
    all_cotangent = lax.all_gather(grad_packed, "dp", tiled=True)

    grad_rows = lax.dot_general(
        grad_packed, proj_weight, (((1,), (1,)), ((), ())), preferred_element_type=F32
    ).astype(BF)
    for mask in bits[:-1]:
        grad_rows = (grad_rows.astype(F32) + swap(grad_rows, mask).astype(F32)).astype(BF)
    other_rows = swap(grad_rows, bits[-1])

    wide = -(-(n1 + n2) // 128) * 128
    feat = features.reshape(utt_count * positions, channels)
    made = call(
        functools.partial(forward_kernel, pairs=pairs, frames=frames, groups=dp_count, owned=owned),
        [
            shape(n2, channels),
            shape(n1, channels, kind=F32),
            shape(n2, channels, kind=F32),
            shape(n1, channels, kind=F32),
            shape(n2, channels, kind=F32),
            shape(n1, 128, kind=F32),
            shape(n2, 128, kind=F32),
        ]
        + [shape(dp_count * owned, wide)] * mp_count,
        (lengths, me_all, feat, conv_weight, norm_gain, norm_shift),
        scalars=2,
        flops=2 * (n1 + n2) * 2 * channels * channels,
        scratch=[pltpu.VMEM((2 * channels, wide), F32)],
    )
    pair_frames, slope1, slope2, hat1, hat2, scale1, scale2 = made[:7]
    in_sides = [side if k == 0 else swap(side, k) for k, side in enumerate(made[7:])]

    sent = call(
        functools.partial(send_kernel, pairs=pairs, frames=frames),
        shape(dp_count, 2 * frames, channels),
        (got_index, dests, grad_rows, other_rows, pair_frames),
        scalars=2,
        scratch=[pltpu.VMEM((seq, channels), F32)],
    )
    slots = lax.all_to_all(sent, "dp", split_axis=0, concat_axis=0, tiled=True)

    grads = call(
        functools.partial(back_kernel, pairs=pairs, frames=frames),
        shape(n1 + n2 + 16, channels),
        (dests, slots, slope1, slope2, hat1, hat2, scale1, scale2, conv_weight, norm_gain),
        scalars=1,
        flops=2 * n2 * 2 * channels * channels,
        scratch=[pltpu.VMEM((n2, channels), F32)],
    )
    by_mask = {0: grads}
    for mask in bits:
        for known in list(by_mask):
            by_mask[known ^ mask] = swap(by_mask[known], mask)

    placed = call(
        functools.partial(place_kernel, frames=frames),
        shape(seq, channels),
        (got_index, slots),
        scalars=1,
        scratch=[pltpu.VMEM((seq, channels), F32)],
    )
    for mask in bits[:-1]:
        placed = placed + swap(placed, mask)
    packed, turned = call(
        project_kernel,
        [shape(seq, width), shape(channels, seq)],
        (placed, swap(placed, bits[-1]), proj_weight),
        flops=2 * seq * channels * width,
    )

    grad_features = call(
        functools.partial(input_kernel, pairs=pairs, frames=frames),
        shape(utt_count * positions, channels),
        (lengths, grads, conv_weight),
        scalars=1,
        flops=2 * n1 * 2 * channels * channels,
    ).reshape(utt_count, positions, channels)

    per_slot = channels // dp_count * seq // channels
    partial = call(
        functools.partial(kernel_grad_kernel, n1=n1, n2=n2, owned=owned, count=mp_count),
        shape(dp_count, 2 * owned + per_slot + 8, channels),
        tuple(by_mask[k] for k in range(mp_count)) + tuple(in_sides) + (turned,),
        flops=2 * (n1 + n2) * 2 * channels * channels,
    )
    arrived = lax.all_to_all(partial, "dp", split_axis=0, concat_axis=0, tiled=True)
    grad_conv, grad_norm, grad_proj = call(
        functools.partial(last_kernel, owned=owned, mp_count=mp_count),
        [
            shape(2, owned, channels, kind=F32),
            shape(2, owned, kind=F32),
            shape(channels // dp_count, width, kind=F32),
        ],
        (me_all, arrived, all_cotangent),
        scalars=1,
    )
    return (packed, grad_features, grad_conv, grad_norm, grad_proj)


def solution(mesh):
    return jax.shard_map(
        local,
        mesh=mesh,
        in_specs=(
            P(("dp", "mp"), None, None),
            P(("dp", "mp")),
            P(("dp", "mp")),
            P(("dp", "mp")),
            P(),
            P(),
            P(),
            P(None, "mp"),
            P("dp", "mp"),
        ),
        out_specs=(
            P("dp", "mp"),
            P(("dp", "mp"), None, None),
            P(None, ("dp", "mp"), None),
            P(None, ("dp", "mp")),
            P("dp", "mp"),
        ),
        check_vma=False,
    )
```

```python
import functools
import math

import jax
import jax.numpy as jnp
from jax import lax
from jax.experimental import pallas as pl
from jax.experimental.pallas import tpu as pltpu
from jax.sharding import PartitionSpec as P

epsilon = 1e-05
BF = jnp.bfloat16
F32 = jnp.float32
VMEM = pltpu.VMEM
SMEM = pltpu.SMEM


def call(body, out, args, scalars=0, flops=0, scratch=()):
    specs = [
        pl.BlockSpec(memory_space=SMEM if i < scalars else VMEM) for i in range(len(args))
    ]
    many = isinstance(out, (list, tuple))
    moved = sum(a.size * a.dtype.itemsize for a in args)
    return pl.pallas_call(
        body,
        out_shape=out,
        in_specs=specs,
        out_specs=[pl.BlockSpec(memory_space=VMEM)] * len(out)
        if many
        else pl.BlockSpec(memory_space=VMEM),
        scratch_shapes=list(scratch),
        compiler_params=pltpu.CompilerParams(vmem_limit_bytes=40 * 2**20),
        cost_estimate=pl.CostEstimate(flops=flops, bytes_accessed=moved, transcendentals=0),
    )(*args)


def shape(*dims, kind=BF):
    return jax.ShapeDtypeStruct(dims, kind)


def dot(a, b):
    return jnp.dot(a, b, preferred_element_type=F32)


def dot_nt(a, b):
    return lax.dot_general(a, b, (((1,), (1,)), ((), ())), preferred_element_type=F32)


def norm_parts(pre):
    average = jnp.mean(pre, axis=-1, keepdims=True)
    centred = pre - average
    spread = jnp.mean(centred * centred, axis=-1, keepdims=True)
    scale = lax.rsqrt(spread + epsilon)
    return centred * scale, scale


def gelu_parts(value):
    half = 0.5 * (1.0 + lax.erf(value * math.sqrt(0.5)))
    density = jnp.exp(-0.5 * value * value) * (1.0 / math.sqrt(2.0 * math.pi))
    return value * half, half + value * density


def source_of(row, lengths_ref, pairs, frames):
    part = lax.div(row, pairs * frames)
    inner = lax.rem(row, pairs * frames)
    pair = lax.div(inner, frames)
    t = lax.rem(inner, frames)
    first = jnp.zeros_like(row)
    for p in range(pairs):
        first = jnp.where(pair == p, lengths_ref[2 * p], first)
    off = jnp.where(part == 1, 2, jnp.where(part == 2, 1, part))
    t_from = jnp.where(t < first, t, t + frames - first)
    return pair * (8 * frames) + 4 * t_from + off


def index_kernel(dests_ref, offsets_ref, out_ref, *, pairs, frames):
    row = lax.broadcasted_iota(jnp.int32, out_ref.shape, 0)
    value = jnp.full(out_ref.shape, -1, jnp.int32)
    for p in range(pairs):
        value = jnp.where(row == dests_ref[2 * p], lax.div(offsets_ref[2 * p], frames), value)
    out_ref[...] = value


def forward_kernel(
    lengths_ref, me_ref, feat_ref, weight_ref, gain_ref, shift_ref, *rest, pairs, frames, far, near, owned
):
    frames_ref, slope1_ref, slope2_ref, hat1_ref, hat2_ref, scale1_ref, scale2_ref = rest[:7]
    turned_refs, in_turned = rest[7:-1], rest[-1]
    channels = feat_ref.shape[1]
    n2 = pairs * frames
    row = lax.broadcasted_iota(jnp.int32, (4 * n2, 1), 0)
    source = source_of(row, lengths_ref, pairs, frames)
    place = lax.broadcasted_iota(jnp.int32, (4 * n2, feat_ref.shape[0]), 1)
    pick = jnp.where(place == source, 1.0, 0.0).astype(BF)
    chosen32 = dot(pick, feat_ref[...])
    chosen = chosen32.astype(BF)
    even, odd = chosen[: 2 * n2], chosen[2 * n2 :]
    first = dot(even, weight_ref[0, :channels, :]) + dot(odd, weight_ref[0, channels:, :])
    hat, scale = norm_parts(first)
    hidden, slope = gelu_parts(hat * gain_ref[0:1, :] + shift_ref[0:1, :])
    slope1_ref[...] = slope
    hat1_ref[...] = hat
    scale1_ref[...] = jnp.broadcast_to(scale, scale1_ref.shape)
    hidden = hidden.astype(BF)
    hidden32 = hidden.astype(F32)
    second = dot(hidden[:n2], weight_ref[1, :channels, :]) + dot(
        hidden[n2:], weight_ref[1, channels:, :]
    )
    hat, scale = norm_parts(second)
    made, slope = gelu_parts(hat * gain_ref[1:2, :] + shift_ref[1:2, :])
    slope2_ref[...] = slope
    hat2_ref[...] = hat
    scale2_ref[...] = jnp.broadcast_to(scale, scale2_ref.shape)
    frames_ref[...] = made.astype(BF)
    wide = in_turned.shape[1]
    fill = [jnp.zeros((wide - 3 * n2, channels), F32)] if wide > 3 * n2 else []
    for tap in range(2):
        stacked = jnp.concatenate(
            [chosen32[2 * n2 * tap : 2 * n2 * (tap + 1)], hidden32[n2 * tap : n2 * (tap + 1)]] + fill,
            axis=0,
        )
        in_turned[channels * tap : channels * (tap + 1), :] = stacked.T
    at = me_ref[1]
    for k, turned_ref in enumerate(turned_refs):
        start = (at ^ k) * owned
        turned_ref[...] = jnp.concatenate(
            [
                in_turned[pl.ds(pl.multiple_of(z * near * owned + start, owned), owned), :]
                for z in range(far)
            ],
            axis=0,
        ).astype(BF)


def send_kernel(got_ref, dests_ref, mine_ref, other_ref, frames_ref, out_ref, rows32, *, pairs, frames):
    rows32[...] = mine_ref[...].astype(F32) + other_ref[...].astype(F32)
    blocks = rows32.shape[0] // frames
    made = frames_ref[...].astype(F32)
    none = jnp.zeros((frames, made.shape[1]), F32)
    for d in range(out_ref.shape[0]):
        block = got_ref[d, 0]
        safe = jnp.clip(block, 0, blocks - 1)
        grads = rows32[pl.ds(pl.multiple_of(safe * frames, frames), frames), :]
        grads = jnp.where(block >= 0, grads, none)
        sent = none
        for p in range(pairs):
            sent = jnp.where(dests_ref[2 * p] == d, made[p * frames : (p + 1) * frames], sent)
        out_ref[d] = jnp.concatenate([grads, sent], axis=0).astype(BF)


def place_kernel(got_ref, slots_ref, out_ref, rows32, *, frames):
    rows32[...] = jnp.zeros_like(rows32)
    for d in range(slots_ref.shape[0]):
        block = got_ref[d, 0]

        @pl.when(block >= 0)
        def _():
            safe = jnp.clip(block, 0, rows32.shape[0] // frames - 1)
            rows32[pl.ds(pl.multiple_of(safe * frames, frames), frames), :] = slots_ref[d].astype(F32)[
                frames:
            ]

    out_ref[...] = rows32[...].astype(BF)


def project_kernel(me_ref, mine_ref, other_ref, weight_ref, cotangent_ref, packed_ref, keep_ref, send_ref):
    rows32 = mine_ref[...].astype(F32) + other_ref[...].astype(F32)
    packed_ref[...] = dot(rows32.astype(BF), weight_ref[...]).astype(BF)
    partial = dot(rows32.T.astype(BF), cotangent_ref[...])
    each = keep_ref.shape[1]
    for z in range(keep_ref.shape[0]):
        low = partial[2 * z * each : (2 * z + 1) * each]
        high = partial[(2 * z + 1) * each : (2 * z + 2) * each]
        keep_ref[z] = jnp.where(me_ref[3] == 0, low, high)
        send_ref[z] = jnp.where(me_ref[3] == 0, high, low).astype(BF)


def fold_kernel(me_ref, keep_ref, got_ref, own_ref, *out_refs):
    for f in range(keep_ref.shape[0]):
        z = me_ref[2] ^ f
        total = keep_ref[z] + got_ref[z].astype(F32)
        if f == 0:
            own_ref[...] = total
        else:
            out_refs[f - 1][...] = total.astype(BF)


def norm_back(grad, slope_ref, hat_ref, scale_ref, gain):
    pre = grad * slope_ref[...]
    hat = hat_ref[...]
    by_hat = pre * hat
    inner = pre * gain
    average = jnp.mean(inner, axis=-1, keepdims=True)
    along = jnp.mean(inner * hat, axis=-1, keepdims=True)
    back = (inner - average - hat * along) * scale_ref[:, 0:1]
    return (
        back.astype(BF),
        jnp.sum(by_hat, axis=0, keepdims=True),
        jnp.sum(pre, axis=0, keepdims=True),
    )


def back_kernel(
    dests_ref, slots_ref, slope1_ref, slope2_ref, hat1_ref, hat2_ref, scale1_ref, scale2_ref,
    weight_ref, gain_ref, out_ref, grads32, *, pairs, frames
):
    channels = weight_ref.shape[2]
    for p in range(pairs):
        slot = jnp.clip(dests_ref[2 * p], 0, slots_ref.shape[0] - 1)
        grads32[p * frames : (p + 1) * frames, :] = slots_ref[slot].astype(F32)[:frames]
    second, gain2, shift2 = norm_back(grads32[...], slope2_ref, hat2_ref, scale2_ref, gain_ref[1:2, :])
    hidden = jnp.concatenate(
        [
            dot_nt(second, weight_ref[1, :channels, :]),
            dot_nt(second, weight_ref[1, channels:, :]),
        ],
        axis=0,
    )
    hidden = hidden.astype(BF).astype(F32)
    first, gain1, shift1 = norm_back(hidden, slope1_ref, hat1_ref, scale1_ref, gain_ref[0:1, :])
    sums = jnp.concatenate([gain1, shift1, gain2, shift2], axis=0)
    high = sums.astype(BF).astype(F32)
    rows = [high, sums - high, jnp.zeros((8, channels), F32)]
    n1, n2 = first.shape[0], second.shape[0]
    out_ref[:n1, :] = first
    out_ref[n1 : n1 + n2, :] = second
    out_ref[n1 + n2 :, :] = jnp.concatenate(rows, axis=0).astype(BF)


def input_kernel(lengths_ref, grad_ref, weight_ref, out_ref, *, pairs, frames):
    channels = weight_ref.shape[2]
    n1 = 2 * pairs * frames
    first = grad_ref[:n1, :]
    rows = jnp.concatenate(
        [dot_nt(first, weight_ref[0, :channels, :]), dot_nt(first, weight_ref[0, channels:, :])],
        axis=0,
    ).astype(BF)
    row = lax.broadcasted_iota(jnp.int32, (1, 2 * n1), 1)
    source = source_of(row, lengths_ref, pairs, frames)
    place = lax.broadcasted_iota(jnp.int32, (out_ref.shape[0], 2 * n1), 0)
    pick = jnp.where(place == source, 1.0, 0.0).astype(BF)
    out_ref[...] = dot(pick, rows).astype(BF)


def kernel_grad_kernel(me_ref, *refs, n1, n2, owned, near, far):
    grad_refs, in_refs = refs[:near], refs[near : 2 * near]
    own_ref, out_refs, held = refs[2 * near], refs[2 * near + 1 : -1], refs[-1]
    first, second, sums = 0.0, 0.0, 0.0
    for grad_ref, in_ref in zip(grad_refs, in_refs):
        side = in_ref[...]
        first += dot(side[:, :n1], grad_ref[:n1, :])
        second += dot(side[:, n1 : n1 + n2], grad_ref[n1 : n1 + n2, :])
        tail = grad_ref[n1 + n2 :, :].astype(F32)
        sums += tail[0:4] + tail[4:8]
    high = sums.astype(BF).astype(F32)
    for z in range(far):
        held[z] = jnp.concatenate(
            [first[z * owned : (z + 1) * owned], second[z * owned : (z + 1) * owned], high, sums - high],
            axis=0,
        )
    own_ref[...] = held[me_ref[2]]
    for f in range(1, far):
        out_refs[f - 1][...] = held[me_ref[2] ^ f].astype(BF)


def last_kernel(me_ref, *refs, owned, far):
    conv_in, proj_in = refs[:far], refs[far : 2 * far]
    conv_ref, norm_ref, proj_ref = refs[2 * far :]
    total = conv_in[0][...]
    proj = proj_in[0][...]
    for f in range(1, far):
        total += conv_in[f][...].astype(F32)
        proj += proj_in[f][...].astype(F32)
    conv_ref[0] = total[:owned]
    conv_ref[1] = total[owned : 2 * owned]
    proj_ref[...] = proj
    channels = total.shape[1]
    sums = total[2 * owned : 2 * owned + 4] + total[2 * owned + 4 : 2 * owned + 8]
    start = me_ref[0] * owned
    later = start >= channels
    lines = jnp.concatenate(
        [jnp.where(later, sums[2 * k + 1 : 2 * k + 2], sums[2 * k : 2 * k + 1]) for k in range(2)]
        + [jnp.zeros((6, channels), F32)],
        axis=0,
    )
    start = jnp.where(later, start - channels, start)
    lines = pltpu.roll(lines, lax.rem(channels - start, channels), 1)
    norm_ref[...] = lines[:2, :owned]


def local(
    features, lengths, dests, offsets, conv_weight, norm_gain, norm_shift, proj_weight, grad_packed
):
    utt_count, positions, channels = features.shape
    frames = positions // 4
    pairs = utt_count // 2
    dp_count = lax.axis_size("dp")
    mp_count = lax.axis_size("mp")
    seq = grad_packed.shape[0]
    width = grad_packed.shape[1]
    owned = 2 * channels // (dp_count * mp_count)
    n1, n2 = 2 * pairs * frames, pairs * frames
    near, far = 2 * mp_count, dp_count // 2
    everyone = ("dp", "mp")

    def swap(x, mask):
        return lax.ppermute(x, everyone, [(i, i ^ mask) for i in range(dp_count * mp_count)])

    bits = [1 << b for b in range(mp_count.bit_length() - 1)][::-1]
    at_dp = lax.axis_index("dp").astype(jnp.int32)
    at_mp = lax.axis_index("mp").astype(jnp.int32)
    x_bit = at_dp & 1
    me = jnp.stack([at_dp * mp_count + at_mp, x_bit * mp_count + at_mp, at_dp >> 1, x_bit])

    index = call(
        functools.partial(index_kernel, pairs=pairs, frames=frames),
        shape(dp_count, 128, kind=jnp.int32),
        (dests, offsets),
        scalars=2,
    )
    got_index = lax.all_to_all(index, "dp", split_axis=0, concat_axis=0, tiled=True)
    index, cotangent = lax.optimization_barrier((index, grad_packed))

    wide = -(-(n1 + n2) // 128) * 128
    feat = features.reshape(utt_count * positions, channels)
    made = call(
        functools.partial(
            forward_kernel, pairs=pairs, frames=frames, far=far, near=near, owned=owned
        ),
        [
            shape(n2, channels),
            shape(n1, channels, kind=F32),
            shape(n2, channels, kind=F32),
            shape(n1, channels, kind=F32),
            shape(n2, channels, kind=F32),
            shape(n1, 128, kind=F32),
            shape(n2, 128, kind=F32),
        ]
        + [shape(far * owned, wide)] * near,
        (lengths, me, feat, conv_weight, norm_gain, norm_shift),
        scalars=2,
        flops=2 * (n1 + n2) * 2 * channels * channels,
        scratch=[pltpu.VMEM((2 * channels, wide), F32)],
    )
    pair_frames, slope1, slope2, hat1, hat2, scale1, scale2 = made[:7]
    in_sides = [side if k == 0 else swap(side, k) for k, side in enumerate(made[7:])]

    grad_rows = lax.dot_general(
        cotangent, proj_weight, (((1,), (1,)), ((), ())), preferred_element_type=F32
    ).astype(BF)
    for mask in bits[:-1]:
        grad_rows = (grad_rows.astype(F32) + swap(grad_rows, mask).astype(F32)).astype(BF)
    other_rows = swap(grad_rows, bits[-1])

    sent = call(
        functools.partial(send_kernel, pairs=pairs, frames=frames),
        shape(dp_count, 2 * frames, channels),
        (got_index, dests, grad_rows, other_rows, pair_frames),
        scalars=2,
        scratch=[pltpu.VMEM((seq, channels), F32)],
    )
    slots = lax.all_to_all(sent, "dp", split_axis=0, concat_axis=0, tiled=True)
    slots, *in_sides = lax.optimization_barrier((slots, *in_sides))

    grads = call(
        functools.partial(back_kernel, pairs=pairs, frames=frames),
        shape(n1 + n2 + 16, channels),
        (dests, slots, slope1, slope2, hat1, hat2, scale1, scale2, conv_weight, norm_gain),
        scalars=1,
        flops=2 * n2 * 2 * channels * channels,
        scratch=[pltpu.VMEM((n2, channels), F32)],
    )
    by_mask = {mask: swap(grads, mask) if mask else grads for mask in range(0, near, 2)}
    for mask in range(0, near, 2):
        by_mask[mask + 1] = swap(by_mask[mask], 1)

    placed = call(
        functools.partial(place_kernel, frames=frames),
        shape(seq, channels),
        (got_index, slots),
        scalars=1,
        scratch=[pltpu.VMEM((seq, channels), F32)],
    )
    for mask in bits[:-1]:
        placed = placed + swap(placed, mask)
    per_dp = channels // dp_count
    packed, keep, send = call(
        project_kernel,
        [
            shape(seq, width),
            shape(far, per_dp, width, kind=F32),
            shape(far, per_dp, width),
        ],
        (me, placed, swap(placed, bits[-1]), proj_weight, grad_packed),
        scalars=1,
        flops=4 * seq * channels * width,
    )
    proj_parts = call(
        fold_kernel,
        [shape(per_dp, width, kind=F32)] + [shape(per_dp, width)] * (far - 1),
        (me, keep, swap(send, mp_count)),
        scalars=1,
    )

    grad_features = call(
        functools.partial(input_kernel, pairs=pairs, frames=frames),
        shape(utt_count * positions, channels),
        (lengths, grads, conv_weight),
        scalars=1,
        flops=2 * n1 * 2 * channels * channels,
    ).reshape(utt_count, positions, channels)

    conv_parts = call(
        functools.partial(kernel_grad_kernel, n1=n1, n2=n2, owned=owned, near=near, far=far),
        [shape(2 * owned + 8, channels, kind=F32)] + [shape(2 * owned + 8, channels)] * (far - 1),
        (me,) + tuple(by_mask[k] for k in range(near)) + tuple(in_sides),
        scalars=1,
        flops=2 * (n1 + n2) * 2 * channels * channels,
        scratch=[pltpu.VMEM((far, 2 * owned + 8, channels), F32)],
    )
    conv_got = [swap(part, near * f) if f else part for f, part in enumerate(conv_parts)]
    proj_got = [swap(part, near * f) if f else part for f, part in enumerate(proj_parts)]
    grad_conv, grad_norm, grad_proj = call(
        functools.partial(last_kernel, owned=owned, far=far),
        [
            shape(2, owned, channels, kind=F32),
            shape(2, owned, kind=F32),
            shape(per_dp, width, kind=F32),
        ],
        (me, *conv_got, *proj_got),
        scalars=1,
    )
    return (packed, grad_features, grad_conv, grad_norm, grad_proj)


def solution(mesh):
    return jax.shard_map(
        local,
        mesh=mesh,
        in_specs=(
            P(("dp", "mp"), None, None),
            P(("dp", "mp")),
            P(("dp", "mp")),
            P(("dp", "mp")),
            P(),
            P(),
            P(),
            P(None, "mp"),
            P("dp", "mp"),
        ),
        out_specs=(
            P("dp", "mp"),
            P(("dp", "mp"), None, None),
            P(None, ("dp", "mp"), None),
            P(None, ("dp", "mp")),
            P("dp", "mp"),
        ),
        check_vma=False,
    )
```

```python
import functools
import math

import jax
import jax.numpy as jnp
from jax import lax
from jax.experimental import pallas as pl
from jax.experimental.pallas import tpu as pltpu
from jax.sharding import PartitionSpec as P

epsilon = 1e-05
BF = jnp.bfloat16
F32 = jnp.float32
VMEM = pltpu.VMEM
SMEM = pltpu.SMEM


def call(body, out, args, scalars=0, flops=0, scratch=()):
    specs = [
        pl.BlockSpec(memory_space=SMEM if i < scalars else VMEM) for i in range(len(args))
    ]
    many = isinstance(out, (list, tuple))
    moved = sum(a.size * a.dtype.itemsize for a in args)
    return pl.pallas_call(
        body,
        out_shape=out,
        in_specs=specs,
        out_specs=[pl.BlockSpec(memory_space=VMEM)] * len(out)
        if many
        else pl.BlockSpec(memory_space=VMEM),
        scratch_shapes=list(scratch),
        compiler_params=pltpu.CompilerParams(vmem_limit_bytes=14 * 2**20),
        cost_estimate=pl.CostEstimate(flops=flops, bytes_accessed=moved, transcendentals=0),
    )(*args)


def shape(*dims, kind=BF):
    return jax.ShapeDtypeStruct(dims, kind)


def dot(a, b):
    return jnp.dot(a, b, preferred_element_type=F32)


def dot_nt(a, b):
    return lax.dot_general(a, b, (((1,), (1,)), ((), ())), preferred_element_type=F32)


def norm_parts(pre):
    average = jnp.mean(pre, axis=-1, keepdims=True)
    centred = pre - average
    spread = jnp.mean(centred * centred, axis=-1, keepdims=True)
    scale = lax.rsqrt(spread + epsilon)
    return centred * scale, scale


def gelu_parts(value):
    half = 0.5 * (1.0 + lax.erf(value * math.sqrt(0.5)))
    density = jnp.exp(-0.5 * value * value) * (1.0 / math.sqrt(2.0 * math.pi))
    return value * half, half + value * density


def source_of(row, me_ref, pairs, frames):
    part = lax.div(row, pairs * frames)
    inner = lax.rem(row, pairs * frames)
    pair = lax.div(inner, frames)
    t = lax.rem(inner, frames)
    first = jnp.zeros_like(row)
    for p in range(pairs):
        first = jnp.where(pair == p, me_ref[4 + 2 * p], first)
    off = jnp.where(part == 1, 2, jnp.where(part == 2, 1, part))
    t_from = jnp.where(t < first, t, t + frames - first)
    return pair * (8 * frames) + 4 * t_from + off


def index_kernel(me_ref, out_ref, *, pairs, frames):
    row = lax.broadcasted_iota(jnp.int32, out_ref.shape, 0)
    shard = lax.broadcasted_iota(jnp.int32, out_ref.shape, 1)
    value = jnp.zeros(out_ref.shape, jnp.int32)
    for p in range(pairs):
        block = lax.div(me_ref[4 + 4 * pairs + 2 * p], frames)
        value = jnp.where(shard == me_ref[4 + 2 * pairs + 2 * p], block + 1, value)
    out_ref[...] = jnp.where(row == me_ref[3], value, 0)


def block_from(got_ref, me_ref, d):
    return got_ref[2 * (me_ref[2] ^ (d // 2)) + d % 2, 2 * me_ref[2] + me_ref[3]] - 1


def forward_kernel(
    me_ref, feat_ref, weight_ref, gain_ref, shift_ref, *rest, pairs, frames, far, near, owned
):
    frames_ref, slope1_ref, slope2_ref, hat1_ref, hat2_ref, scale1_ref, scale2_ref = rest[:7]
    turned_refs, in_turned = rest[7:-1], rest[-1]
    channels = feat_ref.shape[1]
    n2 = pairs * frames
    row = lax.broadcasted_iota(jnp.int32, (4 * n2, 1), 0)
    source = source_of(row, me_ref, pairs, frames)
    place = lax.broadcasted_iota(jnp.int32, (4 * n2, feat_ref.shape[0]), 1)
    pick = jnp.where(place == source, 1.0, 0.0).astype(BF)
    chosen32 = dot(pick, feat_ref[...])
    chosen = chosen32.astype(BF)
    even, odd = chosen[: 2 * n2], chosen[2 * n2 :]
    first = dot(even, weight_ref[0, :channels, :]) + dot(odd, weight_ref[0, channels:, :])
    hat, scale = norm_parts(first)
    hidden, slope = gelu_parts(hat * gain_ref[0:1, :] + shift_ref[0:1, :])
    slope1_ref[...] = slope
    hat1_ref[...] = hat
    scale1_ref[...] = jnp.broadcast_to(scale, scale1_ref.shape)
    hidden = hidden.astype(BF)
    hidden32 = hidden.astype(F32)
    second = dot(hidden[:n2], weight_ref[1, :channels, :]) + dot(
        hidden[n2:], weight_ref[1, channels:, :]
    )
    hat, scale = norm_parts(second)
    made, slope = gelu_parts(hat * gain_ref[1:2, :] + shift_ref[1:2, :])
    slope2_ref[...] = slope
    hat2_ref[...] = hat
    scale2_ref[...] = jnp.broadcast_to(scale, scale2_ref.shape)
    frames_ref[...] = made.astype(BF)
    wide = in_turned.shape[1]
    fill = [jnp.zeros((wide - 3 * n2, channels), F32)] if wide > 3 * n2 else []
    for tap in range(2):
        stacked = jnp.concatenate(
            [chosen32[2 * n2 * tap : 2 * n2 * (tap + 1)], hidden32[n2 * tap : n2 * (tap + 1)]] + fill,
            axis=0,
        )
        in_turned[channels * tap : channels * (tap + 1), :] = stacked.T
    at = me_ref[1]
    for k, turned_ref in enumerate(turned_refs):
        start = (at ^ k) * owned
        turned_ref[...] = jnp.concatenate(
            [
                in_turned[pl.ds(pl.multiple_of(z * near * owned + start, owned), owned), :]
                for z in range(far)
            ],
            axis=0,
        ).astype(BF)


def send_kernel(got_ref, me_ref, mine_ref, other_ref, frames_ref, out_ref, rows32, *, pairs, frames):
    rows32[...] = mine_ref[...].astype(F32) + other_ref[...].astype(F32)
    blocks = rows32.shape[0] // frames
    made = frames_ref[...].astype(F32)
    none = jnp.zeros((frames, made.shape[1]), F32)
    for d in range(out_ref.shape[0]):
        block = block_from(got_ref, me_ref, d)
        safe = jnp.clip(block, 0, blocks - 1)
        grads = rows32[pl.ds(pl.multiple_of(safe * frames, frames), frames), :]
        grads = jnp.where(block >= 0, grads, none)
        sent = none
        for p in range(pairs):
            sent = jnp.where(me_ref[4 + 2 * pairs + 2 * p] == d, made[p * frames : (p + 1) * frames], sent)
        out_ref[d] = jnp.concatenate([grads, sent], axis=0).astype(BF)


def place_kernel(got_ref, me_ref, slots_ref, out_ref, rows32, *, frames):
    rows32[...] = jnp.zeros_like(rows32)
    for d in range(slots_ref.shape[0]):
        block = block_from(got_ref, me_ref, d)

        @pl.when(block >= 0)
        def _():
            safe = jnp.clip(block, 0, rows32.shape[0] // frames - 1)
            rows32[pl.ds(pl.multiple_of(safe * frames, frames), frames), :] = slots_ref[d].astype(F32)[
                frames:
            ]

    out_ref[...] = rows32[...].astype(BF)


def project_kernel(me_ref, mine_ref, other_ref, weight_ref, cotangent_ref, packed_ref, keep_ref, send_ref):
    rows32 = mine_ref[...].astype(F32) + other_ref[...].astype(F32)
    packed_ref[...] = dot_nt(weight_ref[...], rows32.astype(BF)).astype(BF)
    partial = dot_nt(rows32.T.astype(BF), cotangent_ref[...])
    each = keep_ref.shape[1]
    for z in range(keep_ref.shape[0]):
        low = partial[2 * z * each : (2 * z + 1) * each]
        high = partial[(2 * z + 1) * each : (2 * z + 2) * each]
        keep_ref[z] = jnp.where(me_ref[3] == 0, low, high)
        send_ref[z] = jnp.where(me_ref[3] == 0, high, low).astype(BF)


def fold_kernel(me_ref, keep_ref, got_ref, own_ref, *out_refs):
    for f in range(keep_ref.shape[0]):
        z = me_ref[2] ^ f
        total = keep_ref[z] + got_ref[z].astype(F32)
        if f == 0:
            own_ref[...] = total
        else:
            out_refs[f - 1][...] = total.astype(BF)


def norm_back(grad, slope_ref, hat_ref, scale_ref, gain):
    pre = grad * slope_ref[...]
    hat = hat_ref[...]
    by_hat = pre * hat
    inner = pre * gain
    average = jnp.mean(inner, axis=-1, keepdims=True)
    along = jnp.mean(inner * hat, axis=-1, keepdims=True)
    back = (inner - average - hat * along) * scale_ref[:, 0:1]
    return (
        back.astype(BF),
        jnp.sum(by_hat, axis=0, keepdims=True),
        jnp.sum(pre, axis=0, keepdims=True),
    )


def back_kernel(
    me_ref, slots_ref, slope1_ref, slope2_ref, hat1_ref, hat2_ref, scale1_ref, scale2_ref,
    weight_ref, gain_ref, out_ref, grads32, *, pairs, frames
):
    channels = weight_ref.shape[2]
    for p in range(pairs):
        slot = jnp.clip(me_ref[4 + 2 * pairs + 2 * p], 0, slots_ref.shape[0] - 1)
        grads32[p * frames : (p + 1) * frames, :] = slots_ref[slot].astype(F32)[:frames]
    second, gain2, shift2 = norm_back(grads32[...], slope2_ref, hat2_ref, scale2_ref, gain_ref[1:2, :])
    hidden = jnp.concatenate(
        [
            dot_nt(second, weight_ref[1, :channels, :]),
            dot_nt(second, weight_ref[1, channels:, :]),
        ],
        axis=0,
    )
    hidden = hidden.astype(BF).astype(F32)
    first, gain1, shift1 = norm_back(hidden, slope1_ref, hat1_ref, scale1_ref, gain_ref[0:1, :])
    sums = jnp.concatenate([gain1, shift1, gain2, shift2], axis=0)
    high = sums.astype(BF).astype(F32)
    rows = [high, sums - high, jnp.zeros((8, channels), F32)]
    n1, n2 = first.shape[0], second.shape[0]
    out_ref[:n1, :] = first
    out_ref[n1 : n1 + n2, :] = second
    out_ref[n1 + n2 :, :] = jnp.concatenate(rows, axis=0).astype(BF)


def input_kernel(me_ref, grad_ref, weight_ref, out_ref, *, pairs, frames):
    channels = weight_ref.shape[2]
    n1 = 2 * pairs * frames
    first = grad_ref[:n1, :]
    rows = jnp.concatenate(
        [dot_nt(first, weight_ref[0, :channels, :]), dot_nt(first, weight_ref[0, channels:, :])],
        axis=0,
    ).astype(BF)
    row = lax.broadcasted_iota(jnp.int32, (1, 2 * n1), 1)
    source = source_of(row, me_ref, pairs, frames)
    place = lax.broadcasted_iota(jnp.int32, (out_ref.shape[0], 2 * n1), 0)
    pick = jnp.where(place == source, 1.0, 0.0).astype(BF)
    out_ref[...] = dot(pick, rows).astype(BF)


def kernel_grad_kernel(me_ref, *refs, n1, n2, owned, near, far):
    grad_refs, in_refs = refs[:near], refs[near : 2 * near]
    own_ref, out_refs, held = refs[2 * near], refs[2 * near + 1 : -1], refs[-1]
    first, second, sums = 0.0, 0.0, 0.0
    for grad_ref, in_ref in zip(grad_refs, in_refs):
        side = in_ref[...]
        first += dot(side[:, :n1], grad_ref[:n1, :])
        second += dot(side[:, n1 : n1 + n2], grad_ref[n1 : n1 + n2, :])
        tail = grad_ref[n1 + n2 :, :].astype(F32)
        sums += tail[0:4] + tail[4:8]
    high = sums.astype(BF).astype(F32)
    for z in range(far):
        held[z] = jnp.concatenate(
            [first[z * owned : (z + 1) * owned], second[z * owned : (z + 1) * owned], high, sums - high],
            axis=0,
        )
    own_ref[...] = held[me_ref[2]]
    for f in range(1, far):
        out_refs[f - 1][...] = held[me_ref[2] ^ f].astype(BF)


def last_kernel(me_ref, *refs, owned, far):
    conv_in, proj_in = refs[:far], refs[far : 2 * far]
    conv_ref, norm_ref, proj_ref = refs[2 * far :]
    total = conv_in[0][...]
    proj = proj_in[0][...]
    for f in range(1, far):
        total += conv_in[f][...].astype(F32)
        proj += proj_in[f][...].astype(F32)
    conv_ref[0] = total[:owned]
    conv_ref[1] = total[owned : 2 * owned]
    proj_ref[...] = proj
    channels = total.shape[1]
    sums = total[2 * owned : 2 * owned + 4] + total[2 * owned + 4 : 2 * owned + 8]
    start = me_ref[0] * owned
    later = start >= channels
    lines = jnp.concatenate(
        [jnp.where(later, sums[2 * k + 1 : 2 * k + 2], sums[2 * k : 2 * k + 1]) for k in range(2)]
        + [jnp.zeros((6, channels), F32)],
        axis=0,
    )
    start = jnp.where(later, start - channels, start)
    lines = pltpu.roll(lines, lax.rem(channels - start, channels), 1)
    norm_ref[...] = lines[:2, :owned]


def local(
    features, lengths, dests, offsets, conv_weight, norm_gain, norm_shift, proj_weight, grad_packed
):
    utt_count, positions, channels = features.shape
    frames = positions // 4
    pairs = utt_count // 2
    dp_count = lax.axis_size("dp")
    mp_count = lax.axis_size("mp")
    seq = grad_packed.shape[0]
    width = grad_packed.shape[1]
    owned = 2 * channels // (dp_count * mp_count)
    n1, n2 = 2 * pairs * frames, pairs * frames
    near, far = 2 * mp_count, dp_count // 2
    everyone = ("dp", "mp")

    def swap(x, mask):
        return lax.ppermute(x, everyone, [(i, i ^ mask) for i in range(dp_count * mp_count)])

    bits = [1 << b for b in range(mp_count.bit_length() - 1)][::-1]
    at_dp = lax.axis_index("dp").astype(jnp.int32)
    at_mp = lax.axis_index("mp").astype(jnp.int32)
    x_bit = at_dp & 1
    place = jnp.stack([at_dp * mp_count + at_mp, x_bit * mp_count + at_mp, at_dp >> 1, x_bit])
    me = jnp.concatenate([place, lengths, dests, offsets])

    index = call(
        functools.partial(index_kernel, pairs=pairs, frames=frames),
        shape(2, -(-dp_count // 128) * 128, kind=jnp.int32),
        (me,),
        scalars=1,
    )
    index = index + swap(index, mp_count)
    got_index = jnp.concatenate([index] + [swap(index, near * f) for f in range(1, far)], axis=0)

    wide = -(-(n1 + n2) // 128) * 128
    feat = features.reshape(utt_count * positions, channels)
    made = call(
        functools.partial(
            forward_kernel, pairs=pairs, frames=frames, far=far, near=near, owned=owned
        ),
        [
            shape(n2, channels),
            shape(n1, channels, kind=F32),
            shape(n2, channels, kind=F32),
            shape(n1, channels, kind=F32),
            shape(n2, channels, kind=F32),
            shape(n1, 128, kind=F32),
            shape(n2, 128, kind=F32),
        ]
        + [shape(far * owned, wide)] * near,
        (me, feat, conv_weight, norm_gain, norm_shift),
        scalars=1,
        flops=2 * (n1 + n2) * 2 * channels * channels,
        scratch=[pltpu.VMEM((2 * channels, wide), F32)],
    )
    pair_frames, slope1, slope2, hat1, hat2, scale1, scale2 = made[:7]
    in_sides = [side if k == 0 else swap(side, k) for k, side in enumerate(made[7:])]

    grad_rows = lax.dot_general(
        grad_packed, proj_weight, (((1,), (1,)), ((), ())), preferred_element_type=F32
    ).astype(BF)
    for mask in bits[:-1]:
        grad_rows = (grad_rows.astype(F32) + swap(grad_rows, mask).astype(F32)).astype(BF)
    other_rows = swap(grad_rows, bits[-1])

    sent = call(
        functools.partial(send_kernel, pairs=pairs, frames=frames),
        shape(dp_count, 2 * frames, channels),
        (got_index, me, grad_rows, other_rows, pair_frames),
        scalars=2,
        scratch=[pltpu.VMEM((seq, channels), F32)],
    )
    slots = lax.all_to_all(sent, "dp", split_axis=0, concat_axis=0, tiled=True)
    slots, *in_sides = lax.optimization_barrier((slots, *in_sides))

    grads = call(
        functools.partial(back_kernel, pairs=pairs, frames=frames),
        shape(n1 + n2 + 16, channels),
        (me, slots, slope1, slope2, hat1, hat2, scale1, scale2, conv_weight, norm_gain),
        scalars=1,
        flops=2 * n2 * 2 * channels * channels,
        scratch=[pltpu.VMEM((n2, channels), F32)],
    )
    by_mask = {mask: swap(grads, mask) if mask else grads for mask in range(0, near, 2)}
    for mask in range(0, near, 2):
        by_mask[mask + 1] = swap(by_mask[mask], 1)

    placed = call(
        functools.partial(place_kernel, frames=frames),
        shape(seq, channels),
        (got_index, me, slots),
        scalars=2,
        scratch=[pltpu.VMEM((seq, channels), F32)],
    )
    for mask in bits[:-1]:
        placed = placed + swap(placed, mask)
    per_dp = channels // dp_count
    packed, keep, send = call(
        project_kernel,
        [
            shape(width, seq),
            shape(far, per_dp, width, kind=F32),
            shape(far, per_dp, width),
        ],
        (me, placed, swap(placed, bits[-1]), proj_weight.T, grad_packed.T),
        scalars=1,
        flops=4 * seq * channels * width,
    )
    proj_parts = call(
        fold_kernel,
        [shape(per_dp, width, kind=F32)] + [shape(per_dp, width)] * (far - 1),
        (me, keep, swap(send, mp_count)),
        scalars=1,
    )

    grad_features = call(
        functools.partial(input_kernel, pairs=pairs, frames=frames),
        shape(utt_count * positions, channels),
        (me, grads, conv_weight),
        scalars=1,
        flops=2 * n1 * 2 * channels * channels,
    ).reshape(utt_count, positions, channels)

    conv_parts = call(
        functools.partial(kernel_grad_kernel, n1=n1, n2=n2, owned=owned, near=near, far=far),
        [shape(2 * owned + 8, channels, kind=F32)] + [shape(2 * owned + 8, channels)] * (far - 1),
        (me,) + tuple(by_mask[k] for k in range(near)) + tuple(in_sides),
        scalars=1,
        flops=2 * (n1 + n2) * 2 * channels * channels,
        scratch=[pltpu.VMEM((far, 2 * owned + 8, channels), F32)],
    )
    conv_got = [swap(part, near * f) if f else part for f, part in enumerate(conv_parts)]
    proj_got = [swap(part, near * f) if f else part for f, part in enumerate(proj_parts)]
    grad_conv, grad_norm, grad_proj = call(
        functools.partial(last_kernel, owned=owned, far=far),
        [
            shape(2, owned, channels, kind=F32),
            shape(2, owned, kind=F32),
            shape(per_dp, width, kind=F32),
        ],
        (me, *conv_got, *proj_got),
        scalars=1,
    )
    return (packed.T, grad_features, grad_conv, grad_norm, grad_proj)


def solution(mesh):
    return jax.shard_map(
        local,
        mesh=mesh,
        in_specs=(
            P(("dp", "mp"), None, None),
            P(("dp", "mp")),
            P(("dp", "mp")),
            P(("dp", "mp")),
            P(),
            P(),
            P(),
            P(None, "mp"),
            P("dp", "mp"),
        ),
        out_specs=(
            P("dp", "mp"),
            P(("dp", "mp"), None, None),
            P(None, ("dp", "mp"), None),
            P(None, ("dp", "mp")),
            P("dp", "mp"),
        ),
        check_vma=False,
    )
```

```python
import functools
import math

import jax
import jax.numpy as jnp
from jax import lax
from jax.experimental import pallas as pl
from jax.experimental.pallas import tpu as pltpu
from jax.sharding import PartitionSpec as P

epsilon = 1e-05
BF = jnp.bfloat16
F32 = jnp.float32
VMEM = pltpu.VMEM
SMEM = pltpu.SMEM


def call(body, out, args, scalars=0, fetched=0, flops=0, scratch=(), mebibytes=14, to_scalars=0):
    specs = [
        pl.BlockSpec(memory_space=SMEM if i < scalars else pl.ANY if i < scalars + fetched else VMEM)
        for i in range(len(args))
    ]
    many = isinstance(out, (list, tuple))
    moved = sum(a.size * a.dtype.itemsize for a in args)
    return pl.pallas_call(
        body,
        out_shape=out,
        in_specs=specs,
        out_specs=[
            pl.BlockSpec(memory_space=SMEM if i < to_scalars else VMEM) for i in range(len(out))
        ]
        if many
        else pl.BlockSpec(memory_space=VMEM),
        scratch_shapes=list(scratch),
        compiler_params=pltpu.CompilerParams(vmem_limit_bytes=mebibytes * 2**20),
        cost_estimate=pl.CostEstimate(flops=flops, bytes_accessed=moved, transcendentals=0),
    )(*args)


def shape(*dims, kind=BF):
    return jax.ShapeDtypeStruct(dims, kind)


def dot(a, b):
    return jnp.dot(a, b, preferred_element_type=F32)


def dot_nt(a, b):
    return lax.dot_general(a, b, (((1,), (1,)), ((), ())), preferred_element_type=F32)


def norm_parts(pre):
    average = jnp.mean(pre, axis=-1, keepdims=True)
    centred = pre - average
    spread = jnp.mean(centred * centred, axis=-1, keepdims=True)
    scale = lax.rsqrt(spread + epsilon)
    return centred * scale, scale


def gelu_parts(value):
    half = 0.5 * (1.0 + lax.erf(value * math.sqrt(0.5)))
    density = jnp.exp(-0.5 * value * value) * (1.0 / math.sqrt(2.0 * math.pi))
    return value * half, half + value * density


def source_of(row, me_ref, pairs, frames):
    part = lax.div(row, pairs * frames)
    inner = lax.rem(row, pairs * frames)
    pair = lax.div(inner, frames)
    t = lax.rem(inner, frames)
    first = jnp.zeros_like(row)
    for p in range(pairs):
        first = jnp.where(pair == p, me_ref[4 + 2 * p], first)
    off = jnp.where(part == 1, 2, jnp.where(part == 2, 1, part))
    t_from = jnp.where(t < first, t, t + frames - first)
    return pair * (8 * frames) + 4 * t_from + off


def start_kernel(
    place_ref, proj_hbm, cotangent_hbm, lengths_hbm, dests_hbm, offsets_hbm, me_ref, index_ref, rows_ref,
    proj_ref, cotangent_ref, lengths_ref, dests_ref, offsets_ref, copied, *, pairs, frames
):
    sources = (proj_hbm, cotangent_hbm, lengths_hbm, dests_hbm, offsets_hbm)
    targets = (proj_ref, cotangent_ref, lengths_ref, dests_ref, offsets_ref)
    copies = [
        pltpu.make_async_copy(source, target, copied.at[i])
        for i, (source, target) in enumerate(zip(sources, targets))
    ]
    for copy in copies[::-1]:
        copy.start()
    for copy in copies[2:]:
        copy.wait()
    for i in range(4):
        me_ref[i] = place_ref[i]
    for i in range(2 * pairs):
        me_ref[4 + i] = lengths_ref[i]
        me_ref[4 + 2 * pairs + i] = dests_ref[i]
        me_ref[4 + 4 * pairs + i] = offsets_ref[i]
    shard = lax.broadcasted_iota(jnp.int32, index_ref.shape, 1)
    value = jnp.zeros(index_ref.shape, jnp.int32)
    for p in range(pairs):
        block = lax.div(offsets_ref[2 * p], frames)
        value = jnp.where(shard == dests_ref[2 * p], block + 1, value)
    index_ref[...] = value
    copies[0].wait()
    copies[1].wait()
    rows_ref[...] = lax.dot_general(
        cotangent_ref[...], proj_ref[...], (((0,), (0,)), ((), ())), preferred_element_type=F32
    ).astype(BF)


def block_from(got_ref, me_ref, d):
    return got_ref[d, 2 * me_ref[2] + me_ref[3]] - 1


def state_views(state_ref):
    part = state_ref.shape[0] // 9
    spans = ((0, 2), (2, 1), (3, 2), (5, 1), (6, 2), (8, 1))
    return [state_ref.at[a * part : (a + n) * part] for a, n in spans]


def forward_kernel(me_ref, *refs, pairs, frames, far, near, owned):
    weight_ref = refs[3]
    sources = refs[:3] + (weight_ref.at[0], weight_ref.at[1])
    rest, held, in_turned, copied = refs[4:-7], refs[-7:-2], refs[-2], refs[-1]
    copies = [
        pltpu.make_async_copy(source, target, copied.at[i])
        for i, (source, target) in enumerate(zip(sources, held))
    ]
    for copy in copies:
        copy.start()
    feat_ref, gain_ref, shift_ref, first_ref, second_ref = held
    later_ref, frames_ref, state_ref = rest[:3]
    turned_refs = rest[3:]
    for i in range(me_ref.shape[0]):
        later_ref[i] = me_ref[i]
    slope1_ref, slope2_ref, hat1_ref, hat2_ref, scale1_ref, scale2_ref = state_views(state_ref)
    copies[0].wait()
    channels = feat_ref.shape[1]
    n2 = pairs * frames
    row = lax.broadcasted_iota(jnp.int32, (4 * n2, 1), 0)
    source = source_of(row, me_ref, pairs, frames)
    place = lax.broadcasted_iota(jnp.int32, (4 * n2, feat_ref.shape[0]), 1)
    pick = jnp.where(place == source, 1.0, 0.0).astype(BF)
    chosen32 = dot(pick, feat_ref[...])
    chosen = chosen32.astype(BF)
    for copy in copies[1:4]:
        copy.wait()
    even, odd = chosen[: 2 * n2], chosen[2 * n2 :]
    first = dot(even, first_ref[:channels, :]) + dot(odd, first_ref[channels:, :])
    hat, scale = norm_parts(first)
    hidden, slope = gelu_parts(hat * gain_ref[0:1, :] + shift_ref[0:1, :])
    slope1_ref[...] = slope
    hat1_ref[...] = hat
    scale1_ref[...] = jnp.broadcast_to(scale, scale1_ref.shape)
    hidden = hidden.astype(BF)
    hidden32 = hidden.astype(F32)
    copies[4].wait()
    second = dot(hidden[:n2], second_ref[:channels, :]) + dot(hidden[n2:], second_ref[channels:, :])
    hat, scale = norm_parts(second)
    made, slope = gelu_parts(hat * gain_ref[1:2, :] + shift_ref[1:2, :])
    slope2_ref[...] = slope
    hat2_ref[...] = hat
    scale2_ref[...] = jnp.broadcast_to(scale, scale2_ref.shape)
    frames_ref[...] = made.astype(BF)
    wide = in_turned.shape[1]
    fill = [jnp.zeros((wide - 3 * n2, channels), F32)] if wide > 3 * n2 else []
    for tap in range(2):
        stacked = jnp.concatenate(
            [chosen32[2 * n2 * tap : 2 * n2 * (tap + 1)], hidden32[n2 * tap : n2 * (tap + 1)]] + fill,
            axis=0,
        )
        in_turned[channels * tap : channels * (tap + 1), :] = stacked.T
    at = me_ref[1]
    for k, turned_ref in enumerate(turned_refs):
        turned_ref[...] = jnp.concatenate(
            [
                in_turned[pl.ds(pl.multiple_of((z * near + (at ^ (2 * k + c))) * owned, owned), owned), :]
                for c in range(2)
                for z in range(far)
            ],
            axis=0,
        ).astype(BF)


def send_kernel(got_ref, me_ref, mine_ref, other_ref, frames_ref, out_ref, rows32, *, pairs, frames):
    rows32[...] = mine_ref[...].astype(F32) + other_ref[...].astype(F32)
    blocks = rows32.shape[0] // frames
    made = frames_ref[...].astype(F32)
    none = jnp.zeros((frames, made.shape[1]), F32)
    for d in range(out_ref.shape[0]):
        block = block_from(got_ref, me_ref, d)
        safe = jnp.clip(block, 0, blocks - 1)
        grads = rows32[pl.ds(pl.multiple_of(safe * frames, frames), frames), :]
        grads = jnp.where(block >= 0, grads, none)
        sent = none
        for p in range(pairs):
            sent = jnp.where(me_ref[4 + 2 * pairs + 2 * p] == d, made[p * frames : (p + 1) * frames], sent)
        out_ref[d] = jnp.concatenate([grads, sent], axis=0).astype(BF)


def place_kernel(got_ref, me_ref, slots_ref, out_ref, rows32, *, frames):
    rows32[...] = jnp.zeros_like(rows32)
    for d in range(slots_ref.shape[0]):
        block = block_from(got_ref, me_ref, d)

        @pl.when(block >= 0)
        def _():
            safe = jnp.clip(block, 0, rows32.shape[0] // frames - 1)
            rows32[pl.ds(pl.multiple_of(safe * frames, frames), frames), :] = slots_ref[d].astype(F32)[
                frames:
            ]

    out_ref[...] = rows32[...].astype(BF)


def pack(rows, channels):
    r, w = rows.shape
    parts, start = [], 0
    while start < w:
        lanes = min(1 << ((w - start).bit_length() - 1), channels)
        each = r * lanes // channels
        parts.append(
            jnp.concatenate(
                [rows[g * each : (g + 1) * each, start : start + lanes] for g in range(r // each)], axis=1
            )
        )
        start += lanes
    return jnp.concatenate(parts, axis=0)


def unpack(packed, r, w):
    channels = packed.shape[1]
    parts, start, at = [], 0, 0
    while start < w:
        lanes = min(1 << ((w - start).bit_length() - 1), channels)
        each = r * lanes // channels
        block = packed[at : at + each]
        parts.append(
            jnp.concatenate([block[:, g * lanes : (g + 1) * lanes] for g in range(r // each)], axis=0)
        )
        start += lanes
        at += each
    return jnp.concatenate(parts, axis=1)


def project_kernel(me_ref, mine_ref, other_ref, weight_ref, cotangent_ref, packed_ref, keep_ref, send_ref):
    rows32 = mine_ref[...].astype(F32) + other_ref[...].astype(F32)
    packed_ref[...] = dot_nt(weight_ref[...], rows32.astype(BF)).astype(BF)
    partial = dot_nt(rows32.T.astype(BF), cotangent_ref[...])
    channels, width = partial.shape
    each = channels // (2 * keep_ref.shape[0])
    for z in range(keep_ref.shape[0]):
        low = pack(partial[2 * z * each : (2 * z + 1) * each], channels)
        high = pack(partial[(2 * z + 1) * each : (2 * z + 2) * each], channels)
        keep_ref[z] = jnp.where(me_ref[3] == 0, low, high)
        send_ref[z] = jnp.where(me_ref[3] == 0, high, low).astype(BF)


def fold_kernel(me_ref, keep_ref, got_ref, own_ref, *out_refs):
    for f in range(keep_ref.shape[0]):
        z = me_ref[2] ^ f
        total = keep_ref[z] + got_ref[z].astype(F32)
        if f == 0:
            own_ref[...] = total
        else:
            out_refs[f - 1][...] = total.astype(BF)


def norm_back(grad, slope_ref, hat_ref, scale_ref, gain):
    pre = grad * slope_ref[...]
    hat = hat_ref[...]
    by_hat = pre * hat
    inner = pre * gain
    average = jnp.mean(inner, axis=-1, keepdims=True)
    along = jnp.mean(inner * hat, axis=-1, keepdims=True)
    back = (inner - average - hat * along) * scale_ref[:, 0:1]
    return (
        back.astype(BF),
        jnp.sum(by_hat, axis=0, keepdims=True),
        jnp.sum(pre, axis=0, keepdims=True),
    )


def back_kernel(
    me_ref, slots_ref, state_ref, weight_ref, gain_ref, out_ref, grads32, *, pairs, frames
):
    channels = weight_ref.shape[2]
    slope1_ref, slope2_ref, hat1_ref, hat2_ref, scale1_ref, scale2_ref = state_views(state_ref)
    for p in range(pairs):
        slot = jnp.clip(me_ref[4 + 2 * pairs + 2 * p], 0, slots_ref.shape[0] - 1)
        grads32[p * frames : (p + 1) * frames, :] = slots_ref[slot].astype(F32)[:frames]
    second, gain2, shift2 = norm_back(grads32[...], slope2_ref, hat2_ref, scale2_ref, gain_ref[1:2, :])
    hidden = jnp.concatenate(
        [
            dot_nt(second, weight_ref[1, :channels, :]),
            dot_nt(second, weight_ref[1, channels:, :]),
        ],
        axis=0,
    )
    hidden = hidden.astype(BF).astype(F32)
    first, gain1, shift1 = norm_back(hidden, slope1_ref, hat1_ref, scale1_ref, gain_ref[0:1, :])
    sums = jnp.concatenate([gain1, shift1, gain2, shift2], axis=0)
    high = sums.astype(BF).astype(F32)
    rows = [high, sums - high, jnp.zeros((8, channels), F32)]
    n1, n2 = first.shape[0], second.shape[0]
    out_ref[:n1, :] = first
    out_ref[n1 : n1 + n2, :] = second
    out_ref[n1 + n2 :, :] = jnp.concatenate(rows, axis=0).astype(BF)


def input_kernel(me_ref, grad_ref, weight_ref, out_ref, *, pairs, frames):
    channels = weight_ref.shape[2]
    n1 = 2 * pairs * frames
    first = grad_ref[:n1, :]
    rows = jnp.concatenate(
        [dot_nt(first, weight_ref[0, :channels, :]), dot_nt(first, weight_ref[0, channels:, :])],
        axis=0,
    ).astype(BF)
    row = lax.broadcasted_iota(jnp.int32, (1, 2 * n1), 1)
    source = source_of(row, me_ref, pairs, frames)
    place = lax.broadcasted_iota(jnp.int32, (out_ref.shape[0], 2 * n1), 0)
    pick = jnp.where(place == source, 1.0, 0.0).astype(BF)
    out_ref[...] = dot(pick, rows).astype(BF)


def kernel_grad_kernel(me_ref, *refs, n1, n2, owned, near, far):
    grad_refs, side_refs = refs[:near], refs[near : 2 * near]
    rows = side_refs[0].shape[0] // 2
    in_refs = [
        side_refs[near // 2 * (k % 2) + k // 2].at[k % 2 * rows : (k % 2 + 1) * rows] for k in range(near)
    ]
    own_ref, out_refs, held = refs[2 * near], refs[2 * near + 1 : -1], refs[-1]
    first, second, sums = 0.0, 0.0, 0.0
    for grad_ref, in_ref in zip(grad_refs, in_refs):
        side = in_ref[...]
        first += dot(side[:, :n1], grad_ref[:n1, :])
        second += dot(side[:, n1 : n1 + n2], grad_ref[n1 : n1 + n2, :])
        tail = grad_ref[n1 + n2 :, :].astype(F32)
        sums += tail[0:4] + tail[4:8]
    high = sums.astype(BF).astype(F32)
    for z in range(far):
        held[z] = jnp.concatenate(
            [first[z * owned : (z + 1) * owned], second[z * owned : (z + 1) * owned], high, sums - high],
            axis=0,
        )
    own_ref[...] = held[me_ref[2]]
    for f in range(1, far):
        out_refs[f - 1][...] = held[me_ref[2] ^ f].astype(BF)


def last_kernel(me_ref, *refs, owned, far):
    conv_in, proj_in = refs[:far], refs[far : 2 * far]
    conv_ref, norm_ref, proj_ref = refs[2 * far :]
    total = conv_in[0][...]
    proj = proj_in[0][...]
    for f in range(1, far):
        total += conv_in[f][...].astype(F32)
        proj += proj_in[f][...].astype(F32)
    conv_ref[0] = total[:owned]
    conv_ref[1] = total[owned : 2 * owned]
    proj_ref[...] = unpack(proj, *proj_ref.shape)
    channels = total.shape[1]
    sums = total[2 * owned : 2 * owned + 4] + total[2 * owned + 4 : 2 * owned + 8]
    start = me_ref[0] * owned
    later = start >= channels
    lines = jnp.concatenate(
        [jnp.where(later, sums[2 * k + 1 : 2 * k + 2], sums[2 * k : 2 * k + 1]) for k in range(2)]
        + [jnp.zeros((6, channels), F32)],
        axis=0,
    )
    start = jnp.where(later, start - channels, start)
    lines = pltpu.roll(lines, lax.rem(channels - start, channels), 1)
    norm_ref[...] = lines[:2, :owned]


def local(
    features, lengths, dests, offsets, conv_weight, norm_gain, norm_shift, proj_weight, grad_packed
):
    utt_count, positions, channels = features.shape
    frames = positions // 4
    pairs = utt_count // 2
    dp_count = lax.axis_size("dp")
    mp_count = lax.axis_size("mp")
    seq = grad_packed.shape[0]
    width = grad_packed.shape[1]
    owned = 2 * channels // (dp_count * mp_count)
    n1, n2 = 2 * pairs * frames, pairs * frames
    near, far = 2 * mp_count, dp_count // 2
    everyone = ("dp", "mp")

    def swap(x, mask):
        return lax.ppermute(x, everyone, [(i, i ^ mask) for i in range(dp_count * mp_count)])

    bits = [1 << b for b in range(mp_count.bit_length() - 1)][::-1]
    at_dp = lax.axis_index("dp").astype(jnp.int32)
    at_mp = lax.axis_index("mp").astype(jnp.int32)
    x_bit = at_dp & 1
    place = jnp.stack([at_dp * mp_count + at_mp, x_bit * mp_count + at_mp, at_dp >> 1, x_bit])
    me, index, grad_rows = call(
        functools.partial(start_kernel, pairs=pairs, frames=frames),
        [
            shape(4 + 6 * pairs, kind=jnp.int32),
            shape(dp_count, -(-dp_count // 128) * 128, kind=jnp.int32),
            shape(seq, channels),
        ],
        (place, proj_weight.T, grad_packed.T, lengths, dests, offsets),
        scalars=1,
        fetched=5,
        to_scalars=1,
        flops=2 * seq * width * channels,
        scratch=[
            pltpu.VMEM((width, channels), BF),
            pltpu.VMEM((width, seq), BF),
            pltpu.SMEM(lengths.shape, jnp.int32),
            pltpu.SMEM(dests.shape, jnp.int32),
            pltpu.SMEM(offsets.shape, jnp.int32),
            pltpu.SemaphoreType.DMA((5,)),
        ],
        mebibytes=56,
    )
    feat = features.reshape(utt_count * positions, channels)
    got_index = lax.all_to_all(index, "dp", split_axis=0, concat_axis=0, tiled=True)

    wide = -(-(n1 + n2) // 128) * 128
    tall = (2 * channels, channels)
    made = call(
        functools.partial(
            forward_kernel, pairs=pairs, frames=frames, far=far, near=near, owned=owned
        ),
        [
            shape(*me.shape, kind=jnp.int32),
            shape(n2, channels),
            shape(3 * (n1 + n2), channels, kind=F32),
        ]
        + [shape(2 * far * owned, wide)] * (near // 2),
        (me, feat, norm_gain, norm_shift, conv_weight),
        scalars=1,
        fetched=4,
        to_scalars=1,
        flops=2 * (n1 + n2) * 2 * channels * channels,
        scratch=[
            pltpu.VMEM(feat.shape, BF),
            pltpu.VMEM(norm_gain.shape, F32),
            pltpu.VMEM(norm_shift.shape, F32),
            pltpu.VMEM(tall, BF),
            pltpu.VMEM(tall, BF),
            pltpu.VMEM((2 * channels, wide), F32),
            pltpu.SemaphoreType.DMA((5,)),
        ],
        mebibytes=56,
    )
    me, pair_frames, state = made[:3]
    in_sides = [swap(side, 2 * k) if k else side for k, side in enumerate(made[3:])]
    in_sides += [swap(side, 1) for side in in_sides]

    for mask in bits[:-1]:
        arrived, pair_frames, got_index = lax.optimization_barrier(
            (swap(grad_rows, mask), pair_frames, got_index)
        )
        grad_rows = (grad_rows.astype(F32) + arrived.astype(F32)).astype(BF)
    other_rows = swap(grad_rows, bits[-1])

    sent = call(
        functools.partial(send_kernel, pairs=pairs, frames=frames),
        shape(dp_count, 2 * frames, channels),
        (got_index, me, grad_rows, other_rows, pair_frames),
        scalars=2,
        scratch=[pltpu.VMEM((seq, channels), F32)],
    )
    slots = lax.all_to_all(sent, "dp", split_axis=0, concat_axis=0, tiled=True)
    slots, *in_sides = lax.optimization_barrier((slots, *in_sides))

    grads = call(
        functools.partial(back_kernel, pairs=pairs, frames=frames),
        shape(n1 + n2 + 16, channels),
        (me, slots, state, conv_weight, norm_gain),
        scalars=1,
        flops=2 * n2 * 2 * channels * channels,
        scratch=[pltpu.VMEM((n2, channels), F32)],
    )
    by_mask = {mask: swap(grads, mask) if mask else grads for mask in range(0, near, 2)}
    for mask in range(0, near, 2):
        by_mask[mask + 1] = swap(by_mask[mask], 1)

    placed = call(
        functools.partial(place_kernel, frames=frames),
        shape(seq, channels),
        (got_index, me, slots),
        scalars=2,
        scratch=[pltpu.VMEM((seq, channels), F32)],
    )
    for mask in bits[:-1]:
        placed = placed + swap(placed, mask)
    per_dp = channels // dp_count
    packed, keep, send = call(
        project_kernel,
        [
            shape(width, seq),
            shape(far, per_dp * width // channels, channels, kind=F32),
            shape(far, per_dp * width // channels, channels),
        ],
        (me, placed, swap(placed, bits[-1]), proj_weight.T, grad_packed.T),
        scalars=1,
        flops=4 * seq * channels * width,
    )
    proj_parts = call(
        fold_kernel,
        [shape(per_dp * width // channels, channels, kind=F32)]
        + [shape(per_dp * width // channels, channels)] * (far - 1),
        (me, keep, swap(send, mp_count)),
        scalars=1,
    )

    grad_features = call(
        functools.partial(input_kernel, pairs=pairs, frames=frames),
        shape(utt_count * positions, channels),
        (me, grads, conv_weight),
        scalars=1,
        flops=2 * n1 * 2 * channels * channels,
    ).reshape(utt_count, positions, channels)

    conv_parts = call(
        functools.partial(kernel_grad_kernel, n1=n1, n2=n2, owned=owned, near=near, far=far),
        [shape(2 * owned + 8, channels, kind=F32)] + [shape(2 * owned + 8, channels)] * (far - 1),
        (me,) + tuple(by_mask[k] for k in range(near)) + tuple(in_sides),
        scalars=1,
        flops=2 * (n1 + n2) * 2 * channels * channels,
        scratch=[pltpu.VMEM((far, 2 * owned + 8, channels), F32)],
    )
    conv_got = [swap(part, near * f) if f else part for f, part in enumerate(conv_parts)]
    proj_got = [swap(part, near * f) if f else part for f, part in enumerate(proj_parts)]
    grad_conv, grad_norm, grad_proj = call(
        functools.partial(last_kernel, owned=owned, far=far),
        [
            shape(2, owned, channels, kind=F32),
            shape(2, owned, kind=F32),
            shape(per_dp, width, kind=F32),
        ],
        (me, *conv_got, *proj_got),
        scalars=1,
    )
    return (packed.T, grad_features, grad_conv, grad_norm, grad_proj)


def solution(mesh):
    return jax.shard_map(
        local,
        mesh=mesh,
        in_specs=(
            P(("dp", "mp"), None, None),
            P(("dp", "mp")),
            P(("dp", "mp")),
            P(("dp", "mp")),
            P(),
            P(),
            P(),
            P(None, "mp"),
            P("dp", "mp"),
        ),
        out_specs=(
            P("dp", "mp"),
            P(("dp", "mp"), None, None),
            P(None, ("dp", "mp"), None),
            P(None, ("dp", "mp")),
            P("dp", "mp"),
        ),
        check_vma=False,
    )
```

```python
import functools
import math

import jax
import jax.numpy as jnp
from jax import lax
from jax.experimental import pallas as pl
from jax.experimental.pallas import tpu as pltpu
from jax.sharding import PartitionSpec as P

epsilon = 1e-05
BF = jnp.bfloat16
F32 = jnp.float32
VMEM = pltpu.VMEM
SMEM = pltpu.SMEM


def call(body, out, args, scalars=0, fetched=0, flops=0, scratch=(), mebibytes=14, to_scalars=0):
    specs = [
        pl.BlockSpec(memory_space=SMEM if i < scalars else pl.ANY if i < scalars + fetched else VMEM)
        for i in range(len(args))
    ]
    many = isinstance(out, (list, tuple))
    moved = sum(a.size * a.dtype.itemsize for a in args)
    return pl.pallas_call(
        body,
        out_shape=out,
        in_specs=specs,
        out_specs=[
            pl.BlockSpec(memory_space=SMEM if i < to_scalars else VMEM) for i in range(len(out))
        ]
        if many
        else pl.BlockSpec(memory_space=VMEM),
        scratch_shapes=list(scratch),
        compiler_params=pltpu.CompilerParams(vmem_limit_bytes=mebibytes * 2**20),
        cost_estimate=pl.CostEstimate(flops=flops, bytes_accessed=moved, transcendentals=0),
    )(*args)


def shape(*dims, kind=BF):
    return jax.ShapeDtypeStruct(dims, kind)


def dot(a, b):
    return jnp.dot(a, b, preferred_element_type=F32)


def dot_nt(a, b):
    return lax.dot_general(a, b, (((1,), (1,)), ((), ())), preferred_element_type=F32)


def norm_parts(pre):
    average = jnp.mean(pre, axis=-1, keepdims=True)
    centred = pre - average
    spread = jnp.mean(centred * centred, axis=-1, keepdims=True)
    scale = lax.rsqrt(spread + epsilon)
    return centred * scale, scale


def gelu_parts(value):
    half = 0.5 * (1.0 + lax.erf(value * math.sqrt(0.5)))
    density = jnp.exp(-0.5 * value * value) * (1.0 / math.sqrt(2.0 * math.pi))
    return value * half, half + value * density


def source_of(row, me_ref, pairs, frames):
    part = lax.div(row, pairs * frames)
    inner = lax.rem(row, pairs * frames)
    pair = lax.div(inner, frames)
    t = lax.rem(inner, frames)
    first = jnp.zeros_like(row)
    for p in range(pairs):
        first = jnp.where(pair == p, me_ref[4 + 2 * p], first)
    off = jnp.where(part == 1, 2, jnp.where(part == 2, 1, part))
    t_from = jnp.where(t < first, t, t + frames - first)
    return pair * (8 * frames) + 4 * t_from + off


def start_kernel(
    place_ref, proj_hbm, cotangent_hbm, lengths_hbm, dests_hbm, offsets_hbm, me_ref, index_ref, rows_ref,
    proj_ref, cotangent_ref, lengths_ref, dests_ref, offsets_ref, copied, *, pairs, frames
):
    sources = (proj_hbm, cotangent_hbm, lengths_hbm, dests_hbm, offsets_hbm)
    targets = (proj_ref, cotangent_ref, lengths_ref, dests_ref, offsets_ref)
    copies = [
        pltpu.make_async_copy(source, target, copied.at[i])
        for i, (source, target) in enumerate(zip(sources, targets))
    ]
    for copy in copies[::-1]:
        copy.start()
    for copy in copies[2:]:
        copy.wait()
    for i in range(4):
        me_ref[i] = place_ref[i]
    for i in range(2 * pairs):
        me_ref[4 + i] = lengths_ref[i]
        me_ref[4 + 2 * pairs + i] = dests_ref[i]
        me_ref[4 + 4 * pairs + i] = offsets_ref[i]
    shard = lax.broadcasted_iota(jnp.int32, index_ref.shape, 0)
    value = jnp.zeros(index_ref.shape, jnp.int32)
    for p in range(pairs):
        block = lax.div(offsets_ref[2 * p], frames)
        value = jnp.where(shard == dests_ref[2 * p], block + 1, value)
    index_ref[...] = value
    copies[0].wait()
    copies[1].wait()
    rows_ref[...] = lax.dot_general(
        cotangent_ref[...], proj_ref[...], (((0,), (0,)), ((), ())), preferred_element_type=F32
    ).astype(BF)


def state_views(state_ref):
    part = (state_ref.shape[0] - 8) // 10
    spans = ((0, 2), (2, 1), (3, 2), (5, 1), (6, 2), (8, 1), (9, 1))
    return [state_ref.at[a * part : (a + n) * part] for a, n in spans] + [state_ref.at[10 * part :]]


def forward_kernel(me_ref, *refs, pairs, frames, far, near, owned):
    weight_ref = refs[3]
    sources = refs[:3] + (weight_ref.at[0], weight_ref.at[1])
    rest, held, in_turned, copied = refs[4:-7], refs[-7:-2], refs[-2], refs[-1]
    copies = [
        pltpu.make_async_copy(source, target, copied.at[i])
        for i, (source, target) in enumerate(zip(sources, held))
    ]
    for copy in copies:
        copy.start()
    feat_ref, gain_ref, shift_ref, first_ref, second_ref = held
    later_ref, frames_ref, state_ref = rest[:3]
    turned_refs = rest[3:]
    for i in range(me_ref.shape[0]):
        later_ref[i] = me_ref[i]
    slope1_ref, slope2_ref, hat1_ref, hat2_ref, scale1_ref, scale2_ref, pick_ref, gain_at = state_views(state_ref)
    copies[0].wait()
    channels = feat_ref.shape[1]
    n2 = pairs * frames
    row = lax.broadcasted_iota(jnp.int32, (4 * n2, 1), 0)
    source = source_of(row, me_ref, pairs, frames)
    place = lax.broadcasted_iota(jnp.int32, (4 * n2, feat_ref.shape[0]), 1)
    pick = jnp.where(place == source, 1.0, 0.0).astype(BF)
    chosen32 = dot(pick, feat_ref[...])
    chosen = chosen32.astype(BF)
    for copy in copies[1:4]:
        copy.wait()
    even, odd = chosen[: 2 * n2], chosen[2 * n2 :]
    first = dot(even, first_ref[:channels, :]) + dot(odd, first_ref[channels:, :])
    hat, scale = norm_parts(first)
    hidden, slope = gelu_parts(hat * gain_ref[0:1, :] + shift_ref[0:1, :])
    slope1_ref[...] = slope
    hat1_ref[...] = hat
    scale1_ref[...] = jnp.broadcast_to(scale, scale1_ref.shape)
    hidden = hidden.astype(BF)
    hidden32 = hidden.astype(F32)
    copies[4].wait()
    second = dot(hidden[:n2], second_ref[:channels, :]) + dot(hidden[n2:], second_ref[channels:, :])
    hat, scale = norm_parts(second)
    made, slope = gelu_parts(hat * gain_ref[1:2, :] + shift_ref[1:2, :])
    slope2_ref[...] = slope
    hat2_ref[...] = hat
    scale2_ref[...] = jnp.broadcast_to(scale, scale2_ref.shape)
    none = jnp.zeros((frames, channels), F32)
    sent = []
    for d in range(frames_ref.shape[0] // frames):
        rows = none
        for p in range(pairs):
            rows = jnp.where(me_ref[4 + 2 * pairs + 2 * p] == d, made[p * frames : (p + 1) * frames], rows)
        sent.append(rows)
    frames_ref[...] = jnp.concatenate(sent, axis=0).astype(BF)
    row = lax.broadcasted_iota(jnp.int32, (n2, 1), 0)
    slot = jnp.zeros_like(row)
    for p in range(pairs):
        slot = jnp.where(lax.div(row, frames) == p, me_ref[4 + 2 * pairs + 2 * p], slot)
    slot = slot * (2 * frames) + lax.rem(row, frames)
    place = lax.broadcasted_iota(jnp.int32, (n2, channels), 1)
    pick_ref[...] = jnp.where(place == slot, 1.0, 0.0)
    gain_at[...] = jnp.concatenate([gain_ref[...], jnp.zeros((6, channels), F32)], axis=0)
    wide = in_turned.shape[1]
    fill = [jnp.zeros((wide - 3 * n2, channels), F32)] if wide > 3 * n2 else []
    for tap in range(2):
        stacked = jnp.concatenate(
            [chosen32[2 * n2 * tap : 2 * n2 * (tap + 1)], hidden32[n2 * tap : n2 * (tap + 1)]] + fill,
            axis=0,
        )
        in_turned[channels * tap : channels * (tap + 1), :] = stacked.T
    at = me_ref[1]
    for k, turned_ref in enumerate(turned_refs):
        turned_ref[...] = jnp.concatenate(
            [
                in_turned[pl.ds(pl.multiple_of((z * near + (at ^ (2 * k + c))) * owned, owned), owned), :]
                for c in range(2)
                for z in range(far)
            ],
            axis=0,
        ).astype(BF)


def send_kernel(got_ref, mine_ref, other_ref, sent_ref, out_ref, rows32, *, frames):
    rows32[...] = mine_ref[...].astype(F32) + other_ref[...].astype(F32)
    blocks = rows32.shape[0] // frames
    sent = sent_ref[...].astype(F32)
    none = jnp.zeros((frames, sent.shape[1]), F32)
    for d in range(out_ref.shape[0]):
        block = got_ref[d, 0] - 1
        safe = jnp.clip(block, 0, blocks - 1)
        grads = rows32[pl.ds(pl.multiple_of(safe * frames, frames), frames), :]
        grads = jnp.where(block >= 0, grads, none)
        out_ref[d] = jnp.concatenate([grads, sent[d * frames : (d + 1) * frames]], axis=0).astype(BF)


def pack(rows, channels):
    r, w = rows.shape
    parts, start = [], 0
    while start < w:
        lanes = min(1 << ((w - start).bit_length() - 1), channels)
        each = r * lanes // channels
        parts.append(
            jnp.concatenate(
                [rows[g * each : (g + 1) * each, start : start + lanes] for g in range(r // each)], axis=1
            )
        )
        start += lanes
    return jnp.concatenate(parts, axis=0)


def unpack(packed, r, w):
    channels = packed.shape[1]
    parts, start, at = [], 0, 0
    while start < w:
        lanes = min(1 << ((w - start).bit_length() - 1), channels)
        each = r * lanes // channels
        block = packed[at : at + each]
        parts.append(
            jnp.concatenate([block[:, g * lanes : (g + 1) * lanes] for g in range(r // each)], axis=0)
        )
        start += lanes
        at += each
    return jnp.concatenate(parts, axis=1)


def project_kernel(me_ref, *refs, start, near, frames):
    side_refs = refs[:near]
    weight_ref, mine_ref, other_ref, packed_ref, own_ref = refs[near : near + 5]
    out_refs, held = refs[near + 5 : -1], refs[-1]
    channels, seq = weight_ref.shape[1], packed_ref.shape[1]
    dp_count = (side_refs[0].shape[0] - start - 8) // (1 + frames)
    row = lax.broadcasted_iota(jnp.int32, (dp_count * frames, seq), 0)
    lane = lax.broadcasted_iota(jnp.int32, (dp_count * frames, seq), 1)
    block = (lax.div(lane, frames) + 1).astype(F32)
    same = lax.rem(lane, frames) == lax.rem(row, frames)
    shards = [0.0, 0.0]
    for k in range(near):
        tail = side_refs[k][start:, :].astype(F32)
        ids = tail[8 : 8 + dp_count, :seq]
        ids = jnp.broadcast_to(ids[:, None, :], (dp_count, frames, seq)).reshape(dp_count * frames, seq)
        pick = jnp.where(jnp.logical_and(same, ids == block), 1.0, 0.0).astype(BF)
        shards[2 * k // near] += lax.dot_general(
            pick, tail[8 + dp_count :].astype(BF), (((0,), (0,)), ((), ())), preferred_element_type=F32
        )
    packed_ref[...] = dot_nt(weight_ref[...], shards[0].astype(BF)).astype(BF)
    partial = dot_nt(shards[0].T.astype(BF), mine_ref[...]) + dot_nt(shards[1].T.astype(BF), other_ref[...])
    each = channels // dp_count
    for z in range(held.shape[0]):
        low = partial[2 * z * each : (2 * z + 1) * each]
        high = partial[(2 * z + 1) * each : (2 * z + 2) * each]
        held[z] = pack(jnp.where(me_ref[3] == 0, low, high), channels)
    own_ref[...] = held[me_ref[2]]
    for f in range(1, held.shape[0]):
        out_refs[f - 1][...] = held[me_ref[2] ^ f].astype(BF)


def norm_back(grad, slope_ref, hat_ref, scale_ref, gain):
    pre = grad * slope_ref[...]
    hat = hat_ref[...]
    by_hat = pre * hat
    inner = pre * gain
    average = jnp.mean(inner, axis=-1, keepdims=True)
    along = jnp.mean(inner * hat, axis=-1, keepdims=True)
    back = (inner - average - hat * along) * scale_ref[:, 0:1]
    return (
        back.astype(BF),
        jnp.sum(by_hat, axis=0, keepdims=True),
        jnp.sum(pre, axis=0, keepdims=True),
    )


def back_kernel(slots_ref, got_ref, state_ref, weight_ref, out_ref, *, frames):
    channels = weight_ref.shape[2]
    slope1_ref, slope2_ref, hat1_ref, hat2_ref, scale1_ref, scale2_ref, pick_ref, gain_ref = state_views(state_ref)
    slots = slots_ref[...]
    grads = dot(pick_ref[:, : slots.shape[0]].astype(BF), slots)
    second, gain2, shift2 = norm_back(grads, slope2_ref, hat2_ref, scale2_ref, gain_ref[1:2, :])
    hidden = jnp.concatenate(
        [
            dot_nt(second, weight_ref[1, :channels, :]),
            dot_nt(second, weight_ref[1, channels:, :]),
        ],
        axis=0,
    )
    hidden = hidden.astype(BF).astype(F32)
    first, gain1, shift1 = norm_back(hidden, slope1_ref, hat1_ref, scale1_ref, gain_ref[0:1, :])
    sums = jnp.concatenate([gain1, shift1, gain2, shift2], axis=0)
    high = sums.astype(BF).astype(F32)
    ids = got_ref[...].astype(F32)
    slots32 = slots.astype(F32)
    rows = [high, sums - high, jnp.concatenate([ids] * (channels // ids.shape[1]), axis=1)]
    rows += [
        slots32[(2 * d + 1) * frames : (2 * d + 2) * frames] for d in range(slots.shape[0] // (2 * frames))
    ]
    n1, n2 = first.shape[0], second.shape[0]
    out_ref[:n1, :] = first
    out_ref[n1 : n1 + n2, :] = second
    out_ref[n1 + n2 :, :] = jnp.concatenate(rows, axis=0).astype(BF)


def input_kernel(me_ref, grad_ref, weight_ref, out_ref, *, pairs, frames):
    channels = weight_ref.shape[2]
    n1 = 2 * pairs * frames
    first = grad_ref[:n1, :]
    rows = jnp.concatenate(
        [dot_nt(first, weight_ref[0, :channels, :]), dot_nt(first, weight_ref[0, channels:, :])],
        axis=0,
    ).astype(BF)
    row = lax.broadcasted_iota(jnp.int32, (1, 2 * n1), 1)
    source = source_of(row, me_ref, pairs, frames)
    place = lax.broadcasted_iota(jnp.int32, (out_ref.shape[0], 2 * n1), 0)
    pick = jnp.where(place == source, 1.0, 0.0).astype(BF)
    out_ref[...] = dot(pick, rows).astype(BF)


def kernel_grad_kernel(me_ref, *refs, n1, n2, owned, near, far):
    grad_refs, side_refs = refs[:near], refs[near : 2 * near]
    rows = side_refs[0].shape[0] // 2
    in_refs = [
        side_refs[near // 2 * (k % 2) + k // 2].at[k % 2 * rows : (k % 2 + 1) * rows] for k in range(near)
    ]
    own_ref, out_refs, held = refs[2 * near], refs[2 * near + 1 : -1], refs[-1]
    first, second, sums = 0.0, 0.0, 0.0
    for grad_ref, in_ref in zip(grad_refs, in_refs):
        side = in_ref[...]
        first += dot(side[:, :n1], grad_ref[:n1, :])
        second += dot(side[:, n1 : n1 + n2], grad_ref[n1 : n1 + n2, :])
        tail = grad_ref[n1 + n2 : n1 + n2 + 16, :].astype(F32)
        sums += tail[0:4] + tail[4:8]
    high = sums.astype(BF).astype(F32)
    for z in range(far):
        held[z] = jnp.concatenate(
            [first[z * owned : (z + 1) * owned], second[z * owned : (z + 1) * owned], high, sums - high],
            axis=0,
        )
    own_ref[...] = held[me_ref[2]]
    for f in range(1, far):
        out_refs[f - 1][...] = held[me_ref[2] ^ f].astype(BF)


def last_kernel(me_ref, *refs, owned, far):
    conv_in, proj_in = refs[:far], refs[far : 2 * far]
    conv_ref, norm_ref, proj_ref = refs[2 * far :]
    total = conv_in[0][...]
    proj = proj_in[0][...]
    for f in range(1, far):
        total += conv_in[f][...].astype(F32)
        proj += proj_in[f][...].astype(F32)
    conv_ref[0] = total[:owned]
    conv_ref[1] = total[owned : 2 * owned]
    proj_ref[...] = unpack(proj, *proj_ref.shape)
    channels = total.shape[1]
    sums = total[2 * owned : 2 * owned + 4] + total[2 * owned + 4 : 2 * owned + 8]
    start = me_ref[0] * owned
    later = start >= channels
    lines = jnp.concatenate(
        [jnp.where(later, sums[2 * k + 1 : 2 * k + 2], sums[2 * k : 2 * k + 1]) for k in range(2)]
        + [jnp.zeros((6, channels), F32)],
        axis=0,
    )
    start = jnp.where(later, start - channels, start)
    lines = pltpu.roll(lines, lax.rem(channels - start, channels), 1)
    norm_ref[...] = lines[:2, :owned]


def local(
    features, lengths, dests, offsets, conv_weight, norm_gain, norm_shift, proj_weight, grad_packed
):
    utt_count, positions, channels = features.shape
    frames = positions // 4
    pairs = utt_count // 2
    dp_count = lax.axis_size("dp")
    mp_count = lax.axis_size("mp")
    seq = grad_packed.shape[0]
    width = grad_packed.shape[1]
    owned = 2 * channels // (dp_count * mp_count)
    n1, n2 = 2 * pairs * frames, pairs * frames
    near, far = 2 * mp_count, dp_count // 2
    everyone = ("dp", "mp")

    def swap(x, mask):
        return lax.ppermute(x, everyone, [(i, i ^ mask) for i in range(dp_count * mp_count)])

    bits = [1 << b for b in range(mp_count.bit_length() - 1)][::-1]
    at_dp = lax.axis_index("dp").astype(jnp.int32)
    at_mp = lax.axis_index("mp").astype(jnp.int32)
    x_bit = at_dp & 1
    place = jnp.stack([at_dp * mp_count + at_mp, x_bit * mp_count + at_mp, at_dp >> 1, x_bit])
    me, index, grad_rows = call(
        functools.partial(start_kernel, pairs=pairs, frames=frames),
        [
            shape(4 + 6 * pairs, kind=jnp.int32),
            shape(dp_count, 128, kind=jnp.int32),
            shape(seq, channels),
        ],
        (place, proj_weight.T, grad_packed.T, lengths, dests, offsets),
        scalars=1,
        fetched=5,
        to_scalars=1,
        flops=2 * seq * width * channels,
        scratch=[
            pltpu.VMEM((width, channels), BF),
            pltpu.VMEM((width, seq), BF),
            pltpu.SMEM(lengths.shape, jnp.int32),
            pltpu.SMEM(dests.shape, jnp.int32),
            pltpu.SMEM(offsets.shape, jnp.int32),
            pltpu.SemaphoreType.DMA((5,)),
        ],
        mebibytes=56,
    )
    feat = features.reshape(utt_count * positions, channels)
    got_index = lax.all_to_all(index, "dp", split_axis=0, concat_axis=0, tiled=True)

    wide = -(-(n1 + n2) // 128) * 128
    tall = (2 * channels, channels)
    made = call(
        functools.partial(
            forward_kernel, pairs=pairs, frames=frames, far=far, near=near, owned=owned
        ),
        [
            shape(*me.shape, kind=jnp.int32),
            shape(dp_count * frames, channels),
            shape(10 * n2 + 8, channels, kind=F32),
        ]
        + [shape(2 * far * owned, wide)] * (near // 2),
        (me, feat, norm_gain, norm_shift, conv_weight),
        scalars=1,
        fetched=4,
        to_scalars=1,
        flops=10**10,
        scratch=[
            pltpu.VMEM(feat.shape, BF),
            pltpu.VMEM(norm_gain.shape, F32),
            pltpu.VMEM(norm_shift.shape, F32),
            pltpu.VMEM(tall, BF),
            pltpu.VMEM(tall, BF),
            pltpu.VMEM((2 * channels, wide), F32),
            pltpu.SemaphoreType.DMA((5,)),
        ],
        mebibytes=56,
    )
    me, pair_frames, state = made[:3]
    in_sides = [swap(side, 2 * k) if k else side for k, side in enumerate(made[3:])]

    for mask in bits[:-1]:
        arrived, pair_frames, got_index = lax.optimization_barrier(
            (swap(grad_rows, mask), pair_frames, got_index)
        )
        grad_rows = (grad_rows.astype(F32) + arrived.astype(F32)).astype(BF)
    other_rows = swap(grad_rows, bits[-1])

    sent = call(
        functools.partial(send_kernel, frames=frames),
        shape(dp_count, 2 * frames, channels),
        (got_index, grad_rows, other_rows, pair_frames),
        scalars=1,
        scratch=[pltpu.VMEM((seq, channels), F32)],
    )
    slots = lax.all_to_all(sent, "dp", split_axis=0, concat_axis=0, tiled=True)
    cotangent = grad_packed.T
    other_cotangent = swap(cotangent, mp_count)
    slots, other_cotangent, *in_sides[: near // 2] = lax.optimization_barrier(
        (slots, other_cotangent, *in_sides[: near // 2])
    )

    in_sides += [swap(side, 1) for side in in_sides]
    rows_sent = n1 + n2 + 8 + dp_count * (1 + frames)
    grads = call(
        functools.partial(back_kernel, frames=frames),
        shape(rows_sent, channels),
        (slots.reshape(-1, channels), got_index, state, conv_weight),
        flops=2 * n2 * 2 * channels * channels,
    )
    by_mask = {mask: swap(grads, mask) if mask else grads for mask in range(0, near, 2)}
    for mask in range(0, near, 2):
        by_mask[mask + 1] = swap(by_mask[mask], 1)

    per_dp = channels // dp_count
    packed_rows = per_dp * width // channels
    sides = tuple(by_mask[k] for k in range(near))
    packed, *proj_parts = call(
        functools.partial(project_kernel, start=n1 + n2, near=near, frames=frames),
        [shape(width, seq), shape(packed_rows, channels, kind=F32)]
        + [shape(packed_rows, channels)] * (far - 1),
        (me, *sides, proj_weight.T, cotangent, other_cotangent),
        scalars=1,
        flops=6 * seq * channels * width,
        scratch=[pltpu.VMEM((far, packed_rows, channels), F32)],
    )

    grad_features = call(
        functools.partial(input_kernel, pairs=pairs, frames=frames),
        shape(utt_count * positions, channels),
        (me, grads, conv_weight),
        scalars=1,
        flops=2 * n1 * 2 * channels * channels,
    ).reshape(utt_count, positions, channels)

    conv_parts = call(
        functools.partial(kernel_grad_kernel, n1=n1, n2=n2, owned=owned, near=near, far=far),
        [shape(2 * owned + 8, channels, kind=F32)] + [shape(2 * owned + 8, channels)] * (far - 1),
        (me, *sides, *in_sides),
        scalars=1,
        flops=2 * (n1 + n2) * 2 * channels * channels,
        scratch=[pltpu.VMEM((far, 2 * owned + 8, channels), F32)],
    )
    conv_got = [swap(part, near * f) if f else part for f, part in enumerate(conv_parts)]
    proj_got = [swap(part, near * f) if f else part for f, part in enumerate(proj_parts)]
    grad_conv, grad_norm, grad_proj = call(
        functools.partial(last_kernel, owned=owned, far=far),
        [
            shape(2, owned, channels, kind=F32),
            shape(2, owned, kind=F32),
            shape(per_dp, width, kind=F32),
        ],
        (me, *conv_got, *proj_got),
        scalars=1,
    )
    return (packed.T, grad_features, grad_conv, grad_norm, grad_proj)


def solution(mesh):
    return jax.shard_map(
        local,
        mesh=mesh,
        in_specs=(
            P(("dp", "mp"), None, None),
            P(("dp", "mp")),
            P(("dp", "mp")),
            P(("dp", "mp")),
            P(),
            P(),
            P(),
            P(None, "mp"),
            P("dp", "mp"),
        ),
        out_specs=(
            P("dp", "mp"),
            P(("dp", "mp"), None, None),
            P(None, ("dp", "mp"), None),
            P(None, ("dp", "mp")),
            P("dp", "mp"),
        ),
        check_vma=False,
    )
```

```python
import functools
import math

import jax
import jax.numpy as jnp
from jax import lax
from jax.experimental import pallas as pl
from jax.experimental.pallas import tpu as pltpu
from jax.sharding import PartitionSpec as P

epsilon = 1e-05
BF = jnp.bfloat16
F32 = jnp.float32
VMEM = pltpu.VMEM
SMEM = pltpu.SMEM


def call(body, out, args, scalars=0, fetched=0, flops=0, scratch=(), mebibytes=14, to_scalars=0):
    specs = [
        pl.BlockSpec(memory_space=SMEM if i < scalars else pl.ANY if i < scalars + fetched else VMEM)
        for i in range(len(args))
    ]
    many = isinstance(out, (list, tuple))
    moved = sum(a.size * a.dtype.itemsize for a in args)
    return pl.pallas_call(
        body,
        out_shape=out,
        in_specs=specs,
        out_specs=[
            pl.BlockSpec(memory_space=SMEM if i < to_scalars else VMEM) for i in range(len(out))
        ]
        if many
        else pl.BlockSpec(memory_space=VMEM),
        scratch_shapes=list(scratch),
        compiler_params=pltpu.CompilerParams(vmem_limit_bytes=mebibytes * 2**20),
        cost_estimate=pl.CostEstimate(flops=flops, bytes_accessed=moved, transcendentals=0),
    )(*args)


def shape(*dims, kind=BF):
    return jax.ShapeDtypeStruct(dims, kind)


def dot(a, b):
    return jnp.dot(a, b, preferred_element_type=F32)


def dot_nt(a, b):
    return lax.dot_general(a, b, (((1,), (1,)), ((), ())), preferred_element_type=F32)


def norm_parts(pre):
    average = jnp.mean(pre, axis=-1, keepdims=True)
    centred = pre - average
    spread = jnp.mean(centred * centred, axis=-1, keepdims=True)
    scale = lax.rsqrt(spread + epsilon)
    return centred * scale, scale


def gelu_parts(value):
    half = 0.5 * (1.0 + lax.erf(value * math.sqrt(0.5)))
    density = jnp.exp(-0.5 * value * value) * (1.0 / math.sqrt(2.0 * math.pi))
    return value * half, half + value * density


def source_of(row, me_ref, pairs, frames):
    part = lax.div(row, pairs * frames)
    inner = lax.rem(row, pairs * frames)
    pair = lax.div(inner, frames)
    t = lax.rem(inner, frames)
    first = jnp.zeros_like(row)
    for p in range(pairs):
        first = jnp.where(pair == p, me_ref[4 + 2 * p], first)
    off = jnp.where(part == 1, 2, jnp.where(part == 2, 1, part))
    t_from = jnp.where(t < first, t, t + frames - first)
    return pair * (8 * frames) + 4 * t_from + off


def start_kernel(
    proj_hbm, cotangent_hbm, lengths_hbm, dests_hbm, offsets_hbm, me_ref, index_ref, rows_ref,
    proj_ref, cotangent_ref, lengths_ref, dests_ref, offsets_ref, copied, *, pairs, frames, mp_count
):
    sources = (proj_hbm, cotangent_hbm, lengths_hbm, dests_hbm, offsets_hbm)
    targets = (proj_ref, cotangent_ref, lengths_ref, dests_ref, offsets_ref)
    copies = [
        pltpu.make_async_copy(source, target, copied.at[i])
        for i, (source, target) in enumerate(zip(sources, targets))
    ]
    for copy in copies[::-1]:
        copy.start()
    for copy in copies[2:]:
        copy.wait()
    at_dp, at_mp = lax.axis_index("dp"), lax.axis_index("mp")
    me_ref[0] = at_dp * mp_count + at_mp
    me_ref[1] = lax.rem(at_dp, 2) * mp_count + at_mp
    me_ref[2] = lax.div(at_dp, 2)
    me_ref[3] = lax.rem(at_dp, 2)
    for i in range(2 * pairs):
        me_ref[4 + i] = lengths_ref[i]
        me_ref[4 + 2 * pairs + i] = dests_ref[i]
        me_ref[4 + 4 * pairs + i] = offsets_ref[i]
    shard = lax.broadcasted_iota(jnp.int32, index_ref.shape, 0)
    value = jnp.zeros(index_ref.shape, jnp.int32)
    for p in range(pairs):
        block = lax.div(offsets_ref[2 * p], frames)
        value = jnp.where(shard == dests_ref[2 * p], block + 1, value)
    index_ref[...] = value
    copies[0].wait()
    copies[1].wait()
    rows_ref[...] = lax.dot_general(
        cotangent_ref[...], proj_ref[...], (((0,), (0,)), ((), ())), preferred_element_type=F32
    ).astype(BF)


def state_views(state_ref):
    part = (state_ref.shape[0] - 8) // 10
    spans = ((0, 2), (2, 1), (3, 2), (5, 1), (6, 2), (8, 1), (9, 1))
    return [state_ref.at[a * part : (a + n) * part] for a, n in spans] + [state_ref.at[10 * part :]]


def forward_kernel(me_ref, *refs, pairs, frames, far, near, owned):
    weight_ref, cotangent_hbm = refs[3:5]
    rest, held, in_turned, copied = refs[5:-7], refs[-7:-2], refs[-2], refs[-1]
    with_cotangent = rest[3 + near // 4]
    own_rows = 2 * far * owned
    tail = with_cotangent.at[own_rows:, : cotangent_hbm.shape[1]]
    sources = refs[:3] + (weight_ref.at[0], weight_ref.at[1], cotangent_hbm)
    targets = held + (tail,)
    copies = [
        pltpu.make_async_copy(source, target, copied.at[i])
        for i, (source, target) in enumerate(zip(sources, targets))
    ]
    for copy in copies:
        copy.start()
    feat_ref, gain_ref, shift_ref, first_ref, second_ref = held
    later_ref, frames_ref, state_ref = rest[:3]
    turned_refs = rest[3:]
    for i in range(me_ref.shape[0]):
        later_ref[i] = me_ref[i]
    slope1_ref, slope2_ref, hat1_ref, hat2_ref, scale1_ref, scale2_ref, pick_ref, gain_at = state_views(state_ref)
    copies[0].wait()
    channels = feat_ref.shape[1]
    n2 = pairs * frames
    row = lax.broadcasted_iota(jnp.int32, (4 * n2, 1), 0)
    source = source_of(row, me_ref, pairs, frames)
    place = lax.broadcasted_iota(jnp.int32, (4 * n2, feat_ref.shape[0]), 1)
    pick = jnp.where(place == source, 1.0, 0.0).astype(BF)
    chosen32 = dot(pick, feat_ref[...])
    chosen = chosen32.astype(BF)
    for copy in copies[1:4]:
        copy.wait()
    even, odd = chosen[: 2 * n2], chosen[2 * n2 :]
    first = dot(even, first_ref[:channels, :]) + dot(odd, first_ref[channels:, :])
    hat, scale = norm_parts(first)
    hidden, slope = gelu_parts(hat * gain_ref[0:1, :] + shift_ref[0:1, :])
    slope1_ref[...] = slope
    hat1_ref[...] = hat
    scale1_ref[...] = jnp.broadcast_to(scale, scale1_ref.shape)
    hidden = hidden.astype(BF)
    hidden32 = hidden.astype(F32)
    copies[4].wait()
    second = dot(hidden[:n2], second_ref[:channels, :]) + dot(hidden[n2:], second_ref[channels:, :])
    hat, scale = norm_parts(second)
    made, slope = gelu_parts(hat * gain_ref[1:2, :] + shift_ref[1:2, :])
    slope2_ref[...] = slope
    hat2_ref[...] = hat
    scale2_ref[...] = jnp.broadcast_to(scale, scale2_ref.shape)
    none = jnp.zeros((frames, channels), F32)
    sent = []
    for d in range(frames_ref.shape[0] // frames):
        rows = none
        for p in range(pairs):
            rows = jnp.where(me_ref[4 + 2 * pairs + 2 * p] == d, made[p * frames : (p + 1) * frames], rows)
        sent.append(rows)
    frames_ref[...] = jnp.concatenate(sent, axis=0).astype(BF)
    row = lax.broadcasted_iota(jnp.int32, (n2, 1), 0)
    slot = jnp.zeros_like(row)
    for p in range(pairs):
        slot = jnp.where(lax.div(row, frames) == p, me_ref[4 + 2 * pairs + 2 * p], slot)
    slot = slot * (2 * frames) + lax.rem(row, frames)
    place = lax.broadcasted_iota(jnp.int32, (n2, channels), 1)
    pick_ref[...] = jnp.where(place == slot, 1.0, 0.0)
    gain_at[...] = jnp.concatenate([gain_ref[...], jnp.zeros((6, channels), F32)], axis=0)
    wide = in_turned.shape[1]
    fill = [jnp.zeros((wide - 3 * n2, channels), F32)] if wide > 3 * n2 else []
    for tap in range(2):
        stacked = jnp.concatenate(
            [chosen32[2 * n2 * tap : 2 * n2 * (tap + 1)], hidden32[n2 * tap : n2 * (tap + 1)]] + fill,
            axis=0,
        )
        in_turned[channels * tap : channels * (tap + 1), :] = stacked.T
    at = me_ref[1]
    for k, turned_ref in enumerate(turned_refs):
        turned_ref[:own_rows, :] = jnp.concatenate(
            [
                in_turned[pl.ds(pl.multiple_of((z * near + (at ^ (2 * k + c))) * owned, owned), owned), :]
                for c in range(2)
                for z in range(far)
            ],
            axis=0,
        ).astype(BF)
    copies[5].wait()


def send_kernel(got_ref, mine_ref, other_ref, sent_ref, out_ref, rows32, *, frames):
    rows32[...] = mine_ref[...].astype(F32) + other_ref[...].astype(F32)
    blocks = rows32.shape[0] // frames
    sent = sent_ref[...].astype(F32)
    none = jnp.zeros((frames, sent.shape[1]), F32)
    for d in range(out_ref.shape[0]):
        block = got_ref[d, 0] - 1
        safe = jnp.clip(block, 0, blocks - 1)
        grads = rows32[pl.ds(pl.multiple_of(safe * frames, frames), frames), :]
        grads = jnp.where(block >= 0, grads, none)
        out_ref[d] = jnp.concatenate([grads, sent[d * frames : (d + 1) * frames]], axis=0).astype(BF)


def pack(rows, channels):
    r, w = rows.shape
    parts, start = [], 0
    while start < w:
        lanes = min(1 << ((w - start).bit_length() - 1), channels)
        each = r * lanes // channels
        parts.append(
            jnp.concatenate(
                [rows[g * each : (g + 1) * each, start : start + lanes] for g in range(r // each)], axis=1
            )
        )
        start += lanes
    return jnp.concatenate(parts, axis=0)


def unpack(packed, r, w):
    channels = packed.shape[1]
    parts, start, at = [], 0, 0
    while start < w:
        lanes = min(1 << ((w - start).bit_length() - 1), channels)
        each = r * lanes // channels
        block = packed[at : at + each]
        parts.append(
            jnp.concatenate([block[:, g * lanes : (g + 1) * lanes] for g in range(r // each)], axis=0)
        )
        start += lanes
        at += each
    return jnp.concatenate(parts, axis=1)


def gradient_kernel(me_ref, *refs, n1, n2, owned, near, far, frames):
    side_refs, column_refs = refs[:near], refs[near : 2 * near]
    weight_ref, mine_ref, packed_ref, own_ref = refs[2 * near : 2 * near + 4]
    out_refs, held = refs[2 * near + 4 : -1], refs[-1]
    start = n1 + n2
    rows = far * owned
    other = column_refs[near // 4][2 * rows :][:, : mine_ref.shape[1]]
    channels, seq = weight_ref.shape[1], packed_ref.shape[1]
    dp_count = (side_refs[0].shape[0] - start - 8) // (1 + frames)
    row = lax.broadcasted_iota(jnp.int32, (dp_count * frames, seq), 0)
    lane = lax.broadcasted_iota(jnp.int32, (dp_count * frames, seq), 1)
    block = (lax.div(lane, frames) + 1).astype(F32)
    same = lax.rem(lane, frames) == lax.rem(row, frames)
    shards = [0.0, 0.0]
    for k in range(near):
        tail = side_refs[k][start:, :].astype(F32)
        ids = tail[8 : 8 + dp_count, :seq]
        ids = jnp.broadcast_to(ids[:, None, :], (dp_count, frames, seq)).reshape(dp_count * frames, seq)
        pick = jnp.where(jnp.logical_and(same, ids == block), 1.0, 0.0).astype(BF)
        shards[2 * k // near] += lax.dot_general(
            pick, tail[8 + dp_count :].astype(BF), (((0,), (0,)), ((), ())), preferred_element_type=F32
        )
    packed_ref[...] = dot_nt(weight_ref[...], shards[0].astype(BF)).astype(BF)
    partial = dot_nt(shards[0].T.astype(BF), mine_ref[...]) + dot_nt(shards[1].T.astype(BF), other)
    depth = -(-(n1 + n2) // 128) * 128
    lane = lax.broadcasted_iota(jnp.int32, (rows, depth), 1)
    of_first, of_second, factors, sums = [], [], [], 0.0
    for k in range(near):
        at = k % 2 * rows
        side = column_refs[near // 2 * (k % 2) + k // 2][at : at + rows][:, :depth].astype(F32)
        of_first.append(jnp.where(lane < n1, side, 0.0).astype(BF))
        of_second.append(jnp.where(jnp.logical_and(lane >= n1, lane < start), side, 0.0).astype(BF))
        factors.append(side_refs[k][:depth, :])
        tail = side_refs[k][start : start + 16, :].astype(F32)
        sums += tail[0:4] + tail[4:8]
    factors = jnp.concatenate(factors, axis=0)
    first = dot(jnp.concatenate(of_first, axis=1), factors)
    second = dot(jnp.concatenate(of_second, axis=1), factors)
    high = sums.astype(BF).astype(F32)
    each = channels // dp_count
    for z in range(far):
        low_rows = partial[2 * z * each : (2 * z + 1) * each]
        high_rows = partial[(2 * z + 1) * each : (2 * z + 2) * each]
        held[z] = jnp.concatenate(
            [
                first[z * owned : (z + 1) * owned],
                second[z * owned : (z + 1) * owned],
                high,
                sums - high,
                pack(jnp.where(me_ref[3] == 0, low_rows, high_rows), channels),
            ],
            axis=0,
        )
    own_ref[...] = held[me_ref[2]]
    for f in range(1, far):
        out_refs[f - 1][...] = held[me_ref[2] ^ f].astype(BF)


def norm_back(grad, slope_ref, hat_ref, scale_ref, gain):
    pre = grad * slope_ref[...]
    hat = hat_ref[...]
    by_hat = pre * hat
    inner = pre * gain
    average = jnp.mean(inner, axis=-1, keepdims=True)
    along = jnp.mean(inner * hat, axis=-1, keepdims=True)
    back = (inner - average - hat * along) * scale_ref[:, 0:1]
    return (
        back.astype(BF),
        jnp.sum(by_hat, axis=0, keepdims=True),
        jnp.sum(pre, axis=0, keepdims=True),
    )


def back_kernel(slots_ref, got_ref, state_ref, weight_ref, out_ref, *, frames):
    channels = weight_ref.shape[2]
    slope1_ref, slope2_ref, hat1_ref, hat2_ref, scale1_ref, scale2_ref, pick_ref, gain_ref = state_views(state_ref)
    slots = slots_ref[...]
    grads = dot(pick_ref[:, : slots.shape[0]].astype(BF), slots)
    second, gain2, shift2 = norm_back(grads, slope2_ref, hat2_ref, scale2_ref, gain_ref[1:2, :])
    hidden = jnp.concatenate(
        [
            dot_nt(second, weight_ref[1, :channels, :]),
            dot_nt(second, weight_ref[1, channels:, :]),
        ],
        axis=0,
    )
    hidden = hidden.astype(BF).astype(F32)
    first, gain1, shift1 = norm_back(hidden, slope1_ref, hat1_ref, scale1_ref, gain_ref[0:1, :])
    sums = jnp.concatenate([gain1, shift1, gain2, shift2], axis=0)
    high = sums.astype(BF).astype(F32)
    ids = got_ref[...].astype(F32)
    slots32 = slots.astype(F32)
    rows = [high, sums - high, jnp.concatenate([ids] * (channels // ids.shape[1]), axis=1)]
    rows += [
        slots32[(2 * d + 1) * frames : (2 * d + 2) * frames] for d in range(slots.shape[0] // (2 * frames))
    ]
    n1, n2 = first.shape[0], second.shape[0]
    out_ref[:n1, :] = first
    out_ref[n1 : n1 + n2, :] = second
    out_ref[n1 + n2 :, :] = jnp.concatenate(rows, axis=0).astype(BF)


def input_kernel(me_ref, grad_ref, weight_ref, out_ref, *, pairs, frames):
    channels = weight_ref.shape[2]
    n1 = 2 * pairs * frames
    first = grad_ref[:n1, :]
    rows = jnp.concatenate(
        [dot_nt(first, weight_ref[0, :channels, :]), dot_nt(first, weight_ref[0, channels:, :])],
        axis=0,
    ).astype(BF)
    row = lax.broadcasted_iota(jnp.int32, (1, 2 * n1), 1)
    source = source_of(row, me_ref, pairs, frames)
    place = lax.broadcasted_iota(jnp.int32, (out_ref.shape[0], 2 * n1), 0)
    pick = jnp.where(place == source, 1.0, 0.0).astype(BF)
    out_ref[...] = dot(pick, rows).astype(BF)


def last_kernel(me_ref, *refs, owned, far):
    conv_ref, norm_ref, proj_ref = refs[far:]
    total = refs[0][...]
    for f in range(1, far):
        total += refs[f][...].astype(F32)
    conv_ref[0] = total[:owned]
    conv_ref[1] = total[owned : 2 * owned]
    proj_ref[...] = unpack(total[2 * owned + 8 :], *proj_ref.shape)
    channels = total.shape[1]
    sums = total[2 * owned : 2 * owned + 4] + total[2 * owned + 4 : 2 * owned + 8]
    start = me_ref[0] * owned
    later = start >= channels
    lines = jnp.concatenate(
        [jnp.where(later, sums[2 * k + 1 : 2 * k + 2], sums[2 * k : 2 * k + 1]) for k in range(2)]
        + [jnp.zeros((6, channels), F32)],
        axis=0,
    )
    start = jnp.where(later, start - channels, start)
    lines = pltpu.roll(lines, lax.rem(channels - start, channels), 1)
    norm_ref[...] = lines[:2, :owned]


def local(
    features, lengths, dests, offsets, conv_weight, norm_gain, norm_shift, proj_weight, grad_packed
):
    utt_count, positions, channels = features.shape
    frames = positions // 4
    pairs = utt_count // 2
    dp_count = lax.axis_size("dp")
    mp_count = lax.axis_size("mp")
    seq = grad_packed.shape[0]
    width = grad_packed.shape[1]
    owned = 2 * channels // (dp_count * mp_count)
    n1, n2 = 2 * pairs * frames, pairs * frames
    near, far = 2 * mp_count, dp_count // 2
    everyone = ("dp", "mp")

    def swap(x, mask):
        return lax.ppermute(x, everyone, [(i, i ^ mask) for i in range(dp_count * mp_count)])

    bits = [1 << b for b in range(mp_count.bit_length() - 1)][::-1]
    me, index, grad_rows = call(
        functools.partial(start_kernel, pairs=pairs, frames=frames, mp_count=mp_count),
        [
            shape(4 + 6 * pairs, kind=jnp.int32),
            shape(dp_count, 128, kind=jnp.int32),
            shape(seq, channels),
        ],
        (proj_weight.T, grad_packed.T, lengths, dests, offsets),
        fetched=5,
        to_scalars=1,
        flops=2 * seq * width * channels,
        scratch=[
            pltpu.VMEM((width, channels), BF),
            pltpu.VMEM((width, seq), BF),
            pltpu.SMEM(lengths.shape, jnp.int32),
            pltpu.SMEM(dests.shape, jnp.int32),
            pltpu.SMEM(offsets.shape, jnp.int32),
            pltpu.SemaphoreType.DMA((5,)),
        ],
        mebibytes=56,
    )
    feat = features.reshape(utt_count * positions, channels)
    got_index = lax.all_to_all(index, "dp", split_axis=0, concat_axis=0, tiled=True)

    wide = max(-(-(n1 + n2) // 128) * 128, seq)
    cotangent = grad_packed.T
    tall = (2 * channels, channels)
    made = call(
        functools.partial(
            forward_kernel, pairs=pairs, frames=frames, far=far, near=near, owned=owned
        ),
        [
            shape(*me.shape, kind=jnp.int32),
            shape(dp_count * frames, channels),
            shape(10 * n2 + 8, channels, kind=F32),
        ]
        + [
            shape(2 * far * owned + (width if 2 * k == mp_count else 0), wide)
            for k in range(near // 2)
        ],
        (me, feat, norm_gain, norm_shift, conv_weight, cotangent),
        scalars=1,
        fetched=5,
        to_scalars=1,
        flops=10**10,
        scratch=[
            pltpu.VMEM(feat.shape, BF),
            pltpu.VMEM(norm_gain.shape, F32),
            pltpu.VMEM(norm_shift.shape, F32),
            pltpu.VMEM(tall, BF),
            pltpu.VMEM(tall, BF),
            pltpu.VMEM((2 * channels, wide), F32),
            pltpu.SemaphoreType.DMA((6,)),
        ],
        mebibytes=56,
    )
    me, pair_frames, state = made[:3]
    in_sides = [swap(side, 2 * k) if k else side for k, side in enumerate(made[3:])]

    for mask in bits[:0:-1]:
        grad_rows = (grad_rows.astype(F32) + swap(grad_rows, mask).astype(F32)).astype(BF)
    other_rows = swap(grad_rows, bits[0])

    sent = call(
        functools.partial(send_kernel, frames=frames),
        shape(dp_count, 2 * frames, channels),
        (got_index, grad_rows, other_rows, pair_frames),
        scalars=1,
        scratch=[pltpu.VMEM((seq, channels), F32)],
    )
    slots = lax.all_to_all(sent, "dp", split_axis=0, concat_axis=0, tiled=True)
    slots, *in_sides[: near // 2] = lax.optimization_barrier((slots, *in_sides[: near // 2]))

    in_sides += [swap(side, 1) for side in in_sides]
    rows_sent = n1 + n2 + 8 + dp_count * (1 + frames)
    grads = call(
        functools.partial(back_kernel, frames=frames),
        shape(rows_sent, channels),
        (slots.reshape(-1, channels), got_index, state, conv_weight),
        flops=2 * n2 * 2 * channels * channels,
    )
    by_mask = {mask: swap(grads, mask) if mask else grads for mask in range(0, near, 2)}
    for mask in range(0, near, 2):
        by_mask[mask + 1] = swap(by_mask[mask], 1)

    per_dp = channels // dp_count
    packed_rows = per_dp * width // channels
    sides = tuple(by_mask[k] for k in range(near))
    rows_out = 2 * owned + 8 + packed_rows
    packed, *parts = call(
        functools.partial(
            gradient_kernel, n1=n1, n2=n2, owned=owned, near=near, far=far, frames=frames
        ),
        [shape(width, seq), shape(rows_out, channels, kind=F32)]
        + [shape(rows_out, channels)] * (far - 1),
        (me, *sides, *in_sides, proj_weight.T, cotangent),
        scalars=1,
        flops=2 * (n1 + n2) * 2 * channels * channels,
        scratch=[pltpu.VMEM((far, rows_out, channels), F32)],
    )

    grad_features = call(
        functools.partial(input_kernel, pairs=pairs, frames=frames),
        shape(utt_count * positions, channels),
        (me, grads, conv_weight),
        scalars=1,
        flops=2 * n1 * 2 * channels * channels,
    ).reshape(utt_count, positions, channels)

    got = [swap(part, near * f) if f else part for f, part in enumerate(parts)]
    grad_conv, grad_norm, grad_proj = call(
        functools.partial(last_kernel, owned=owned, far=far),
        [
            shape(2, owned, channels, kind=F32),
            shape(2, owned, kind=F32),
            shape(per_dp, width, kind=F32),
        ],
        (me, *got),
        scalars=1,
    )
    return (packed.T, grad_features, grad_conv, grad_norm, grad_proj)


def solution(mesh):
    return jax.shard_map(
        local,
        mesh=mesh,
        in_specs=(
            P(("dp", "mp"), None, None),
            P(("dp", "mp")),
            P(("dp", "mp")),
            P(("dp", "mp")),
            P(),
            P(),
            P(),
            P(None, "mp"),
            P("dp", "mp"),
        ),
        out_specs=(
            P("dp", "mp"),
            P(("dp", "mp"), None, None),
            P(None, ("dp", "mp"), None),
            P(None, ("dp", "mp")),
            P("dp", "mp"),
        ),
        check_vma=False,
    )
```

```python
import functools
import math

import jax
import jax.numpy as jnp
from jax import lax
from jax.experimental import pallas as pl
from jax.experimental.pallas import tpu as pltpu
from jax.sharding import PartitionSpec as P

epsilon = 1e-05
BF = jnp.bfloat16
F32 = jnp.float32
VMEM = pltpu.VMEM
SMEM = pltpu.SMEM


def call(body, out, args, scalars=0, fetched=0, flops=0, scratch=(), mebibytes=14, to_scalars=0):
    specs = [
        pl.BlockSpec(memory_space=SMEM if i < scalars else pl.ANY if i < scalars + fetched else VMEM)
        for i in range(len(args))
    ]
    many = isinstance(out, (list, tuple))
    moved = sum(a.size * a.dtype.itemsize for a in args)
    return pl.pallas_call(
        body,
        out_shape=out,
        in_specs=specs,
        out_specs=[
            pl.BlockSpec(memory_space=SMEM if i < to_scalars else VMEM) for i in range(len(out))
        ]
        if many
        else pl.BlockSpec(memory_space=VMEM),
        scratch_shapes=list(scratch),
        compiler_params=pltpu.CompilerParams(vmem_limit_bytes=mebibytes * 2**20),
        cost_estimate=pl.CostEstimate(flops=flops, bytes_accessed=moved, transcendentals=0),
    )(*args)


def shape(*dims, kind=BF):
    return jax.ShapeDtypeStruct(dims, kind)


def dot(a, b):
    return jnp.dot(a, b, preferred_element_type=F32)


def dot_nt(a, b):
    return lax.dot_general(a, b, (((1,), (1,)), ((), ())), preferred_element_type=F32)


def norm_parts(pre):
    average = jnp.mean(pre, axis=-1, keepdims=True)
    centred = pre - average
    spread = jnp.mean(centred * centred, axis=-1, keepdims=True)
    scale = lax.rsqrt(spread + epsilon)
    return centred * scale, scale


def gelu_parts(value):
    half = 0.5 * (1.0 + lax.erf(value * math.sqrt(0.5)))
    density = jnp.exp(-0.5 * value * value) * (1.0 / math.sqrt(2.0 * math.pi))
    return value * half, half + value * density


def source_of(row, me_ref, pairs, frames):
    part = lax.div(row, pairs * frames)
    inner = lax.rem(row, pairs * frames)
    pair = lax.div(inner, frames)
    t = lax.rem(inner, frames)
    first = jnp.zeros_like(row)
    for p in range(pairs):
        first = jnp.where(pair == p, me_ref[4 + 2 * p], first)
    off = jnp.where(part == 1, 2, jnp.where(part == 2, 1, part))
    t_from = jnp.where(t < first, t, t + frames - first)
    return pair * (8 * frames) + 4 * t_from + off


def start_kernel(
    proj_hbm, cotangent_hbm, lengths_hbm, dests_hbm, offsets_hbm, me_ref, index_ref, rows_ref,
    proj_ref, cotangent_ref, lengths_ref, dests_ref, offsets_ref, copied, *, pairs, frames, mp_count
):
    sources = (proj_hbm, cotangent_hbm, lengths_hbm, dests_hbm, offsets_hbm)
    targets = (proj_ref, cotangent_ref, lengths_ref, dests_ref, offsets_ref)
    copies = [
        pltpu.make_async_copy(source, target, copied.at[i])
        for i, (source, target) in enumerate(zip(sources, targets))
    ]
    for copy in copies[::-1]:
        copy.start()
    for copy in copies[2:]:
        copy.wait()
    at_dp, at_mp = lax.axis_index("dp"), lax.axis_index("mp")
    me_ref[0] = at_dp * mp_count + at_mp
    me_ref[1] = lax.rem(at_dp, 2) * mp_count + at_mp
    me_ref[2] = lax.div(at_dp, 2)
    me_ref[3] = lax.rem(at_dp, 2)
    for i in range(2 * pairs):
        me_ref[4 + i] = lengths_ref[i]
        me_ref[4 + 2 * pairs + i] = dests_ref[i]
        me_ref[4 + 4 * pairs + i] = offsets_ref[i]
    shard = lax.broadcasted_iota(jnp.int32, index_ref.shape, 0)
    value = jnp.zeros(index_ref.shape, jnp.int32)
    for p in range(pairs):
        block = lax.div(offsets_ref[2 * p], frames)
        value = jnp.where(shard == dests_ref[2 * p], block + 1, value)
    index_ref[...] = value
    copies[0].wait()
    copies[1].wait()
    rows_ref[...] = lax.dot_general(
        cotangent_ref[...], proj_ref[...], (((0,), (0,)), ((), ())), preferred_element_type=F32
    ).astype(BF)


def state_views(state_ref):
    part = (state_ref.shape[0] - 8) // 7
    spans = ((0, 2), (2, 1), (3, 2), (5, 1), (6, 1))
    return [state_ref.at[a * part : (a + n) * part] for a, n in spans] + [state_ref.at[7 * part :]]


def forward_kernel(me_ref, *refs, pairs, frames, far, near, owned):
    weight_ref, cotangent_hbm = refs[3:5]
    rest, held, in_turned, copied = refs[5:-7], refs[-7:-2], refs[-2], refs[-1]
    with_cotangent = rest[3 + near // 4]
    own_rows = 2 * far * owned
    tail = with_cotangent.at[own_rows:, : cotangent_hbm.shape[1]]
    sources = refs[:3] + (weight_ref.at[0], weight_ref.at[1], cotangent_hbm)
    targets = held + (tail,)
    copies = [
        pltpu.make_async_copy(source, target, copied.at[i])
        for i, (source, target) in enumerate(zip(sources, targets))
    ]
    for copy in copies:
        copy.start()
    feat_ref, gain_ref, shift_ref, first_ref, second_ref = held
    later_ref, frames_ref, state_ref = rest[:3]
    turned_refs = rest[3:]
    for i in range(me_ref.shape[0]):
        later_ref[i] = me_ref[i]
    slope1_ref, slope2_ref, hat1_ref, hat2_ref, aux_ref, gain_at = state_views(state_ref)
    copies[0].wait()
    channels = feat_ref.shape[1]
    n2 = pairs * frames
    row = lax.broadcasted_iota(jnp.int32, (4 * n2, 1), 0)
    source = source_of(row, me_ref, pairs, frames)
    place = lax.broadcasted_iota(jnp.int32, (4 * n2, feat_ref.shape[0]), 1)
    pick = jnp.where(place == source, 1.0, 0.0).astype(BF)
    chosen32 = dot(pick, feat_ref[...])
    chosen = chosen32.astype(BF)
    for copy in copies[1:4]:
        copy.wait()
    even, odd = chosen[: 2 * n2], chosen[2 * n2 :]
    first = dot(even, first_ref[:channels, :]) + dot(odd, first_ref[channels:, :])
    hat, scale = norm_parts(first)
    hidden, slope = gelu_parts(hat * gain_ref[0:1, :] + shift_ref[0:1, :])
    slope1_ref[...] = slope
    hat1_ref[...] = hat
    aux = [scale[:n2], scale[n2:]]
    hidden = hidden.astype(BF)
    hidden32 = hidden.astype(F32)
    copies[4].wait()
    second = dot(hidden[:n2], second_ref[:channels, :]) + dot(hidden[n2:], second_ref[channels:, :])
    hat, scale = norm_parts(second)
    made, slope = gelu_parts(hat * gain_ref[1:2, :] + shift_ref[1:2, :])
    slope2_ref[...] = slope
    hat2_ref[...] = hat
    aux.append(scale)
    none = jnp.zeros((frames, channels), F32)
    sent = []
    for d in range(frames_ref.shape[0] // frames):
        rows = none
        for p in range(pairs):
            rows = jnp.where(me_ref[4 + 2 * pairs + 2 * p] == d, made[p * frames : (p + 1) * frames], rows)
        sent.append(rows)
    frames_ref[...] = jnp.concatenate(sent, axis=0).astype(BF)
    row = lax.broadcasted_iota(jnp.int32, (n2, 1), 0)
    slot = jnp.zeros_like(row)
    for p in range(pairs):
        slot = jnp.where(lax.div(row, frames) == p, me_ref[4 + 2 * pairs + 2 * p], slot)
    slot = slot * (2 * frames) + lax.rem(row, frames)
    aux.append(slot.astype(F32))
    aux_ref[...] = jnp.concatenate([jnp.broadcast_to(a, (n2, channels // 4)) for a in aux], axis=1)
    gain_at[...] = jnp.concatenate([gain_ref[...], jnp.zeros((6, channels), F32)], axis=0)
    wide = in_turned.shape[1]
    fill = [jnp.zeros((wide - 3 * n2, channels), F32)] if wide > 3 * n2 else []
    for tap in range(2):
        stacked = jnp.concatenate(
            [chosen32[2 * n2 * tap : 2 * n2 * (tap + 1)], hidden32[n2 * tap : n2 * (tap + 1)]] + fill,
            axis=0,
        )
        in_turned[channels * tap : channels * (tap + 1), :] = stacked.T
    at = me_ref[1]
    for k, turned_ref in enumerate(turned_refs):
        turned_ref[:own_rows, :] = jnp.concatenate(
            [
                in_turned[pl.ds(pl.multiple_of((z * near + (at ^ (2 * k + c))) * owned, owned), owned), :]
                for c in range(2)
                for z in range(far)
            ],
            axis=0,
        ).astype(BF)
    copies[5].wait()


def send_kernel(got_ref, mine_ref, other_ref, sent_ref, out_ref, rows32, *, frames):
    rows32[...] = mine_ref[...].astype(F32) + other_ref[...].astype(F32)
    blocks = rows32.shape[0] // frames
    sent = sent_ref[...].astype(F32)
    none = jnp.zeros((frames, sent.shape[1]), F32)
    for d in range(out_ref.shape[0]):
        block = got_ref[d, 0] - 1
        safe = jnp.clip(block, 0, blocks - 1)
        grads = rows32[pl.ds(pl.multiple_of(safe * frames, frames), frames), :]
        grads = jnp.where(block >= 0, grads, none)
        out_ref[d] = jnp.concatenate([grads, sent[d * frames : (d + 1) * frames]], axis=0).astype(BF)


def pack(rows, channels):
    r, w = rows.shape
    parts, start = [], 0
    while start < w:
        lanes = min(1 << ((w - start).bit_length() - 1), channels)
        each = r * lanes // channels
        parts.append(
            jnp.concatenate(
                [rows[g * each : (g + 1) * each, start : start + lanes] for g in range(r // each)], axis=1
            )
        )
        start += lanes
    return jnp.concatenate(parts, axis=0)


def unpack(packed, r, w):
    channels = packed.shape[1]
    parts, start, at = [], 0, 0
    while start < w:
        lanes = min(1 << ((w - start).bit_length() - 1), channels)
        each = r * lanes // channels
        block = packed[at : at + each]
        parts.append(
            jnp.concatenate([block[:, g * lanes : (g + 1) * lanes] for g in range(r // each)], axis=0)
        )
        start += lanes
        at += each
    return jnp.concatenate(parts, axis=1)


def gradient_kernel(me_ref, *refs, n1, n2, owned, near, far, frames):
    side_refs, column_refs = refs[:near], refs[near : 2 * near]
    weight_ref, mine_ref, packed_ref, own_ref = refs[2 * near : 2 * near + 4]
    out_refs, held = refs[2 * near + 4 : -1], refs[-1]
    start = n1 + n2
    rows = far * owned
    other = column_refs[near // 4][2 * rows :][:, : mine_ref.shape[1]]
    channels, seq = weight_ref.shape[1], packed_ref.shape[1]
    dp_count = (side_refs[0].shape[0] - start - 8) // (1 + frames)
    row = lax.broadcasted_iota(jnp.int32, (dp_count * frames, seq), 0)
    lane = lax.broadcasted_iota(jnp.int32, (dp_count * frames, seq), 1)
    block = (lax.div(lane, frames) + 1).astype(F32)
    same = lax.rem(lane, frames) == lax.rem(row, frames)
    shards = []
    for first_k in range(0, near, near // 2):
        picks, sent = [], []
        for k in range(first_k, first_k + near // 2):
            tail = side_refs[k][start:, :].astype(F32)
            ids = tail[8 : 8 + dp_count, :seq]
            ids = jnp.broadcast_to(ids[:, None, :], (dp_count, frames, seq)).reshape(dp_count * frames, seq)
            picks.append(jnp.where(jnp.logical_and(same, ids == block), 1.0, 0.0))
            sent.append(tail[8 + dp_count :].astype(BF))
        pick = jnp.concatenate(picks, axis=0).T.astype(BF)
        shards.append(dot(pick, jnp.concatenate(sent, axis=0)))
    packed_ref[...] = dot_nt(weight_ref[...], shards[0].astype(BF)).astype(BF)
    partial = dot_nt(shards[0].T.astype(BF), mine_ref[...]) + dot_nt(shards[1].T.astype(BF), other)
    depth = -(-(n1 + n2) // 128) * 128
    lane = lax.broadcasted_iota(jnp.int32, (rows, depth), 1)
    of_first, of_second, factors, sums = [], [], [], 0.0
    for k in range(near):
        at = k % 2 * rows
        side = column_refs[near // 2 * (k % 2) + k // 2][at : at + rows][:, :depth].astype(F32)
        of_first.append(jnp.where(lane < n1, side, 0.0).astype(BF))
        of_second.append(jnp.where(jnp.logical_and(lane >= n1, lane < start), side, 0.0).astype(BF))
        factors.append(side_refs[k][:depth, :])
        tail = side_refs[k][start : start + 16, :].astype(F32)
        sums += tail[0:4] + tail[4:8]
    factors = jnp.concatenate(factors, axis=0)
    first = dot(jnp.concatenate(of_first, axis=1), factors)
    second = dot(jnp.concatenate(of_second, axis=1), factors)
    high = sums.astype(BF).astype(F32)
    each = channels // dp_count
    for z in range(far):
        low_rows = partial[2 * z * each : (2 * z + 1) * each]
        high_rows = partial[(2 * z + 1) * each : (2 * z + 2) * each]
        held[z] = jnp.concatenate(
            [
                first[z * owned : (z + 1) * owned],
                second[z * owned : (z + 1) * owned],
                high,
                sums - high,
                pack(jnp.where(me_ref[3] == 0, low_rows, high_rows), channels),
            ],
            axis=0,
        )
    own_ref[...] = held[me_ref[2]]
    for f in range(1, far):
        out_refs[f - 1][...] = held[me_ref[2] ^ f].astype(BF)


def norm_back(grad, slope_ref, hat_ref, scale, gain):
    pre = grad * slope_ref[...]
    hat = hat_ref[...]
    by_hat = pre * hat
    inner = pre * gain
    average = jnp.mean(inner, axis=-1, keepdims=True)
    along = jnp.mean(inner * hat, axis=-1, keepdims=True)
    back = (inner - average - hat * along) * scale
    return (
        back.astype(BF),
        jnp.sum(by_hat, axis=0, keepdims=True),
        jnp.sum(pre, axis=0, keepdims=True),
    )


def back_kernel(slots_ref, got_ref, state_ref, weight_ref, out_ref, *, frames):
    channels = weight_ref.shape[2]
    slope1_ref, slope2_ref, hat1_ref, hat2_ref, aux_ref, gain_ref = state_views(state_ref)
    slots = slots_ref[...]
    lanes = channels // 4
    scale1 = jnp.concatenate([aux_ref[:, 0:1], aux_ref[:, lanes : lanes + 1]], axis=0)
    scale2 = aux_ref[:, 2 * lanes : 2 * lanes + 1]
    n2 = aux_ref.shape[0]
    place = lax.broadcasted_iota(jnp.int32, (n2, slots.shape[0]), 1).astype(F32)
    pick = jnp.where(place == aux_ref[:, 3 * lanes : 3 * lanes + 1], 1.0, 0.0).astype(BF)
    grads = dot(pick, slots)
    second, gain2, shift2 = norm_back(grads, slope2_ref, hat2_ref, scale2, gain_ref[1:2, :])
    hidden = jnp.concatenate(
        [
            dot_nt(second, weight_ref[1, :channels, :]),
            dot_nt(second, weight_ref[1, channels:, :]),
        ],
        axis=0,
    )
    hidden = hidden.astype(BF).astype(F32)
    first, gain1, shift1 = norm_back(hidden, slope1_ref, hat1_ref, scale1, gain_ref[0:1, :])
    sums = jnp.concatenate([gain1, shift1, gain2, shift2], axis=0)
    high = sums.astype(BF).astype(F32)
    ids = got_ref[...].astype(F32)
    slots32 = slots.astype(F32)
    rows = [high, sums - high, jnp.concatenate([ids] * (channels // ids.shape[1]), axis=1)]
    rows += [
        slots32[(2 * d + 1) * frames : (2 * d + 2) * frames] for d in range(slots.shape[0] // (2 * frames))
    ]
    n1, n2 = first.shape[0], second.shape[0]
    out_ref[:n1, :] = first
    out_ref[n1 : n1 + n2, :] = second
    out_ref[n1 + n2 :, :] = jnp.concatenate(rows, axis=0).astype(BF)


def input_kernel(me_ref, grad_ref, weight_ref, out_ref, *, pairs, frames):
    channels = weight_ref.shape[2]
    n1 = 2 * pairs * frames
    first = grad_ref[:n1, :]
    rows = jnp.concatenate(
        [dot_nt(first, weight_ref[0, :channels, :]), dot_nt(first, weight_ref[0, channels:, :])],
        axis=0,
    ).astype(BF)
    row = lax.broadcasted_iota(jnp.int32, (1, 2 * n1), 1)
    source = source_of(row, me_ref, pairs, frames)
    place = lax.broadcasted_iota(jnp.int32, (out_ref.shape[0], 2 * n1), 0)
    pick = jnp.where(place == source, 1.0, 0.0).astype(BF)
    out_ref[...] = dot(pick, rows).astype(BF)


def last_kernel(me_ref, *refs, owned, far):
    conv_ref, norm_ref, proj_ref = refs[far:]
    total = refs[0][...]
    for f in range(1, far):
        total += refs[f][...].astype(F32)
    conv_ref[0] = total[:owned]
    conv_ref[1] = total[owned : 2 * owned]
    proj_ref[...] = unpack(total[2 * owned + 8 :], *proj_ref.shape)
    channels = total.shape[1]
    sums = total[2 * owned : 2 * owned + 4] + total[2 * owned + 4 : 2 * owned + 8]
    start = me_ref[0] * owned
    later = start >= channels
    lines = jnp.concatenate(
        [jnp.where(later, sums[2 * k + 1 : 2 * k + 2], sums[2 * k : 2 * k + 1]) for k in range(2)]
        + [jnp.zeros((6, channels), F32)],
        axis=0,
    )
    start = jnp.where(later, start - channels, start)
    lines = pltpu.roll(lines, lax.rem(channels - start, channels), 1)
    norm_ref[...] = lines[:2, :owned]


def local(
    features, lengths, dests, offsets, conv_weight, norm_gain, norm_shift, proj_weight, grad_packed
):
    utt_count, positions, channels = features.shape
    frames = positions // 4
    pairs = utt_count // 2
    dp_count = lax.axis_size("dp")
    mp_count = lax.axis_size("mp")
    seq = grad_packed.shape[0]
    width = grad_packed.shape[1]
    owned = 2 * channels // (dp_count * mp_count)
    n1, n2 = 2 * pairs * frames, pairs * frames
    near, far = 2 * mp_count, dp_count // 2
    everyone = ("dp", "mp")

    def swap(x, mask):
        return lax.ppermute(x, everyone, [(i, i ^ mask) for i in range(dp_count * mp_count)])

    bits = [1 << b for b in range(mp_count.bit_length() - 1)][::-1]
    me, index, grad_rows = call(
        functools.partial(start_kernel, pairs=pairs, frames=frames, mp_count=mp_count),
        [
            shape(4 + 6 * pairs, kind=jnp.int32),
            shape(dp_count, 128, kind=jnp.int32),
            shape(seq, channels),
        ],
        (proj_weight.T, grad_packed.T, lengths, dests, offsets),
        fetched=5,
        to_scalars=1,
        flops=2 * seq * width * channels,
        scratch=[
            pltpu.VMEM((width, channels), BF),
            pltpu.VMEM((width, seq), BF),
            pltpu.SMEM(lengths.shape, jnp.int32),
            pltpu.SMEM(dests.shape, jnp.int32),
            pltpu.SMEM(offsets.shape, jnp.int32),
            pltpu.SemaphoreType.DMA((5,)),
        ],
        mebibytes=56,
    )
    feat = features.reshape(utt_count * positions, channels)
    got_index = lax.all_to_all(index, "dp", split_axis=0, concat_axis=0, tiled=True)

    wide = max(-(-(n1 + n2) // 128) * 128, seq)
    cotangent = grad_packed.T
    tall = (2 * channels, channels)
    made = call(
        functools.partial(
            forward_kernel, pairs=pairs, frames=frames, far=far, near=near, owned=owned
        ),
        [
            shape(*me.shape, kind=jnp.int32),
            shape(dp_count * frames, channels),
            shape(7 * n2 + 8, channels, kind=F32),
        ]
        + [
            shape(2 * far * owned + (width if 2 * k == mp_count else 0), wide)
            for k in range(near // 2)
        ],
        (me, feat, norm_gain, norm_shift, conv_weight, cotangent),
        scalars=1,
        fetched=5,
        to_scalars=1,
        flops=10**10,
        scratch=[
            pltpu.VMEM(feat.shape, BF),
            pltpu.VMEM(norm_gain.shape, F32),
            pltpu.VMEM(norm_shift.shape, F32),
            pltpu.VMEM(tall, BF),
            pltpu.VMEM(tall, BF),
            pltpu.VMEM((2 * channels, wide), F32),
            pltpu.SemaphoreType.DMA((6,)),
        ],
        mebibytes=56,
    )
    me, pair_frames, state = made[:3]
    in_sides = [swap(side, 2 * k) if k else side for k, side in enumerate(made[3:])]

    for mask in bits[:0:-1]:
        grad_rows = (grad_rows.astype(F32) + swap(grad_rows, mask).astype(F32)).astype(BF)
    other_rows = swap(grad_rows, bits[0])

    sent = call(
        functools.partial(send_kernel, frames=frames),
        shape(dp_count, 2 * frames, channels),
        (got_index, grad_rows, other_rows, pair_frames),
        scalars=1,
        scratch=[pltpu.VMEM((seq, channels), F32)],
    )
    slots = lax.all_to_all(sent, "dp", split_axis=0, concat_axis=0, tiled=True)
    slots, *in_sides[:2] = lax.optimization_barrier((slots, *in_sides[:2]))

    rows_sent = n1 + n2 + 8 + dp_count * (1 + frames)
    grads = call(
        functools.partial(back_kernel, frames=frames),
        shape(rows_sent, channels),
        (slots.reshape(-1, channels), got_index, state, conv_weight),
        flops=2 * n2 * 2 * channels * channels,
    )
    by_mask = {0: grads}
    for mask in range(2, near, 2):
        leaving = grads
        if mask == near - 2:
            leaving, *in_sides[2 : near // 2] = lax.optimization_barrier(
                (grads, *in_sides[2 : near // 2])
            )
        by_mask[mask] = swap(leaving, mask)
    in_sides += [swap(side, 1) for side in in_sides]
    for mask in range(0, near, 2):
        by_mask[mask + 1] = swap(by_mask[mask], 1)

    per_dp = channels // dp_count
    packed_rows = per_dp * width // channels
    sides = tuple(by_mask[k] for k in range(near))
    rows_out = 2 * owned + 8 + packed_rows
    packed, *parts = call(
        functools.partial(
            gradient_kernel, n1=n1, n2=n2, owned=owned, near=near, far=far, frames=frames
        ),
        [shape(width, seq), shape(rows_out, channels, kind=F32)]
        + [shape(rows_out, channels)] * (far - 1),
        (me, *sides, *in_sides, proj_weight.T, cotangent),
        scalars=1,
        flops=2 * (n1 + n2) * 2 * channels * channels,
        scratch=[pltpu.VMEM((far, rows_out, channels), F32)],
    )

    grad_features = call(
        functools.partial(input_kernel, pairs=pairs, frames=frames),
        shape(utt_count * positions, channels),
        (me, grads, conv_weight),
        scalars=1,
        flops=2 * n1 * 2 * channels * channels,
    ).reshape(utt_count, positions, channels)

    got = [swap(part, near * f) if f else part for f, part in enumerate(parts)]
    grad_conv, grad_norm, grad_proj = call(
        functools.partial(last_kernel, owned=owned, far=far),
        [
            shape(2, owned, channels, kind=F32),
            shape(2, owned, kind=F32),
            shape(per_dp, width, kind=F32),
        ],
        (me, *got),
        scalars=1,
    )
    return (packed.T, grad_features, grad_conv, grad_norm, grad_proj)


def solution(mesh):
    return jax.shard_map(
        local,
        mesh=mesh,
        in_specs=(
            P(("dp", "mp"), None, None),
            P(("dp", "mp")),
            P(("dp", "mp")),
            P(("dp", "mp")),
            P(),
            P(),
            P(),
            P(None, "mp"),
            P("dp", "mp"),
        ),
        out_specs=(
            P("dp", "mp"),
            P(("dp", "mp"), None, None),
            P(None, ("dp", "mp"), None),
            P(None, ("dp", "mp")),
            P("dp", "mp"),
        ),
        check_vma=False,
    )
```

```python
import functools
import math

import jax
import jax.numpy as jnp
from jax import lax
from jax.experimental import pallas as pl
from jax.experimental.pallas import tpu as pltpu
from jax.sharding import PartitionSpec as P

epsilon = 1e-05
BF = jnp.bfloat16
F32 = jnp.float32
VMEM = pltpu.VMEM
SMEM = pltpu.SMEM


def call(body, out, args, scalars=0, fetched=0, flops=0, scratch=(), mebibytes=14, to_scalars=0):
    specs = [
        pl.BlockSpec(memory_space=SMEM if i < scalars else pl.ANY if i < scalars + fetched else VMEM)
        for i in range(len(args))
    ]
    many = isinstance(out, (list, tuple))
    moved = sum(a.size * a.dtype.itemsize for a in args)
    return pl.pallas_call(
        body,
        out_shape=out,
        in_specs=specs,
        out_specs=[
            pl.BlockSpec(memory_space=SMEM if i < to_scalars else VMEM) for i in range(len(out))
        ]
        if many
        else pl.BlockSpec(memory_space=VMEM),
        scratch_shapes=list(scratch),
        compiler_params=pltpu.CompilerParams(vmem_limit_bytes=mebibytes * 2**20),
        cost_estimate=pl.CostEstimate(flops=flops, bytes_accessed=moved, transcendentals=0),
    )(*args)


def shape(*dims, kind=BF):
    return jax.ShapeDtypeStruct(dims, kind)


def dot(a, b):
    return jnp.dot(a, b, preferred_element_type=F32)


def dot_nt(a, b):
    return lax.dot_general(a, b, (((1,), (1,)), ((), ())), preferred_element_type=F32)


def norm_parts(pre):
    average = jnp.mean(pre, axis=-1, keepdims=True)
    centred = pre - average
    spread = jnp.mean(centred * centred, axis=-1, keepdims=True)
    scale = lax.rsqrt(spread + epsilon)
    return centred * scale, scale


def gelu_parts(value):
    half = 0.5 * (1.0 + lax.erf(value * math.sqrt(0.5)))
    density = jnp.exp(-0.5 * value * value) * (1.0 / math.sqrt(2.0 * math.pi))
    return value * half, half + value * density


def source_of(row, me_ref, pairs, frames):
    part = lax.div(row, pairs * frames)
    inner = lax.rem(row, pairs * frames)
    pair = lax.div(inner, frames)
    t = lax.rem(inner, frames)
    first = jnp.zeros_like(row)
    for p in range(pairs):
        first = jnp.where(pair == p, me_ref[4 + 2 * p], first)
    off = jnp.where(part == 1, 2, jnp.where(part == 2, 1, part))
    t_from = jnp.where(t < first, t, t + frames - first)
    return pair * (8 * frames) + 4 * t_from + off


def start_kernel(
    proj_hbm, cotangent_hbm, lengths_hbm, dests_hbm, offsets_hbm, me_ref, index_ref, rows_ref,
    proj_ref, cotangent_ref, lengths_ref, dests_ref, offsets_ref, copied, *, pairs, frames, mp_count
):
    sources = (proj_hbm, cotangent_hbm, lengths_hbm, dests_hbm, offsets_hbm)
    targets = (proj_ref, cotangent_ref, lengths_ref, dests_ref, offsets_ref)
    copies = [
        pltpu.make_async_copy(source, target, copied.at[i])
        for i, (source, target) in enumerate(zip(sources, targets))
    ]
    for copy in copies[::-1]:
        copy.start()
    for copy in copies[2:]:
        copy.wait()
    at_dp, at_mp = lax.axis_index("dp"), lax.axis_index("mp")
    me_ref[0] = at_dp * mp_count + at_mp
    me_ref[1] = lax.rem(at_dp, 2) * mp_count + at_mp
    me_ref[2] = lax.div(at_dp, 2)
    me_ref[3] = lax.rem(at_dp, 2)
    for i in range(2 * pairs):
        me_ref[4 + i] = lengths_ref[i]
        me_ref[4 + 2 * pairs + i] = dests_ref[i]
        me_ref[4 + 4 * pairs + i] = offsets_ref[i]
    shard = lax.broadcasted_iota(jnp.int32, index_ref.shape, 0)
    value = jnp.zeros(index_ref.shape, jnp.int32)
    for p in range(pairs):
        block = lax.div(offsets_ref[2 * p], frames)
        value = jnp.where(shard == dests_ref[2 * p], block + 1, value)
    index_ref[...] = value
    copies[0].wait()
    copies[1].wait()
    rows_ref[...] = lax.dot_general(
        cotangent_ref[...], proj_ref[...], (((0,), (0,)), ((), ())), preferred_element_type=F32
    ).astype(BF)


def state_views(state_ref):
    part = (state_ref.shape[0] - 8) // 7
    spans = ((0, 2), (2, 1), (3, 2), (5, 1), (6, 1))
    return [state_ref.at[a * part : (a + n) * part] for a, n in spans] + [state_ref.at[7 * part :]]


def forward_kernel(me_ref, *refs, pairs, frames, far, near, owned):
    weight_ref, cotangent_hbm = refs[3:5]
    rest, held, in_turned, copied = refs[5:-7], refs[-7:-2], refs[-2], refs[-1]
    with_cotangent = rest[3 + near // 4]
    own_rows = 2 * far * owned
    tail = with_cotangent.at[own_rows:, : cotangent_hbm.shape[1]]
    sources = refs[:3] + (weight_ref.at[0], weight_ref.at[1], cotangent_hbm)
    targets = held + (tail,)
    copies = [
        pltpu.make_async_copy(source, target, copied.at[i])
        for i, (source, target) in enumerate(zip(sources, targets))
    ]
    for copy in copies:
        copy.start()
    feat_ref, gain_ref, shift_ref, first_ref, second_ref = held
    later_ref, frames_ref, state_ref = rest[:3]
    turned_refs = rest[3:]
    for i in range(me_ref.shape[0]):
        later_ref[i] = me_ref[i]
    slope1_ref, slope2_ref, hat1_ref, hat2_ref, aux_ref, gain_at = state_views(state_ref)
    copies[0].wait()
    channels = feat_ref.shape[1]
    n2 = pairs * frames
    row = lax.broadcasted_iota(jnp.int32, (4 * n2, 1), 0)
    source = source_of(row, me_ref, pairs, frames)
    place = lax.broadcasted_iota(jnp.int32, (4 * n2, feat_ref.shape[0]), 1)
    pick = jnp.where(place == source, 1.0, 0.0).astype(BF)
    chosen32 = dot(pick, feat_ref[...])
    chosen = chosen32.astype(BF)
    for copy in copies[1:4]:
        copy.wait()
    even, odd = chosen[: 2 * n2], chosen[2 * n2 :]
    first = dot(even, first_ref[:channels, :]) + dot(odd, first_ref[channels:, :])
    hat, scale = norm_parts(first)
    hidden, slope = gelu_parts(hat * gain_ref[0:1, :] + shift_ref[0:1, :])
    slope1_ref[...] = slope
    hat1_ref[...] = hat
    aux = [scale[:n2], scale[n2:]]
    hidden = hidden.astype(BF)
    hidden32 = hidden.astype(F32)
    copies[4].wait()
    second = dot(hidden[:n2], second_ref[:channels, :]) + dot(hidden[n2:], second_ref[channels:, :])
    hat, scale = norm_parts(second)
    made, slope = gelu_parts(hat * gain_ref[1:2, :] + shift_ref[1:2, :])
    slope2_ref[...] = slope
    hat2_ref[...] = hat
    aux.append(scale)
    none = jnp.zeros((frames, channels), F32)
    sent = []
    for d in range(frames_ref.shape[0] // frames):
        rows = none
        for p in range(pairs):
            rows = jnp.where(me_ref[4 + 2 * pairs + 2 * p] == d, made[p * frames : (p + 1) * frames], rows)
        sent.append(rows)
    frames_ref[...] = jnp.concatenate(sent, axis=0).astype(BF)
    row = lax.broadcasted_iota(jnp.int32, (n2, 1), 0)
    slot = jnp.zeros_like(row)
    for p in range(pairs):
        slot = jnp.where(lax.div(row, frames) == p, me_ref[4 + 2 * pairs + 2 * p], slot)
    slot = slot * (2 * frames) + lax.rem(row, frames)
    aux.append(slot.astype(F32))
    aux_ref[...] = jnp.concatenate([jnp.broadcast_to(a, (n2, channels // 4)) for a in aux], axis=1)
    gain_at[...] = jnp.concatenate([gain_ref[...], jnp.zeros((6, channels), F32)], axis=0)
    wide = in_turned.shape[1]
    fill = [jnp.zeros((wide - 3 * n2, channels), F32)] if wide > 3 * n2 else []
    for tap in range(2):
        stacked = jnp.concatenate(
            [chosen32[2 * n2 * tap : 2 * n2 * (tap + 1)], hidden32[n2 * tap : n2 * (tap + 1)]] + fill,
            axis=0,
        )
        in_turned[channels * tap : channels * (tap + 1), :] = stacked.T
    at = me_ref[1]
    for k, turned_ref in enumerate(turned_refs):
        turned_ref[:own_rows, :] = jnp.concatenate(
            [
                in_turned[pl.ds(pl.multiple_of((z * near + (at ^ (2 * k + c))) * owned, owned), owned), :]
                for c in range(2)
                for z in range(far)
            ],
            axis=0,
        ).astype(BF)
    copies[5].wait()


def send_kernel(got_ref, mine_ref, other_ref, sent_ref, out_ref, rows32, *, frames):
    rows32[...] = mine_ref[...].astype(F32) + other_ref[...].astype(F32)
    blocks = rows32.shape[0] // frames
    sent = sent_ref[...].astype(F32)
    none = jnp.zeros((frames, sent.shape[1]), F32)
    for d in range(out_ref.shape[0]):
        block = got_ref[d, 0] - 1
        safe = jnp.clip(block, 0, blocks - 1)
        grads = rows32[pl.ds(pl.multiple_of(safe * frames, frames), frames), :]
        grads = jnp.where(block >= 0, grads, none)
        out_ref[d] = jnp.concatenate([grads, sent[d * frames : (d + 1) * frames]], axis=0).astype(BF)


def pack(rows, channels):
    r, w = rows.shape
    parts, start = [], 0
    while start < w:
        lanes = min(1 << ((w - start).bit_length() - 1), channels)
        each = r * lanes // channels
        parts.append(
            jnp.concatenate(
                [rows[g * each : (g + 1) * each, start : start + lanes] for g in range(r // each)], axis=1
            )
        )
        start += lanes
    return jnp.concatenate(parts, axis=0)


def unpack(packed, r, w):
    channels = packed.shape[1]
    parts, start, at = [], 0, 0
    while start < w:
        lanes = min(1 << ((w - start).bit_length() - 1), channels)
        each = r * lanes // channels
        block = packed[at : at + each]
        parts.append(
            jnp.concatenate([block[:, g * lanes : (g + 1) * lanes] for g in range(r // each)], axis=0)
        )
        start += lanes
        at += each
    return jnp.concatenate(parts, axis=1)


def gradient_kernel(me_ref, *refs, n1, n2, owned, near, far, frames):
    side_refs, column_refs = refs[:near], refs[near : 2 * near]
    weight_ref, mine_ref, packed_ref, own_ref = refs[2 * near : 2 * near + 4]
    out_refs, held = refs[2 * near + 4 : -1], refs[-1]
    start = n1 + n2
    rows = far * owned
    other = column_refs[near // 4][2 * rows :][:, : mine_ref.shape[1]]
    channels, seq = weight_ref.shape[1], packed_ref.shape[1]
    dp_count = (side_refs[0].shape[0] - start - 8) // (1 + frames)
    row = lax.broadcasted_iota(jnp.int32, (dp_count * frames, seq), 0)
    lane = lax.broadcasted_iota(jnp.int32, (dp_count * frames, seq), 1)
    block = (lax.div(lane, frames) + 1).astype(F32)
    same = lax.rem(lane, frames) == lax.rem(row, frames)
    shards = []
    for first_k in range(0, near, near // 2):
        picks, sent = [], []
        for k in range(first_k, first_k + near // 2):
            tail = side_refs[k][start:, :].astype(F32)
            ids = tail[8 : 8 + dp_count, :seq]
            ids = jnp.broadcast_to(ids[:, None, :], (dp_count, frames, seq)).reshape(dp_count * frames, seq)
            picks.append(jnp.where(jnp.logical_and(same, ids == block), 1.0, 0.0))
            rows_of = tail[8 + dp_count :]
            if first_k:
                rows_of = jnp.concatenate([rows_of[:, : channels // 2], rows_of[:, channels // 2 :]], axis=0)
            sent.append(rows_of.astype(BF))
        pick = jnp.concatenate(picks, axis=0).T.astype(BF)
        shards.append(dot(pick, jnp.concatenate(sent, axis=0)))
    packed_ref[...] = dot_nt(weight_ref[...], shards[0].astype(BF)).astype(BF)
    partial = dot_nt(shards[0].T.astype(BF), mine_ref[...])
    theirs = dot_nt(shards[1].T.astype(BF), other)
    each = channels // dp_count
    depth = -(-(n1 + n2) // 128) * 128
    lane = lax.broadcasted_iota(jnp.int32, (rows, depth), 1)
    of_first, of_second, factors, sums = [], [], [], 0.0
    for k in range(near):
        at = k % 2 * rows
        side = column_refs[near // 2 * (k % 2) + k // 2][at : at + rows][:, :depth].astype(F32)
        of_first.append(jnp.where(lane < n1, side, 0.0).astype(BF))
        of_second.append(jnp.where(jnp.logical_and(lane >= n1, lane < start), side, 0.0).astype(BF))
        factors.append(side_refs[k][:depth, :])
        tail = side_refs[k][start : start + 16, :].astype(F32)
        sums += tail[0:4] + tail[4:8]
    factors = jnp.concatenate(factors, axis=0)
    first = dot(jnp.concatenate(of_first, axis=1), factors)
    second = dot(jnp.concatenate(of_second, axis=1), factors)
    high = sums.astype(BF).astype(F32)
    each = channels // dp_count
    for z in range(far):
        low_rows = partial[2 * z * each : (2 * z + 1) * each]
        high_rows = partial[(2 * z + 1) * each : (2 * z + 2) * each]
        held[z] = jnp.concatenate(
            [
                first[z * owned : (z + 1) * owned],
                second[z * owned : (z + 1) * owned],
                high,
                sums - high,
                pack(
                    jnp.where(me_ref[3] == 0, low_rows, high_rows) + theirs[z * each : (z + 1) * each], channels
                ),
            ],
            axis=0,
        )
    own_ref[...] = held[me_ref[2]]
    for f in range(1, far):
        out_refs[f - 1][...] = held[me_ref[2] ^ f].astype(BF)


def norm_back(grad, slope_ref, hat_ref, scale, gain):
    pre = grad * slope_ref[...]
    hat = hat_ref[...]
    by_hat = pre * hat
    inner = pre * gain
    average = jnp.mean(inner, axis=-1, keepdims=True)
    along = jnp.mean(inner * hat, axis=-1, keepdims=True)
    back = (inner - average - hat * along) * scale
    return (
        back.astype(BF),
        jnp.sum(by_hat, axis=0, keepdims=True),
        jnp.sum(pre, axis=0, keepdims=True),
    )


def back_kernel(slots_ref, got_ref, state_ref, weight_ref, out_ref, half_ref, *, frames):
    channels = weight_ref.shape[2]
    slope1_ref, slope2_ref, hat1_ref, hat2_ref, aux_ref, gain_ref = state_views(state_ref)
    slots = slots_ref[...]
    lanes = channels // 4
    scale1 = jnp.concatenate([aux_ref[:, 0:1], aux_ref[:, lanes : lanes + 1]], axis=0)
    scale2 = aux_ref[:, 2 * lanes : 2 * lanes + 1]
    n2 = aux_ref.shape[0]
    place = lax.broadcasted_iota(jnp.int32, (n2, slots.shape[0]), 1).astype(F32)
    pick = jnp.where(place == aux_ref[:, 3 * lanes : 3 * lanes + 1], 1.0, 0.0).astype(BF)
    grads = dot(pick, slots)
    second, gain2, shift2 = norm_back(grads, slope2_ref, hat2_ref, scale2, gain_ref[1:2, :])
    hidden = jnp.concatenate(
        [
            dot_nt(second, weight_ref[1, :channels, :]),
            dot_nt(second, weight_ref[1, channels:, :]),
        ],
        axis=0,
    )
    hidden = hidden.astype(BF).astype(F32)
    first, gain1, shift1 = norm_back(hidden, slope1_ref, hat1_ref, scale1, gain_ref[0:1, :])
    sums = jnp.concatenate([gain1, shift1, gain2, shift2], axis=0)
    high = sums.astype(BF).astype(F32)
    ids = got_ref[...].astype(F32)
    slots32 = slots.astype(F32)
    rows = [high, sums - high, jnp.concatenate([ids] * (channels // ids.shape[1]), axis=1)]
    sent = jnp.concatenate(
        [
            slots32[(2 * d + 1) * frames : (2 * d + 2) * frames]
            for d in range(slots.shape[0] // (2 * frames))
        ],
        axis=0,
    )
    dp_count = ids.shape[0]
    each = channels // dp_count
    odd_here = lax.rem(lax.axis_index("dp"), 2) == 1
    half = jnp.concatenate(
        [
            jnp.where(
                odd_here,
                sent[:, 2 * z * each : (2 * z + 1) * each],
                sent[:, (2 * z + 1) * each : (2 * z + 2) * each],
            )
            for z in range(dp_count // 2)
        ],
        axis=1,
    )
    middle = half.shape[0] // 2
    half = jnp.concatenate([half[:middle], half[middle:]], axis=1)
    n1, n2 = first.shape[0], second.shape[0]
    out_ref[:n1, :] = first
    out_ref[n1 : n1 + n2, :] = second
    out_ref[n1 + n2 :, :] = jnp.concatenate(rows + [sent], axis=0).astype(BF)
    half_ref[:n1, :] = first
    half_ref[n1 : n1 + n2, :] = second
    half_ref[n1 + n2 :, :] = jnp.concatenate(rows + [half], axis=0).astype(BF)


def input_kernel(me_ref, grad_ref, weight_ref, out_ref, *, pairs, frames):
    channels = weight_ref.shape[2]
    n1 = 2 * pairs * frames
    first = grad_ref[:n1, :]
    rows = jnp.concatenate(
        [dot_nt(first, weight_ref[0, :channels, :]), dot_nt(first, weight_ref[0, channels:, :])],
        axis=0,
    ).astype(BF)
    row = lax.broadcasted_iota(jnp.int32, (1, 2 * n1), 1)
    source = source_of(row, me_ref, pairs, frames)
    place = lax.broadcasted_iota(jnp.int32, (out_ref.shape[0], 2 * n1), 0)
    pick = jnp.where(place == source, 1.0, 0.0).astype(BF)
    out_ref[...] = dot(pick, rows).astype(BF)


def last_kernel(me_ref, *refs, owned, far):
    conv_ref, norm_ref, proj_ref = refs[far:]
    total = refs[0][...]
    for f in range(1, far):
        total += refs[f][...].astype(F32)
    conv_ref[0] = total[:owned]
    conv_ref[1] = total[owned : 2 * owned]
    proj_ref[...] = unpack(total[2 * owned + 8 :], *proj_ref.shape)
    channels = total.shape[1]
    sums = total[2 * owned : 2 * owned + 4] + total[2 * owned + 4 : 2 * owned + 8]
    start = me_ref[0] * owned
    later = start >= channels
    lines = jnp.concatenate(
        [jnp.where(later, sums[2 * k + 1 : 2 * k + 2], sums[2 * k : 2 * k + 1]) for k in range(2)]
        + [jnp.zeros((6, channels), F32)],
        axis=0,
    )
    start = jnp.where(later, start - channels, start)
    lines = pltpu.roll(lines, lax.rem(channels - start, channels), 1)
    norm_ref[...] = lines[:2, :owned]


def local(
    features, lengths, dests, offsets, conv_weight, norm_gain, norm_shift, proj_weight, grad_packed
):
    utt_count, positions, channels = features.shape
    frames = positions // 4
    pairs = utt_count // 2
    dp_count = lax.axis_size("dp")
    mp_count = lax.axis_size("mp")
    seq = grad_packed.shape[0]
    width = grad_packed.shape[1]
    owned = 2 * channels // (dp_count * mp_count)
    n1, n2 = 2 * pairs * frames, pairs * frames
    near, far = 2 * mp_count, dp_count // 2
    everyone = ("dp", "mp")

    def swap(x, mask):
        return lax.ppermute(x, everyone, [(i, i ^ mask) for i in range(dp_count * mp_count)])

    bits = [1 << b for b in range(mp_count.bit_length() - 1)][::-1]
    me, index, grad_rows = call(
        functools.partial(start_kernel, pairs=pairs, frames=frames, mp_count=mp_count),
        [
            shape(4 + 6 * pairs, kind=jnp.int32),
            shape(dp_count, 128, kind=jnp.int32),
            shape(seq, channels),
        ],
        (proj_weight.T, grad_packed.T, lengths, dests, offsets),
        fetched=5,
        to_scalars=1,
        flops=2 * seq * width * channels,
        scratch=[
            pltpu.VMEM((width, channels), BF),
            pltpu.VMEM((width, seq), BF),
            pltpu.SMEM(lengths.shape, jnp.int32),
            pltpu.SMEM(dests.shape, jnp.int32),
            pltpu.SMEM(offsets.shape, jnp.int32),
            pltpu.SemaphoreType.DMA((5,)),
        ],
        mebibytes=56,
    )
    feat = features.reshape(utt_count * positions, channels)
    got_index = lax.all_to_all(index, "dp", split_axis=0, concat_axis=0, tiled=True)

    wide = max(-(-(n1 + n2) // 128) * 128, seq)
    cotangent = grad_packed.T
    tall = (2 * channels, channels)
    made = call(
        functools.partial(
            forward_kernel, pairs=pairs, frames=frames, far=far, near=near, owned=owned
        ),
        [
            shape(*me.shape, kind=jnp.int32),
            shape(dp_count * frames, channels),
            shape(7 * n2 + 8, channels, kind=F32),
        ]
        + [
            shape(2 * far * owned + (width if 2 * k == mp_count else 0), wide)
            for k in range(near // 2)
        ],
        (me, feat, norm_gain, norm_shift, conv_weight, cotangent),
        scalars=1,
        fetched=5,
        to_scalars=1,
        flops=10**10,
        scratch=[
            pltpu.VMEM(feat.shape, BF),
            pltpu.VMEM(norm_gain.shape, F32),
            pltpu.VMEM(norm_shift.shape, F32),
            pltpu.VMEM(tall, BF),
            pltpu.VMEM(tall, BF),
            pltpu.VMEM((2 * channels, wide), F32),
            pltpu.SemaphoreType.DMA((6,)),
        ],
        mebibytes=56,
    )
    me, pair_frames, state = made[:3]
    in_sides = [swap(side, 2 * k) if k else side for k, side in enumerate(made[3:])]

    for mask in bits[:0:-1]:
        grad_rows = (grad_rows.astype(F32) + swap(grad_rows, mask).astype(F32)).astype(BF)
    other_rows = swap(grad_rows, bits[0])

    sent = call(
        functools.partial(send_kernel, frames=frames),
        shape(dp_count, 2 * frames, channels),
        (got_index, grad_rows, other_rows, pair_frames),
        scalars=1,
        scratch=[pltpu.VMEM((seq, channels), F32)],
    )
    slots = lax.all_to_all(sent, "dp", split_axis=0, concat_axis=0, tiled=True)
    slots, *in_sides[:2] = lax.optimization_barrier((slots, *in_sides[:2]))

    rows_sent = n1 + n2 + 8 + dp_count * (1 + frames)
    grads, half_grads = call(
        functools.partial(back_kernel, frames=frames),
        [shape(rows_sent, channels), shape(rows_sent - dp_count * frames // 2, channels)],
        (slots.reshape(-1, channels), got_index, state, conv_weight),
        flops=2 * n2 * 2 * channels * channels,
    )
    by_mask = {0: grads}
    for mask in range(2, near, 2):
        leaving = grads if mask < mp_count else half_grads
        if mask == near - 2:
            leaving, *in_sides[2 : near // 2] = lax.optimization_barrier(
                (leaving, *in_sides[2 : near // 2])
            )
        by_mask[mask] = swap(leaving, mask)
    in_sides += [swap(side, 1) for side in in_sides]
    for mask in range(0, near, 2):
        by_mask[mask + 1] = swap(by_mask[mask], 1)

    per_dp = channels // dp_count
    packed_rows = per_dp * width // channels
    sides = tuple(by_mask[k] for k in range(near))
    rows_out = 2 * owned + 8 + packed_rows
    packed, *parts = call(
        functools.partial(
            gradient_kernel, n1=n1, n2=n2, owned=owned, near=near, far=far, frames=frames
        ),
        [shape(width, seq), shape(rows_out, channels, kind=F32)]
        + [shape(rows_out, channels)] * (far - 1),
        (me, *sides, *in_sides, proj_weight.T, cotangent),
        scalars=1,
        flops=2 * (n1 + n2) * 2 * channels * channels,
        scratch=[pltpu.VMEM((far, rows_out, channels), F32)],
    )

    grad_features = call(
        functools.partial(input_kernel, pairs=pairs, frames=frames),
        shape(utt_count * positions, channels),
        (me, grads, conv_weight),
        scalars=1,
        flops=2 * n1 * 2 * channels * channels,
    ).reshape(utt_count, positions, channels)

    got = [swap(part, near * f) if f else part for f, part in enumerate(parts)]
    grad_conv, grad_norm, grad_proj = call(
        functools.partial(last_kernel, owned=owned, far=far),
        [
            shape(2, owned, channels, kind=F32),
            shape(2, owned, kind=F32),
            shape(per_dp, width, kind=F32),
        ],
        (me, *got),
        scalars=1,
    )
    return (packed.T, grad_features, grad_conv, grad_norm, grad_proj)


def solution(mesh):
    return jax.shard_map(
        local,
        mesh=mesh,
        in_specs=(
            P(("dp", "mp"), None, None),
            P(("dp", "mp")),
            P(("dp", "mp")),
            P(("dp", "mp")),
            P(),
            P(),
            P(),
            P(None, "mp"),
            P("dp", "mp"),
        ),
        out_specs=(
            P("dp", "mp"),
            P(("dp", "mp"), None, None),
            P(None, ("dp", "mp"), None),
            P(None, ("dp", "mp")),
            P("dp", "mp"),
        ),
        check_vma=False,
    )
```

```python
import functools
import math

import jax
import jax.numpy as jnp
from jax import lax
from jax.experimental import pallas as pl
from jax.experimental.pallas import tpu as pltpu
from jax.sharding import PartitionSpec as P

epsilon = 1e-05
BF = jnp.bfloat16
F32 = jnp.float32
VMEM = pltpu.VMEM
SMEM = pltpu.SMEM


def call(body, out, args, scalars=0, fetched=0, flops=0, scratch=(), mebibytes=14, to_scalars=0):
    specs = [
        pl.BlockSpec(memory_space=SMEM if i < scalars else pl.ANY if i < scalars + fetched else VMEM)
        for i in range(len(args))
    ]
    many = isinstance(out, (list, tuple))
    moved = sum(a.size * a.dtype.itemsize for a in args)
    return pl.pallas_call(
        body,
        out_shape=out,
        in_specs=specs,
        out_specs=[
            pl.BlockSpec(memory_space=SMEM if i < to_scalars else VMEM) for i in range(len(out))
        ]
        if many
        else pl.BlockSpec(memory_space=VMEM),
        scratch_shapes=list(scratch),
        compiler_params=pltpu.CompilerParams(vmem_limit_bytes=mebibytes * 2**20),
        cost_estimate=pl.CostEstimate(flops=flops, bytes_accessed=moved, transcendentals=0),
    )(*args)


def shape(*dims, kind=BF):
    return jax.ShapeDtypeStruct(dims, kind)


def dot(a, b):
    return jnp.dot(a, b, preferred_element_type=F32)


def dot_nt(a, b):
    return lax.dot_general(a, b, (((1,), (1,)), ((), ())), preferred_element_type=F32)


def norm_parts(pre):
    average = jnp.mean(pre, axis=-1, keepdims=True)
    centred = pre - average
    spread = jnp.mean(centred * centred, axis=-1, keepdims=True)
    scale = lax.rsqrt(spread + epsilon)
    return centred * scale, scale


def gelu_parts(value):
    half = 0.5 * (1.0 + lax.erf(value * math.sqrt(0.5)))
    density = jnp.exp(-0.5 * value * value) * (1.0 / math.sqrt(2.0 * math.pi))
    return value * half, half + value * density


def source_of(row, me_ref, pairs, frames):
    part = lax.div(row, pairs * frames)
    inner = lax.rem(row, pairs * frames)
    pair = lax.div(inner, frames)
    t = lax.rem(inner, frames)
    first = jnp.zeros_like(row)
    for p in range(pairs):
        first = jnp.where(pair == p, me_ref[4 + 2 * p], first)
    off = jnp.where(part == 1, 2, jnp.where(part == 2, 1, part))
    t_from = jnp.where(t < first, t, t + frames - first)
    return pair * (8 * frames) + 4 * t_from + off


def start_kernel(
    proj_hbm, cotangent_hbm, lengths_hbm, dests_hbm, offsets_hbm, me_ref, index_ref, rows_ref,
    proj_ref, cotangent_ref, lengths_ref, dests_ref, offsets_ref, copied, *, pairs, frames, mp_count
):
    sources = (proj_hbm, cotangent_hbm, lengths_hbm, dests_hbm, offsets_hbm)
    targets = (proj_ref, cotangent_ref, lengths_ref, dests_ref, offsets_ref)
    copies = [
        pltpu.make_async_copy(source, target, copied.at[i])
        for i, (source, target) in enumerate(zip(sources, targets))
    ]
    for copy in copies[::-1]:
        copy.start()
    for copy in copies[2:]:
        copy.wait()
    at_dp, at_mp = lax.axis_index("dp"), lax.axis_index("mp")
    me_ref[0] = at_dp * mp_count + at_mp
    me_ref[1] = lax.rem(at_dp, 2) * mp_count + at_mp
    me_ref[2] = lax.div(at_dp, 2)
    me_ref[3] = lax.rem(at_dp, 2)
    for i in range(2 * pairs):
        me_ref[4 + i] = lengths_ref[i]
        me_ref[4 + 2 * pairs + i] = dests_ref[i]
        me_ref[4 + 4 * pairs + i] = offsets_ref[i]
    shard = lax.broadcasted_iota(jnp.int32, index_ref.shape, 0)
    value = jnp.zeros(index_ref.shape, jnp.int32)
    for p in range(pairs):
        block = lax.div(offsets_ref[2 * p], frames)
        value = jnp.where(shard == dests_ref[2 * p], block + 1, value)
    index_ref[...] = value
    copies[0].wait()
    copies[1].wait()
    rows_ref[...] = lax.dot_general(
        cotangent_ref[...], proj_ref[...], (((0,), (0,)), ((), ())), preferred_element_type=F32
    ).astype(BF)


def state_views(state_ref):
    part = (state_ref.shape[0] - 8) // 7
    spans = ((0, 2), (2, 1), (3, 2), (5, 1), (6, 1))
    return [state_ref.at[a * part : (a + n) * part] for a, n in spans] + [state_ref.at[7 * part :]]


def forward_kernel(me_ref, *refs, pairs, frames, far, near, owned):
    weight_ref, cotangent_hbm = refs[3:5]
    rest, held, in_turned, copied = refs[5:-7], refs[-7:-2], refs[-2], refs[-1]
    with_cotangent = rest[3 + near // 4]
    own_rows = 2 * far * owned
    tail = with_cotangent.at[own_rows:, : cotangent_hbm.shape[1]]
    sources = refs[:3] + (weight_ref.at[0], weight_ref.at[1], cotangent_hbm)
    targets = held + (tail,)
    copies = [
        pltpu.make_async_copy(source, target, copied.at[i])
        for i, (source, target) in enumerate(zip(sources, targets))
    ]
    for copy in copies:
        copy.start()
    feat_ref, gain_ref, shift_ref, first_ref, second_ref = held
    later_ref, frames_ref, state_ref = rest[:3]
    turned_refs = rest[3:]
    for i in range(me_ref.shape[0]):
        later_ref[i] = me_ref[i]
    slope1_ref, slope2_ref, hat1_ref, hat2_ref, aux_ref, gain_at = state_views(state_ref)
    copies[0].wait()
    channels = feat_ref.shape[1]
    n2 = pairs * frames
    row = lax.broadcasted_iota(jnp.int32, (4 * n2, 1), 0)
    source = source_of(row, me_ref, pairs, frames)
    place = lax.broadcasted_iota(jnp.int32, (4 * n2, feat_ref.shape[0]), 1)
    pick = jnp.where(place == source, 1.0, 0.0).astype(BF)
    chosen32 = dot(pick, feat_ref[...])
    chosen = chosen32.astype(BF)
    for copy in copies[1:4]:
        copy.wait()
    even, odd = chosen[: 2 * n2], chosen[2 * n2 :]
    first = dot(even, first_ref[:channels, :]) + dot(odd, first_ref[channels:, :])
    hat, scale = norm_parts(first)
    hidden, slope = gelu_parts(hat * gain_ref[0:1, :] + shift_ref[0:1, :])
    slope1_ref[...] = slope
    hat1_ref[...] = hat
    aux = [scale[:n2], scale[n2:]]
    hidden = hidden.astype(BF)
    hidden32 = hidden.astype(F32)
    copies[4].wait()
    second = dot(hidden[:n2], second_ref[:channels, :]) + dot(hidden[n2:], second_ref[channels:, :])
    hat, scale = norm_parts(second)
    made, slope = gelu_parts(hat * gain_ref[1:2, :] + shift_ref[1:2, :])
    slope2_ref[...] = slope
    hat2_ref[...] = hat
    aux.append(scale)
    none = jnp.zeros((frames, channels), F32)
    sent = []
    for d in range(frames_ref.shape[0] // frames):
        rows = none
        for p in range(pairs):
            rows = jnp.where(me_ref[4 + 2 * pairs + 2 * p] == d, made[p * frames : (p + 1) * frames], rows)
        sent.append(rows)
    frames_ref[...] = jnp.concatenate(sent, axis=0).astype(BF)
    row = lax.broadcasted_iota(jnp.int32, (n2, 1), 0)
    slot = jnp.zeros_like(row)
    for p in range(pairs):
        slot = jnp.where(lax.div(row, frames) == p, me_ref[4 + 2 * pairs + 2 * p], slot)
    slot = slot * (2 * frames) + lax.rem(row, frames)
    aux.append(slot.astype(F32))
    aux_ref[...] = jnp.concatenate([jnp.broadcast_to(a, (n2, channels // 4)) for a in aux], axis=1)
    gain_at[...] = jnp.concatenate([gain_ref[...], jnp.zeros((6, channels), F32)], axis=0)
    wide = in_turned.shape[1]
    fill = [jnp.zeros((wide - 3 * n2, channels), F32)] if wide > 3 * n2 else []
    for tap in range(2):
        stacked = jnp.concatenate(
            [chosen32[2 * n2 * tap : 2 * n2 * (tap + 1)], hidden32[n2 * tap : n2 * (tap + 1)]] + fill,
            axis=0,
        )
        in_turned[channels * tap : channels * (tap + 1), :] = stacked.T
    at = me_ref[1]
    for k, turned_ref in enumerate(turned_refs):
        turned_ref[:own_rows, :] = jnp.concatenate(
            [
                in_turned[pl.ds(pl.multiple_of((z * near + (at ^ (2 * k + c))) * owned, owned), owned), :]
                for c in range(2)
                for z in range(far)
            ],
            axis=0,
        ).astype(BF)
    copies[5].wait()


def send_kernel(got_ref, mine_ref, other_ref, sent_ref, out_ref, rows32, *, frames):
    rows32[...] = mine_ref[...].astype(F32) + other_ref[...].astype(F32)
    blocks = rows32.shape[0] // frames
    sent = sent_ref[...].astype(F32)
    none = jnp.zeros((frames, sent.shape[1]), F32)
    for d in range(out_ref.shape[0]):
        block = got_ref[d, 0] - 1
        safe = jnp.clip(block, 0, blocks - 1)
        grads = rows32[pl.ds(pl.multiple_of(safe * frames, frames), frames), :]
        grads = jnp.where(block >= 0, grads, none)
        out_ref[d] = jnp.concatenate([grads, sent[d * frames : (d + 1) * frames]], axis=0).astype(BF)


def pack(rows, channels):
    r, w = rows.shape
    parts, start = [], 0
    while start < w:
        lanes = min(1 << ((w - start).bit_length() - 1), channels)
        each = r * lanes // channels
        parts.append(
            jnp.concatenate(
                [rows[g * each : (g + 1) * each, start : start + lanes] for g in range(r // each)], axis=1
            )
        )
        start += lanes
    return jnp.concatenate(parts, axis=0)


def unpack(packed, r, w):
    channels = packed.shape[1]
    parts, start, at = [], 0, 0
    while start < w:
        lanes = min(1 << ((w - start).bit_length() - 1), channels)
        each = r * lanes // channels
        block = packed[at : at + each]
        parts.append(
            jnp.concatenate([block[:, g * lanes : (g + 1) * lanes] for g in range(r // each)], axis=0)
        )
        start += lanes
        at += each
    return jnp.concatenate(parts, axis=1)


def gradient_kernel(me_ref, *refs, n1, n2, owned, near, far, frames):
    side_refs, column_refs = refs[:near], refs[near : 2 * near]
    weight_ref, mine_ref, packed_ref, own_ref = refs[2 * near : 2 * near + 4]
    out_refs, held = refs[2 * near + 4 : -1], refs[-1]
    start = n1 + n2
    rows = far * owned
    other = column_refs[near // 4][2 * rows :][:, : mine_ref.shape[1]]
    channels, seq = weight_ref.shape[1], packed_ref.shape[1]
    dp_count = (side_refs[0].shape[0] - start - 8) // (1 + frames)
    row = lax.broadcasted_iota(jnp.int32, (dp_count * frames, seq), 0)
    lane = lax.broadcasted_iota(jnp.int32, (dp_count * frames, seq), 1)
    block = (lax.div(lane, frames) + 1).astype(F32)
    same = lax.rem(lane, frames) == lax.rem(row, frames)
    shards = []
    for first_k in range(0, near, near // 2):
        picks, sent = [], []
        for k in range(first_k, first_k + near // 2):
            tail = side_refs[k][start:, :].astype(F32)
            ids = tail[8 : 8 + dp_count, :seq]
            ids = jnp.broadcast_to(ids[:, None, :], (dp_count, frames, seq)).reshape(dp_count * frames, seq)
            picks.append(jnp.where(jnp.logical_and(same, ids == block), 1.0, 0.0))
            rows_of = tail[8 + dp_count :]
            if first_k:
                rows_of = jnp.concatenate([rows_of[:, : channels // 2], rows_of[:, channels // 2 :]], axis=0)
            sent.append(rows_of.astype(BF))
        pick = jnp.concatenate(picks, axis=0).T.astype(BF)
        shards.append(dot(pick, jnp.concatenate(sent, axis=0)))
    packed_ref[...] = dot_nt(weight_ref[...], shards[0].astype(BF)).astype(BF)
    partial = dot_nt(shards[0].T.astype(BF), mine_ref[...])
    theirs = dot_nt(shards[1].T.astype(BF), other)
    each = channels // dp_count
    depth = -(-(n1 + n2) // 128) * 128
    lane = lax.broadcasted_iota(jnp.int32, (rows, depth), 1)
    of_first, of_second, factors, sums = [], [], [], 0.0
    for k in range(near):
        at = k % 2 * rows
        side = column_refs[near // 2 * (k % 2) + k // 2][at : at + rows][:, :depth].astype(F32)
        of_first.append(jnp.where(lane < n1, side, 0.0).astype(BF))
        of_second.append(jnp.where(jnp.logical_and(lane >= n1, lane < start), side, 0.0).astype(BF))
        factors.append(side_refs[k][:depth, :])
        tail = side_refs[k][start : start + 16, :].astype(F32)
        sums += tail[0:4] + tail[4:8]
    factors = jnp.concatenate(factors, axis=0)
    first = dot(jnp.concatenate(of_first, axis=1), factors)
    second = dot(jnp.concatenate(of_second, axis=1), factors)
    high = sums.astype(BF).astype(F32)
    each = channels // dp_count
    for z in range(far):
        low_rows = partial[2 * z * each : (2 * z + 1) * each]
        high_rows = partial[(2 * z + 1) * each : (2 * z + 2) * each]
        held[z] = jnp.concatenate(
            [
                first[z * owned : (z + 1) * owned],
                second[z * owned : (z + 1) * owned],
                high,
                sums - high,
                pack(
                    jnp.where(me_ref[3] == 0, low_rows, high_rows) + theirs[z * each : (z + 1) * each], channels
                ),
            ],
            axis=0,
        )
    own_ref[...] = held[me_ref[2]]
    for f in range(1, far):
        out_refs[f - 1][...] = held[me_ref[2] ^ f].astype(BF)


def norm_back(grad, slope_ref, hat_ref, scale, gain):
    pre = grad * slope_ref[...]
    hat = hat_ref[...]
    by_hat = pre * hat
    inner = pre * gain
    average = jnp.mean(inner, axis=-1, keepdims=True)
    along = jnp.mean(inner * hat, axis=-1, keepdims=True)
    back = (inner - average - hat * along) * scale
    return (
        back.astype(BF),
        jnp.sum(by_hat, axis=0, keepdims=True),
        jnp.sum(pre, axis=0, keepdims=True),
    )


def back_kernel(slots_ref, got_ref, state_ref, weight_ref, out_ref, half_ref, *, frames):
    channels = weight_ref.shape[2]
    slope1_ref, slope2_ref, hat1_ref, hat2_ref, aux_ref, gain_ref = state_views(state_ref)
    slots = slots_ref[...]
    lanes = channels // 4
    scale1 = jnp.concatenate([aux_ref[:, 0:1], aux_ref[:, lanes : lanes + 1]], axis=0)
    scale2 = aux_ref[:, 2 * lanes : 2 * lanes + 1]
    n2 = aux_ref.shape[0]
    place = lax.broadcasted_iota(jnp.int32, (n2, slots.shape[0]), 1).astype(F32)
    pick = jnp.where(place == aux_ref[:, 3 * lanes : 3 * lanes + 1], 1.0, 0.0).astype(BF)
    grads = dot(pick, slots)
    second, gain2, shift2 = norm_back(grads, slope2_ref, hat2_ref, scale2, gain_ref[1:2, :])
    hidden = jnp.concatenate(
        [
            dot_nt(second, weight_ref[1, :channels, :]),
            dot_nt(second, weight_ref[1, channels:, :]),
        ],
        axis=0,
    )
    hidden = hidden.astype(BF).astype(F32)
    first, gain1, shift1 = norm_back(hidden, slope1_ref, hat1_ref, scale1, gain_ref[0:1, :])
    sums = jnp.concatenate([gain1, shift1, gain2, shift2], axis=0)
    high = sums.astype(BF).astype(F32)
    ids = got_ref[...].astype(F32)
    slots32 = slots.astype(F32)
    rows = [high, sums - high, jnp.concatenate([ids] * (channels // ids.shape[1]), axis=1)]
    sent = jnp.concatenate(
        [
            slots32[(2 * d + 1) * frames : (2 * d + 2) * frames]
            for d in range(slots.shape[0] // (2 * frames))
        ],
        axis=0,
    )
    dp_count = ids.shape[0]
    each = channels // dp_count
    odd_here = lax.rem(lax.axis_index("dp"), 2) == 1
    half = jnp.concatenate(
        [
            jnp.where(
                odd_here,
                sent[:, 2 * z * each : (2 * z + 1) * each],
                sent[:, (2 * z + 1) * each : (2 * z + 2) * each],
            )
            for z in range(dp_count // 2)
        ],
        axis=1,
    )
    middle = half.shape[0] // 2
    half = jnp.concatenate([half[:middle], half[middle:]], axis=1)
    n1, n2 = first.shape[0], second.shape[0]
    out_ref[:n1, :] = first
    out_ref[n1 : n1 + n2, :] = second
    out_ref[n1 + n2 :, :] = jnp.concatenate(rows + [sent], axis=0).astype(BF)
    half_ref[:n1, :] = first
    half_ref[n1 : n1 + n2, :] = second
    half_ref[n1 + n2 :, :] = jnp.concatenate(rows + [half], axis=0).astype(BF)


def input_kernel(me_ref, grad_ref, weight_ref, out_ref, *, pairs, frames):
    channels = weight_ref.shape[2]
    n1 = 2 * pairs * frames
    first = grad_ref[:n1, :]
    rows = jnp.concatenate(
        [dot_nt(first, weight_ref[0, :channels, :]), dot_nt(first, weight_ref[0, channels:, :])],
        axis=0,
    ).astype(BF)
    row = lax.broadcasted_iota(jnp.int32, (1, 2 * n1), 1)
    source = source_of(row, me_ref, pairs, frames)
    place = lax.broadcasted_iota(jnp.int32, (out_ref.shape[0], 2 * n1), 0)
    pick = jnp.where(place == source, 1.0, 0.0).astype(BF)
    out_ref[...] = dot(pick, rows).astype(BF)


def last_kernel(me_ref, *refs, owned, far):
    conv_ref, norm_ref, proj_ref = refs[far:]
    total = refs[0][...]
    for f in range(1, far):
        total += refs[f][...].astype(F32)
    conv_ref[0] = total[:owned]
    conv_ref[1] = total[owned : 2 * owned]
    proj_ref[...] = unpack(total[2 * owned + 8 :], *proj_ref.shape)
    channels = total.shape[1]
    sums = total[2 * owned : 2 * owned + 4] + total[2 * owned + 4 : 2 * owned + 8]
    start = me_ref[0] * owned
    later = start >= channels
    lines = jnp.concatenate(
        [jnp.where(later, sums[2 * k + 1 : 2 * k + 2], sums[2 * k : 2 * k + 1]) for k in range(2)]
        + [jnp.zeros((6, channels), F32)],
        axis=0,
    )
    start = jnp.where(later, start - channels, start)
    lines = pltpu.roll(lines, lax.rem(channels - start, channels), 1)
    norm_ref[...] = lines[:2, :owned]


def local(
    features, lengths, dests, offsets, conv_weight, norm_gain, norm_shift, proj_weight, grad_packed
):
    utt_count, positions, channels = features.shape
    frames = positions // 4
    pairs = utt_count // 2
    dp_count = lax.axis_size("dp")
    mp_count = lax.axis_size("mp")
    seq = grad_packed.shape[0]
    width = grad_packed.shape[1]
    owned = 2 * channels // (dp_count * mp_count)
    n1, n2 = 2 * pairs * frames, pairs * frames
    near, far = 2 * mp_count, dp_count // 2
    everyone = ("dp", "mp")

    def swap(x, mask):
        return lax.ppermute(x, everyone, [(i, i ^ mask) for i in range(dp_count * mp_count)])

    bits = [1 << b for b in range(mp_count.bit_length() - 1)][::-1]
    me, index, grad_rows = call(
        functools.partial(start_kernel, pairs=pairs, frames=frames, mp_count=mp_count),
        [
            shape(4 + 6 * pairs, kind=jnp.int32),
            shape(dp_count, 128, kind=jnp.int32),
            shape(seq, channels),
        ],
        (proj_weight.T, grad_packed.T, lengths, dests, offsets),
        fetched=5,
        to_scalars=1,
        flops=2 * seq * width * channels,
        scratch=[
            pltpu.VMEM((width, channels), BF),
            pltpu.VMEM((width, seq), BF),
            pltpu.SMEM(lengths.shape, jnp.int32),
            pltpu.SMEM(dests.shape, jnp.int32),
            pltpu.SMEM(offsets.shape, jnp.int32),
            pltpu.SemaphoreType.DMA((5,)),
        ],
        mebibytes=56,
    )
    feat = features.reshape(utt_count * positions, channels)
    got_index = lax.all_to_all(index, "dp", split_axis=0, concat_axis=0, tiled=True)

    wide = max(-(-(n1 + n2) // 128) * 128, seq)
    cotangent = grad_packed.T
    tall = (2 * channels, channels)
    made = call(
        functools.partial(
            forward_kernel, pairs=pairs, frames=frames, far=far, near=near, owned=owned
        ),
        [
            shape(*me.shape, kind=jnp.int32),
            shape(dp_count * frames, channels),
            shape(7 * n2 + 8, channels, kind=F32),
        ]
        + [
            shape(2 * far * owned + (width if 2 * k == mp_count else 0), wide)
            for k in range(near // 2)
        ],
        (me, feat, norm_gain, norm_shift, conv_weight, cotangent),
        scalars=1,
        fetched=5,
        to_scalars=1,
        flops=10**10,
        scratch=[
            pltpu.VMEM(feat.shape, BF),
            pltpu.VMEM(norm_gain.shape, F32),
            pltpu.VMEM(norm_shift.shape, F32),
            pltpu.VMEM(tall, BF),
            pltpu.VMEM(tall, BF),
            pltpu.VMEM((2 * channels, wide), F32),
            pltpu.SemaphoreType.DMA((6,)),
        ],
        mebibytes=56,
    )
    me, pair_frames, state = made[:3]
    in_sides = [swap(side, 2 * k) if k else side for k, side in enumerate(made[3:])]

    for mask in bits[:0:-1]:
        grad_rows = (grad_rows.astype(F32) + swap(grad_rows, mask).astype(F32)).astype(BF)
    other_rows = swap(grad_rows, bits[0])

    sent = call(
        functools.partial(send_kernel, frames=frames),
        shape(dp_count, 2 * frames, channels),
        (got_index, grad_rows, other_rows, pair_frames),
        scalars=1,
        scratch=[pltpu.VMEM((seq, channels), F32)],
    )
    slots = lax.all_to_all(sent, "dp", split_axis=0, concat_axis=0, tiled=True)

    rows_sent = n1 + n2 + 8 + dp_count * (1 + frames)
    grads, half_grads = call(
        functools.partial(back_kernel, frames=frames),
        [shape(rows_sent, channels), shape(rows_sent - dp_count * frames // 2, channels)],
        (slots.reshape(-1, channels), got_index, state, conv_weight),
        flops=2 * n2 * 2 * channels * channels,
    )
    by_mask = {0: grads}
    for mask in range(2, near, 2):
        leaving = grads if mask < mp_count else half_grads
        if mask == 4:
            leaving, *in_sides[1 : near // 2] = lax.optimization_barrier(
                (leaving, *in_sides[1 : near // 2])
            )
        by_mask[mask] = swap(leaving, mask)
    in_sides += [swap(side, 1) for side in in_sides]
    for mask in range(0, near, 2):
        by_mask[mask + 1] = swap(by_mask[mask], 1)

    per_dp = channels // dp_count
    packed_rows = per_dp * width // channels
    sides = tuple(by_mask[k] for k in range(near))
    rows_out = 2 * owned + 8 + packed_rows
    packed, *parts = call(
        functools.partial(
            gradient_kernel, n1=n1, n2=n2, owned=owned, near=near, far=far, frames=frames
        ),
        [shape(width, seq), shape(rows_out, channels, kind=F32)]
        + [shape(rows_out, channels)] * (far - 1),
        (me, *sides, *in_sides, proj_weight.T, cotangent),
        scalars=1,
        flops=2 * (n1 + n2) * 2 * channels * channels,
        scratch=[pltpu.VMEM((far, rows_out, channels), F32)],
    )

    grad_features = call(
        functools.partial(input_kernel, pairs=pairs, frames=frames),
        shape(utt_count * positions, channels),
        (me, grads, conv_weight),
        scalars=1,
        flops=2 * n1 * 2 * channels * channels,
    ).reshape(utt_count, positions, channels)

    got = [swap(part, near * f) if f else part for f, part in enumerate(parts)]
    grad_conv, grad_norm, grad_proj = call(
        functools.partial(last_kernel, owned=owned, far=far),
        [
            shape(2, owned, channels, kind=F32),
            shape(2, owned, kind=F32),
            shape(per_dp, width, kind=F32),
        ],
        (me, *got),
        scalars=1,
    )
    return (packed.T, grad_features, grad_conv, grad_norm, grad_proj)


def solution(mesh):
    return jax.shard_map(
        local,
        mesh=mesh,
        in_specs=(
            P(("dp", "mp"), None, None),
            P(("dp", "mp")),
            P(("dp", "mp")),
            P(("dp", "mp")),
            P(),
            P(),
            P(),
            P(None, "mp"),
            P("dp", "mp"),
        ),
        out_specs=(
            P("dp", "mp"),
            P(("dp", "mp"), None, None),
            P(None, ("dp", "mp"), None),
            P(None, ("dp", "mp")),
            P("dp", "mp"),
        ),
        check_vma=False,
    )
```

```python
import functools
import math

import jax
import jax.numpy as jnp
from jax import lax
from jax.experimental import pallas as pl
from jax.experimental.pallas import tpu as pltpu
from jax.sharding import PartitionSpec as P

epsilon = 1e-05
BF = jnp.bfloat16
F32 = jnp.float32
VMEM = pltpu.VMEM
SMEM = pltpu.SMEM


def call(body, out, args, scalars=0, fetched=0, flops=0, scratch=(), mebibytes=14, to_scalars=0):
    specs = [
        pl.BlockSpec(memory_space=SMEM if i < scalars else pl.ANY if i < scalars + fetched else VMEM)
        for i in range(len(args))
    ]
    many = isinstance(out, (list, tuple))
    moved = sum(a.size * a.dtype.itemsize for a in args)
    return pl.pallas_call(
        body,
        out_shape=out,
        in_specs=specs,
        out_specs=[
            pl.BlockSpec(memory_space=SMEM if i < to_scalars else VMEM) for i in range(len(out))
        ]
        if many
        else pl.BlockSpec(memory_space=VMEM),
        scratch_shapes=list(scratch),
        compiler_params=pltpu.CompilerParams(vmem_limit_bytes=mebibytes * 2**20),
        cost_estimate=pl.CostEstimate(flops=flops, bytes_accessed=moved, transcendentals=0),
    )(*args)


def shape(*dims, kind=BF):
    return jax.ShapeDtypeStruct(dims, kind)


def dot(a, b):
    return jnp.dot(a, b, preferred_element_type=F32)


def dot_nt(a, b):
    return lax.dot_general(a, b, (((1,), (1,)), ((), ())), preferred_element_type=F32)


def norm_parts(pre):
    average = jnp.mean(pre, axis=-1, keepdims=True)
    centred = pre - average
    spread = jnp.mean(centred * centred, axis=-1, keepdims=True)
    scale = lax.rsqrt(spread + epsilon)
    return centred * scale, scale


def gelu_parts(value):
    half = 0.5 * (1.0 + lax.erf(value * math.sqrt(0.5)))
    density = jnp.exp(-0.5 * value * value) * (1.0 / math.sqrt(2.0 * math.pi))
    return value * half, half + value * density


def source_of(row, me_ref, pairs, frames):
    part = lax.div(row, pairs * frames)
    inner = lax.rem(row, pairs * frames)
    pair = lax.div(inner, frames)
    t = lax.rem(inner, frames)
    first = jnp.zeros_like(row)
    for p in range(pairs):
        first = jnp.where(pair == p, me_ref[4 + 2 * p], first)
    off = jnp.where(part == 1, 2, jnp.where(part == 2, 1, part))
    t_from = jnp.where(t < first, t, t + frames - first)
    return pair * (8 * frames) + 4 * t_from + off


def start_kernel(
    proj_hbm, cotangent_hbm, lengths_hbm, dests_hbm, offsets_hbm, me_ref, index_ref, rows_ref,
    proj_ref, cotangent_ref, lengths_ref, dests_ref, offsets_ref, copied, *, pairs, frames, mp_count
):
    sources = (proj_hbm, cotangent_hbm, lengths_hbm, dests_hbm, offsets_hbm)
    targets = (proj_ref, cotangent_ref, lengths_ref, dests_ref, offsets_ref)
    copies = [
        pltpu.make_async_copy(source, target, copied.at[i])
        for i, (source, target) in enumerate(zip(sources, targets))
    ]
    for copy in copies[::-1]:
        copy.start()
    for copy in copies[2:]:
        copy.wait()
    at_dp, at_mp = lax.axis_index("dp"), lax.axis_index("mp")
    me_ref[0] = at_dp * mp_count + at_mp
    me_ref[1] = lax.rem(at_dp, 2) * mp_count + at_mp
    me_ref[2] = lax.div(at_dp, 2)
    me_ref[3] = lax.rem(at_dp, 2)
    for i in range(2 * pairs):
        me_ref[4 + i] = lengths_ref[i]
        me_ref[4 + 2 * pairs + i] = dests_ref[i]
        me_ref[4 + 4 * pairs + i] = offsets_ref[i]
    shard = lax.broadcasted_iota(jnp.int32, index_ref.shape, 0)
    value = jnp.zeros(index_ref.shape, jnp.int32)
    for p in range(pairs):
        block = lax.div(offsets_ref[2 * p], frames)
        value = jnp.where(shard == dests_ref[2 * p], block + 1, value)
    index_ref[...] = value
    copies[0].wait()
    copies[1].wait()
    rows_ref[...] = lax.dot_general(
        cotangent_ref[...], proj_ref[...], (((0,), (0,)), ((), ())), preferred_element_type=F32
    ).astype(BF)


def state_views(state_ref):
    part = (state_ref.shape[0] - 8) // 7
    spans = ((0, 2), (2, 1), (3, 2), (5, 1), (6, 1))
    return [state_ref.at[a * part : (a + n) * part] for a, n in spans] + [state_ref.at[7 * part :]]


def forward_kernel(me_ref, *refs, pairs, frames, far, near, owned):
    weight_ref, cotangent_hbm = refs[3:5]
    rest, held, in_turned, copied = refs[5:-7], refs[-7:-2], refs[-2], refs[-1]
    with_cotangent = rest[3 + near // 4]
    own_rows = 2 * far * owned
    tail = with_cotangent.at[own_rows:, : cotangent_hbm.shape[1]]
    sources = refs[:3] + (weight_ref.at[0], weight_ref.at[1], cotangent_hbm)
    targets = held + (tail,)
    copies = [
        pltpu.make_async_copy(source, target, copied.at[i])
        for i, (source, target) in enumerate(zip(sources, targets))
    ]
    for copy in copies:
        copy.start()
    feat_ref, gain_ref, shift_ref, first_ref, second_ref = held
    later_ref, frames_ref, state_ref = rest[:3]
    turned_refs = rest[3:]
    for i in range(me_ref.shape[0]):
        later_ref[i] = me_ref[i]
    slope1_ref, slope2_ref, hat1_ref, hat2_ref, aux_ref, gain_at = state_views(state_ref)
    copies[0].wait()
    channels = feat_ref.shape[1]
    n2 = pairs * frames
    row = lax.broadcasted_iota(jnp.int32, (4 * n2, 1), 0)
    source = source_of(row, me_ref, pairs, frames)
    place = lax.broadcasted_iota(jnp.int32, (4 * n2, feat_ref.shape[0]), 1)
    pick = jnp.where(place == source, 1.0, 0.0).astype(BF)
    chosen32 = dot(pick, feat_ref[...])
    chosen = chosen32.astype(BF)
    for copy in copies[1:4]:
        copy.wait()
    even, odd = chosen[: 2 * n2], chosen[2 * n2 :]
    first = dot(even, first_ref[:channels, :]) + dot(odd, first_ref[channels:, :])
    hat, scale = norm_parts(first)
    hidden, slope = gelu_parts(hat * gain_ref[0:1, :] + shift_ref[0:1, :])
    slope1_ref[...] = slope
    hat1_ref[...] = hat
    aux = [scale[:n2], scale[n2:]]
    hidden = hidden.astype(BF)
    hidden32 = hidden.astype(F32)
    copies[4].wait()
    second = dot(hidden[:n2], second_ref[:channels, :]) + dot(hidden[n2:], second_ref[channels:, :])
    hat, scale = norm_parts(second)
    made, slope = gelu_parts(hat * gain_ref[1:2, :] + shift_ref[1:2, :])
    slope2_ref[...] = slope
    hat2_ref[...] = hat
    aux.append(scale)
    none = jnp.zeros((frames, channels), F32)
    sent = []
    for d in range(frames_ref.shape[0] // frames):
        rows = none
        for p in range(pairs):
            rows = jnp.where(me_ref[4 + 2 * pairs + 2 * p] == d, made[p * frames : (p + 1) * frames], rows)
        sent.append(rows)
    frames_ref[...] = jnp.concatenate(sent, axis=0).astype(BF)
    row = lax.broadcasted_iota(jnp.int32, (n2, 1), 0)
    slot = jnp.zeros_like(row)
    for p in range(pairs):
        slot = jnp.where(lax.div(row, frames) == p, me_ref[4 + 2 * pairs + 2 * p], slot)
    slot = slot * (2 * frames) + lax.rem(row, frames)
    aux.append(slot.astype(F32))
    aux_ref[...] = jnp.concatenate([jnp.broadcast_to(a, (n2, channels // 4)) for a in aux], axis=1)
    gain_at[...] = jnp.concatenate([gain_ref[...], jnp.zeros((6, channels), F32)], axis=0)
    wide = in_turned.shape[1]
    fill = [jnp.zeros((wide - 3 * n2, channels), F32)] if wide > 3 * n2 else []
    for tap in range(2):
        stacked = jnp.concatenate(
            [chosen32[2 * n2 * tap : 2 * n2 * (tap + 1)], hidden32[n2 * tap : n2 * (tap + 1)]] + fill,
            axis=0,
        )
        in_turned[channels * tap : channels * (tap + 1), :] = stacked.T
    at = me_ref[1]
    for k, turned_ref in enumerate(turned_refs):
        turned_ref[:own_rows, :] = jnp.concatenate(
            [
                in_turned[pl.ds(pl.multiple_of((z * near + (at ^ (2 * k + c))) * owned, owned), owned), :]
                for c in range(2)
                for z in range(far)
            ],
            axis=0,
        ).astype(BF)
    copies[5].wait()


def send_kernel(got_ref, mine_ref, other_ref, sent_ref, out_ref, rows32, *, frames):
    rows32[...] = mine_ref[...].astype(F32) + other_ref[...].astype(F32)
    blocks = rows32.shape[0] // frames
    sent = sent_ref[...].astype(F32)
    none = jnp.zeros((frames, sent.shape[1]), F32)
    for d in range(out_ref.shape[0]):
        block = got_ref[d, 0] - 1
        safe = jnp.clip(block, 0, blocks - 1)
        grads = rows32[pl.ds(pl.multiple_of(safe * frames, frames), frames), :]
        grads = jnp.where(block >= 0, grads, none)
        out_ref[d] = jnp.concatenate([grads, sent[d * frames : (d + 1) * frames]], axis=0).astype(BF)


def pack(rows, channels):
    r, w = rows.shape
    parts, start = [], 0
    while start < w:
        lanes = min(1 << ((w - start).bit_length() - 1), channels)
        each = r * lanes // channels
        parts.append(
            jnp.concatenate(
                [rows[g * each : (g + 1) * each, start : start + lanes] for g in range(r // each)], axis=1
            )
        )
        start += lanes
    return jnp.concatenate(parts, axis=0)


def unpack(packed, r, w):
    channels = packed.shape[1]
    parts, start, at = [], 0, 0
    while start < w:
        lanes = min(1 << ((w - start).bit_length() - 1), channels)
        each = r * lanes // channels
        block = packed[at : at + each]
        parts.append(
            jnp.concatenate([block[:, g * lanes : (g + 1) * lanes] for g in range(r // each)], axis=0)
        )
        start += lanes
        at += each
    return jnp.concatenate(parts, axis=1)


def gradient_kernel(me_ref, *refs, n1, n2, owned, near, far, frames):
    side_refs, column_refs = refs[:near], refs[near : 2 * near]
    weight_ref, mine_ref, packed_ref, own_ref = refs[2 * near : 2 * near + 4]
    out_refs, held = refs[2 * near + 4 : -1], refs[-1]
    start = n1 + n2
    rows = far * owned
    other = column_refs[near // 4][2 * rows :][:, : mine_ref.shape[1]]
    channels, seq = weight_ref.shape[1], packed_ref.shape[1]
    dp_count = (side_refs[0].shape[0] - start - 8) // (1 + frames)
    row = lax.broadcasted_iota(jnp.int32, (dp_count * frames, seq), 0)
    lane = lax.broadcasted_iota(jnp.int32, (dp_count * frames, seq), 1)
    block = (lax.div(lane, frames) + 1).astype(F32)
    same = lax.rem(lane, frames) == lax.rem(row, frames)
    shards = []
    for first_k in range(0, near, near // 2):
        picks, sent = [], []
        for k in range(first_k, first_k + near // 2):
            tail = side_refs[k][start:, :].astype(F32)
            ids = tail[8 : 8 + dp_count, :seq]
            ids = jnp.broadcast_to(ids[:, None, :], (dp_count, frames, seq)).reshape(dp_count * frames, seq)
            picks.append(jnp.where(jnp.logical_and(same, ids == block), 1.0, 0.0))
            rows_of = tail[8 + dp_count :]
            if first_k:
                rows_of = jnp.concatenate([rows_of[:, : channels // 2], rows_of[:, channels // 2 :]], axis=0)
            sent.append(rows_of.astype(BF))
        pick = jnp.concatenate(picks, axis=0).T.astype(BF)
        shards.append(dot(pick, jnp.concatenate(sent, axis=0)))
    packed_ref[...] = dot_nt(weight_ref[...], shards[0].astype(BF)).astype(BF)
    turn = (((0,), (1,)), ((), ()))
    partial = lax.dot_general(shards[0].astype(BF), mine_ref[...], turn, preferred_element_type=F32)
    theirs = lax.dot_general(shards[1].astype(BF), other, turn, preferred_element_type=F32)
    each = channels // dp_count
    depth = -(-(n1 + n2) // 128) * 128
    lane = lax.broadcasted_iota(jnp.int32, (rows, depth), 1)
    of_first, of_second, factors, sums = [], [], [], 0.0
    for k in range(near):
        at = k % 2 * rows
        side = column_refs[near // 2 * (k % 2) + k // 2][at : at + rows][:, :depth].astype(F32)
        of_first.append(jnp.where(lane < n1, side, 0.0).astype(BF))
        of_second.append(jnp.where(jnp.logical_and(lane >= n1, lane < start), side, 0.0).astype(BF))
        factors.append(side_refs[k][:depth, :])
        tail = side_refs[k][start : start + 16, :].astype(F32)
        sums += tail[0:4] + tail[4:8]
    factors = jnp.concatenate(factors, axis=0)
    first = dot(jnp.concatenate(of_first, axis=1), factors)
    second = dot(jnp.concatenate(of_second, axis=1), factors)
    high = sums.astype(BF).astype(F32)
    each = channels // dp_count
    for z in range(far):
        low_rows = partial[2 * z * each : (2 * z + 1) * each]
        high_rows = partial[(2 * z + 1) * each : (2 * z + 2) * each]
        held[z] = jnp.concatenate(
            [
                first[z * owned : (z + 1) * owned],
                second[z * owned : (z + 1) * owned],
                high,
                sums - high,
                pack(
                    jnp.where(me_ref[3] == 0, low_rows, high_rows) + theirs[z * each : (z + 1) * each], channels
                ),
            ],
            axis=0,
        )
    own_ref[...] = held[me_ref[2]]
    for f in range(1, far):
        out_refs[f - 1][...] = held[me_ref[2] ^ f].astype(BF)


def norm_back(grad, slope_ref, hat_ref, scale, gain):
    pre = grad * slope_ref[...]
    hat = hat_ref[...]
    by_hat = pre * hat
    inner = pre * gain
    average = jnp.mean(inner, axis=-1, keepdims=True)
    along = jnp.mean(inner * hat, axis=-1, keepdims=True)
    back = (inner - average - hat * along) * scale
    return (
        back.astype(BF),
        jnp.sum(by_hat, axis=0, keepdims=True),
        jnp.sum(pre, axis=0, keepdims=True),
    )


def back_kernel(slots_ref, got_ref, state_ref, weight_ref, out_ref, half_ref, *, frames):
    channels = weight_ref.shape[2]
    slope1_ref, slope2_ref, hat1_ref, hat2_ref, aux_ref, gain_ref = state_views(state_ref)
    slots = slots_ref[...]
    lanes = channels // 4
    scale1 = jnp.concatenate([aux_ref[:, 0:1], aux_ref[:, lanes : lanes + 1]], axis=0)
    scale2 = aux_ref[:, 2 * lanes : 2 * lanes + 1]
    n2 = aux_ref.shape[0]
    place = lax.broadcasted_iota(jnp.int32, (n2, slots.shape[0]), 1).astype(F32)
    pick = jnp.where(place == aux_ref[:, 3 * lanes : 3 * lanes + 1], 1.0, 0.0).astype(BF)
    grads = dot(pick, slots)
    second, gain2, shift2 = norm_back(grads, slope2_ref, hat2_ref, scale2, gain_ref[1:2, :])
    hidden = jnp.concatenate(
        [
            dot_nt(second, weight_ref[1, :channels, :]),
            dot_nt(second, weight_ref[1, channels:, :]),
        ],
        axis=0,
    )
    hidden = hidden.astype(BF).astype(F32)
    first, gain1, shift1 = norm_back(hidden, slope1_ref, hat1_ref, scale1, gain_ref[0:1, :])
    sums = jnp.concatenate([gain1, shift1, gain2, shift2], axis=0)
    high = sums.astype(BF).astype(F32)
    ids = got_ref[...].astype(F32)
    slots32 = slots.astype(F32)
    rows = [high, sums - high, jnp.concatenate([ids] * (channels // ids.shape[1]), axis=1)]
    sent = jnp.concatenate(
        [
            slots32[(2 * d + 1) * frames : (2 * d + 2) * frames]
            for d in range(slots.shape[0] // (2 * frames))
        ],
        axis=0,
    )
    dp_count = ids.shape[0]
    each = channels // dp_count
    odd_here = lax.rem(lax.axis_index("dp"), 2) == 1
    half = jnp.concatenate(
        [
            jnp.where(
                odd_here,
                sent[:, 2 * z * each : (2 * z + 1) * each],
                sent[:, (2 * z + 1) * each : (2 * z + 2) * each],
            )
            for z in range(dp_count // 2)
        ],
        axis=1,
    )
    middle = half.shape[0] // 2
    half = jnp.concatenate([half[:middle], half[middle:]], axis=1)
    n1, n2 = first.shape[0], second.shape[0]
    out_ref[:n1, :] = first
    out_ref[n1 : n1 + n2, :] = second
    out_ref[n1 + n2 :, :] = jnp.concatenate(rows + [sent], axis=0).astype(BF)
    half_ref[:n1, :] = first
    half_ref[n1 : n1 + n2, :] = second
    half_ref[n1 + n2 :, :] = jnp.concatenate(rows + [half], axis=0).astype(BF)


def input_kernel(me_ref, grad_ref, weight_ref, out_ref, *, pairs, frames):
    channels = weight_ref.shape[2]
    n1 = 2 * pairs * frames
    first = grad_ref[:n1, :]
    rows = jnp.concatenate(
        [dot_nt(first, weight_ref[0, :channels, :]), dot_nt(first, weight_ref[0, channels:, :])],
        axis=0,
    ).astype(BF)
    row = lax.broadcasted_iota(jnp.int32, (1, 2 * n1), 1)
    source = source_of(row, me_ref, pairs, frames)
    place = lax.broadcasted_iota(jnp.int32, (out_ref.shape[0], 2 * n1), 0)
    pick = jnp.where(place == source, 1.0, 0.0).astype(BF)
    out_ref[...] = dot(pick, rows).astype(BF)


def last_kernel(me_ref, *refs, owned, far):
    conv_ref, norm_ref, proj_ref = refs[far:]
    total = refs[0][...]
    for f in range(1, far):
        total += refs[f][...].astype(F32)
    conv_ref[0] = total[:owned]
    conv_ref[1] = total[owned : 2 * owned]
    proj_ref[...] = unpack(total[2 * owned + 8 :], *proj_ref.shape)
    channels = total.shape[1]
    sums = total[2 * owned : 2 * owned + 4] + total[2 * owned + 4 : 2 * owned + 8]
    start = me_ref[0] * owned
    later = start >= channels
    lines = jnp.concatenate(
        [jnp.where(later, sums[2 * k + 1 : 2 * k + 2], sums[2 * k : 2 * k + 1]) for k in range(2)]
        + [jnp.zeros((6, channels), F32)],
        axis=0,
    )
    start = jnp.where(later, start - channels, start)
    lines = pltpu.roll(lines, lax.rem(channels - start, channels), 1)
    norm_ref[...] = lines[:2, :owned]


def local(
    features, lengths, dests, offsets, conv_weight, norm_gain, norm_shift, proj_weight, grad_packed
):
    utt_count, positions, channels = features.shape
    frames = positions // 4
    pairs = utt_count // 2
    dp_count = lax.axis_size("dp")
    mp_count = lax.axis_size("mp")
    seq = grad_packed.shape[0]
    width = grad_packed.shape[1]
    owned = 2 * channels // (dp_count * mp_count)
    n1, n2 = 2 * pairs * frames, pairs * frames
    near, far = 2 * mp_count, dp_count // 2
    everyone = ("dp", "mp")

    def swap(x, mask):
        return lax.ppermute(x, everyone, [(i, i ^ mask) for i in range(dp_count * mp_count)])

    bits = [1 << b for b in range(mp_count.bit_length() - 1)][::-1]
    me, index, grad_rows = call(
        functools.partial(start_kernel, pairs=pairs, frames=frames, mp_count=mp_count),
        [
            shape(4 + 6 * pairs, kind=jnp.int32),
            shape(dp_count, 128, kind=jnp.int32),
            shape(seq, channels),
        ],
        (proj_weight.T, grad_packed.T, lengths, dests, offsets),
        fetched=5,
        to_scalars=1,
        flops=2 * seq * width * channels,
        scratch=[
            pltpu.VMEM((width, channels), BF),
            pltpu.VMEM((width, seq), BF),
            pltpu.SMEM(lengths.shape, jnp.int32),
            pltpu.SMEM(dests.shape, jnp.int32),
            pltpu.SMEM(offsets.shape, jnp.int32),
            pltpu.SemaphoreType.DMA((5,)),
        ],
        mebibytes=56,
    )
    feat = features.reshape(utt_count * positions, channels)
    got_index = lax.all_to_all(index, "dp", split_axis=0, concat_axis=0, tiled=True)

    wide = max(-(-(n1 + n2) // 128) * 128, seq)
    cotangent = grad_packed.T
    tall = (2 * channels, channels)
    made = call(
        functools.partial(
            forward_kernel, pairs=pairs, frames=frames, far=far, near=near, owned=owned
        ),
        [
            shape(*me.shape, kind=jnp.int32),
            shape(dp_count * frames, channels),
            shape(7 * n2 + 8, channels, kind=F32),
        ]
        + [
            shape(2 * far * owned + (width if 2 * k == mp_count else 0), wide)
            for k in range(near // 2)
        ],
        (me, feat, norm_gain, norm_shift, conv_weight, cotangent),
        scalars=1,
        fetched=5,
        to_scalars=1,
        flops=10**10,
        scratch=[
            pltpu.VMEM(feat.shape, BF),
            pltpu.VMEM(norm_gain.shape, F32),
            pltpu.VMEM(norm_shift.shape, F32),
            pltpu.VMEM(tall, BF),
            pltpu.VMEM(tall, BF),
            pltpu.VMEM((2 * channels, wide), F32),
            pltpu.SemaphoreType.DMA((6,)),
        ],
        mebibytes=56,
    )
    me, pair_frames, state = made[:3]
    in_sides = [swap(side, 2 * k) if k else side for k, side in enumerate(made[3:])]

    for mask in bits[:0:-1]:
        grad_rows = (grad_rows.astype(F32) + swap(grad_rows, mask).astype(F32)).astype(BF)
    other_rows = swap(grad_rows, bits[0])

    sent = call(
        functools.partial(send_kernel, frames=frames),
        shape(dp_count, 2 * frames, channels),
        (got_index, grad_rows, other_rows, pair_frames),
        scalars=1,
        scratch=[pltpu.VMEM((seq, channels), F32)],
    )
    slots = lax.all_to_all(sent, "dp", split_axis=0, concat_axis=0, tiled=True)

    rows_sent = n1 + n2 + 8 + dp_count * (1 + frames)
    grads, half_grads = call(
        functools.partial(back_kernel, frames=frames),
        [shape(rows_sent, channels), shape(rows_sent - dp_count * frames // 2, channels)],
        (slots.reshape(-1, channels), got_index, state, conv_weight),
        flops=2 * n2 * 2 * channels * channels,
    )
    by_mask = {0: grads}
    for mask in range(2, near, 2):
        leaving = grads if mask < mp_count else half_grads
        if mask == mp_count:
            leaving, *in_sides[1 : near // 2] = lax.optimization_barrier(
                (leaving, *in_sides[1 : near // 2])
            )
        by_mask[mask] = swap(leaving, mask)
    in_sides += [swap(side, 1) for side in in_sides]
    for mask in range(0, near, 2):
        by_mask[mask + 1] = swap(by_mask[mask], 1)

    per_dp = channels // dp_count
    packed_rows = per_dp * width // channels
    sides = tuple(by_mask[k] for k in range(near))
    rows_out = 2 * owned + 8 + packed_rows
    packed, *parts = call(
        functools.partial(
            gradient_kernel, n1=n1, n2=n2, owned=owned, near=near, far=far, frames=frames
        ),
        [shape(width, seq), shape(rows_out, channels, kind=F32)]
        + [shape(rows_out, channels)] * (far - 1),
        (me, *sides, *in_sides, proj_weight.T, cotangent),
        scalars=1,
        flops=2 * (n1 + n2) * 2 * channels * channels,
        scratch=[pltpu.VMEM((far, rows_out, channels), F32)],
    )

    grad_features = call(
        functools.partial(input_kernel, pairs=pairs, frames=frames),
        shape(utt_count * positions, channels),
        (me, grads, conv_weight),
        scalars=1,
        flops=2 * n1 * 2 * channels * channels,
    ).reshape(utt_count, positions, channels)

    got = [swap(part, near * f) if f else part for f, part in enumerate(parts)]
    grad_conv, grad_norm, grad_proj = call(
        functools.partial(last_kernel, owned=owned, far=far),
        [
            shape(2, owned, channels, kind=F32),
            shape(2, owned, kind=F32),
            shape(per_dp, width, kind=F32),
        ],
        (me, *got),
        scalars=1,
    )
    return (packed.T, grad_features, grad_conv, grad_norm, grad_proj)


def solution(mesh):
    return jax.shard_map(
        local,
        mesh=mesh,
        in_specs=(
            P(("dp", "mp"), None, None),
            P(("dp", "mp")),
            P(("dp", "mp")),
            P(("dp", "mp")),
            P(),
            P(),
            P(),
            P(None, "mp"),
            P("dp", "mp"),
        ),
        out_specs=(
            P("dp", "mp"),
            P(("dp", "mp"), None, None),
            P(None, ("dp", "mp"), None),
            P(None, ("dp", "mp")),
            P("dp", "mp"),
        ),
        check_vma=False,
    )
```

```python
import functools
import math

import jax
import jax.numpy as jnp
from jax import lax
from jax.experimental import pallas as pl
from jax.experimental.pallas import tpu as pltpu
from jax.sharding import PartitionSpec as P

epsilon = 1e-05
BF = jnp.bfloat16
F32 = jnp.float32
VMEM = pltpu.VMEM
SMEM = pltpu.SMEM


def call(body, out, args, scalars=0, fetched=0, flops=0, scratch=(), mebibytes=14, to_scalars=0):
    specs = [
        pl.BlockSpec(memory_space=SMEM if i < scalars else pl.ANY if i < scalars + fetched else VMEM)
        for i in range(len(args))
    ]
    many = isinstance(out, (list, tuple))
    moved = sum(a.size * a.dtype.itemsize for a in args)
    return pl.pallas_call(
        body,
        out_shape=out,
        in_specs=specs,
        out_specs=[
            pl.BlockSpec(memory_space=SMEM if i < to_scalars else VMEM) for i in range(len(out))
        ]
        if many
        else pl.BlockSpec(memory_space=VMEM),
        scratch_shapes=list(scratch),
        compiler_params=pltpu.CompilerParams(vmem_limit_bytes=mebibytes * 2**20),
        cost_estimate=pl.CostEstimate(flops=flops, bytes_accessed=moved, transcendentals=0),
    )(*args)


def shape(*dims, kind=BF):
    return jax.ShapeDtypeStruct(dims, kind)


def dot(a, b):
    return jnp.dot(a, b, preferred_element_type=F32)


def dot_nt(a, b):
    return lax.dot_general(a, b, (((1,), (1,)), ((), ())), preferred_element_type=F32)


def norm_parts(pre):
    average = jnp.mean(pre, axis=-1, keepdims=True)
    centred = pre - average
    spread = jnp.mean(centred * centred, axis=-1, keepdims=True)
    scale = lax.rsqrt(spread + epsilon)
    return centred * scale, scale


def gelu_parts(value):
    half = 0.5 * (1.0 + lax.erf(value * math.sqrt(0.5)))
    density = jnp.exp(-0.5 * value * value) * (1.0 / math.sqrt(2.0 * math.pi))
    return value * half, half + value * density


def source_of(row, me_ref, pairs, frames):
    part = lax.div(row, pairs * frames)
    inner = lax.rem(row, pairs * frames)
    pair = lax.div(inner, frames)
    t = lax.rem(inner, frames)
    first = jnp.zeros_like(row)
    for p in range(pairs):
        first = jnp.where(pair == p, me_ref[4 + 2 * p], first)
    off = jnp.where(part == 1, 2, jnp.where(part == 2, 1, part))
    t_from = jnp.where(t < first, t, t + frames - first)
    return pair * (8 * frames) + 4 * t_from + off


def start_kernel(
    proj_hbm, cotangent_hbm, lengths_hbm, dests_hbm, offsets_hbm, me_ref, index_ref, rows_ref,
    proj_ref, cotangent_ref, lengths_ref, dests_ref, offsets_ref, copied, *, pairs, frames, mp_count
):
    sources = (proj_hbm, cotangent_hbm, lengths_hbm, dests_hbm, offsets_hbm)
    targets = (proj_ref, cotangent_ref, lengths_ref, dests_ref, offsets_ref)
    copies = [
        pltpu.make_async_copy(source, target, copied.at[i])
        for i, (source, target) in enumerate(zip(sources, targets))
    ]
    for copy in copies:
        copy.start()
    for copy in copies[2:]:
        copy.wait()
    at_dp, at_mp = lax.axis_index("dp"), lax.axis_index("mp")
    me_ref[0] = at_dp * mp_count + at_mp
    me_ref[1] = lax.rem(at_dp, 2) * mp_count + at_mp
    me_ref[2] = lax.div(at_dp, 2)
    me_ref[3] = lax.rem(at_dp, 2)
    for i in range(2 * pairs):
        me_ref[4 + i] = lengths_ref[i]
        me_ref[4 + 2 * pairs + i] = dests_ref[i]
        me_ref[4 + 4 * pairs + i] = offsets_ref[i]
    shard = lax.broadcasted_iota(jnp.int32, index_ref.shape, 0)
    value = jnp.zeros(index_ref.shape, jnp.int32)
    for p in range(pairs):
        block = lax.div(offsets_ref[2 * p], frames)
        value = jnp.where(shard == dests_ref[2 * p], block + 1, value)
    index_ref[...] = value
    copies[0].wait()
    copies[1].wait()
    rows_ref[...] = lax.dot_general(
        cotangent_ref[...], proj_ref[...], (((0,), (0,)), ((), ())), preferred_element_type=F32
    ).astype(BF)


def state_views(state_ref):
    part = (state_ref.shape[0] - 8) // 7
    spans = ((0, 2), (2, 1), (3, 2), (5, 1), (6, 1))
    return [state_ref.at[a * part : (a + n) * part] for a, n in spans] + [state_ref.at[7 * part :]]


def forward_kernel(me_ref, *refs, pairs, frames, far, near, owned):
    weight_ref, cotangent_hbm = refs[3:5]
    rest, held, in_turned, copied = refs[5:-7], refs[-7:-2], refs[-2], refs[-1]
    with_cotangent = rest[3 + near // 4]
    own_rows = 2 * far * owned
    tail = with_cotangent.at[own_rows:, : cotangent_hbm.shape[1]]
    sources = refs[:3] + (weight_ref.at[0], weight_ref.at[1], cotangent_hbm)
    targets = held + (tail,)
    copies = [
        pltpu.make_async_copy(source, target, copied.at[i])
        for i, (source, target) in enumerate(zip(sources, targets))
    ]
    for copy in copies:
        copy.start()
    feat_ref, gain_ref, shift_ref, first_ref, second_ref = held
    later_ref, frames_ref, state_ref = rest[:3]
    turned_refs = rest[3:]
    for i in range(me_ref.shape[0]):
        later_ref[i] = me_ref[i]
    slope1_ref, slope2_ref, hat1_ref, hat2_ref, aux_ref, gain_at = state_views(state_ref)
    copies[0].wait()
    channels = feat_ref.shape[1]
    n2 = pairs * frames
    row = lax.broadcasted_iota(jnp.int32, (4 * n2, 1), 0)
    source = source_of(row, me_ref, pairs, frames)
    place = lax.broadcasted_iota(jnp.int32, (4 * n2, feat_ref.shape[0]), 1)
    pick = jnp.where(place == source, 1.0, 0.0).astype(BF)
    chosen32 = dot(pick, feat_ref[...])
    chosen = chosen32.astype(BF)
    for copy in copies[1:4]:
        copy.wait()
    even, odd = chosen[: 2 * n2], chosen[2 * n2 :]
    first = dot(even, first_ref[:channels, :]) + dot(odd, first_ref[channels:, :])
    hat, scale = norm_parts(first)
    hidden, slope = gelu_parts(hat * gain_ref[0:1, :] + shift_ref[0:1, :])
    slope1_ref[...] = slope
    hat1_ref[...] = hat
    aux = [scale[:n2], scale[n2:]]
    hidden = hidden.astype(BF)
    hidden32 = hidden.astype(F32)
    copies[4].wait()
    second = dot(hidden[:n2], second_ref[:channels, :]) + dot(hidden[n2:], second_ref[channels:, :])
    hat, scale = norm_parts(second)
    made, slope = gelu_parts(hat * gain_ref[1:2, :] + shift_ref[1:2, :])
    slope2_ref[...] = slope
    hat2_ref[...] = hat
    aux.append(scale)
    none = jnp.zeros((frames, channels), F32)
    sent = []
    for d in range(frames_ref.shape[0] // frames):
        rows = none
        for p in range(pairs):
            rows = jnp.where(me_ref[4 + 2 * pairs + 2 * p] == d, made[p * frames : (p + 1) * frames], rows)
        sent.append(rows)
    frames_ref[...] = jnp.concatenate(sent, axis=0).astype(BF)
    row = lax.broadcasted_iota(jnp.int32, (n2, 1), 0)
    slot = jnp.zeros_like(row)
    for p in range(pairs):
        slot = jnp.where(lax.div(row, frames) == p, me_ref[4 + 2 * pairs + 2 * p], slot)
    slot = slot * (2 * frames) + lax.rem(row, frames)
    aux.append(slot.astype(F32))
    aux_ref[...] = jnp.concatenate([jnp.broadcast_to(a, (n2, channels // 4)) for a in aux], axis=1)
    gain_at[...] = jnp.concatenate([gain_ref[...], jnp.zeros((6, channels), F32)], axis=0)
    wide = in_turned.shape[1]
    fill = [jnp.zeros((wide - 3 * n2, channels), F32)] if wide > 3 * n2 else []
    for tap in range(2):
        stacked = jnp.concatenate(
            [chosen32[2 * n2 * tap : 2 * n2 * (tap + 1)], hidden32[n2 * tap : n2 * (tap + 1)]] + fill,
            axis=0,
        )
        in_turned[channels * tap : channels * (tap + 1), :] = stacked.T
    at = me_ref[1]
    for k, turned_ref in enumerate(turned_refs):
        turned_ref[:own_rows, :] = jnp.concatenate(
            [
                in_turned[pl.ds(pl.multiple_of((z * near + (at ^ (2 * k + c))) * owned, owned), owned), :]
                for c in range(2)
                for z in range(far)
            ],
            axis=0,
        ).astype(BF)
    copies[5].wait()


def send_kernel(got_ref, mine_ref, other_ref, sent_ref, out_ref, rows32, *, frames):
    rows32[...] = mine_ref[...].astype(F32) + other_ref[...].astype(F32)
    blocks = rows32.shape[0] // frames
    sent = sent_ref[...].astype(F32)
    none = jnp.zeros((frames, sent.shape[1]), F32)
    for d in range(out_ref.shape[0]):
        block = got_ref[d, 0] - 1
        safe = jnp.clip(block, 0, blocks - 1)
        grads = rows32[pl.ds(pl.multiple_of(safe * frames, frames), frames), :]
        grads = jnp.where(block >= 0, grads, none)
        out_ref[d] = jnp.concatenate([grads, sent[d * frames : (d + 1) * frames]], axis=0).astype(BF)


def pack(rows, channels):
    r, w = rows.shape
    parts, start = [], 0
    while start < w:
        lanes = min(1 << ((w - start).bit_length() - 1), channels)
        each = r * lanes // channels
        parts.append(
            jnp.concatenate(
                [rows[g * each : (g + 1) * each, start : start + lanes] for g in range(r // each)], axis=1
            )
        )
        start += lanes
    return jnp.concatenate(parts, axis=0)


def unpack(packed, r, w):
    channels = packed.shape[1]
    parts, start, at = [], 0, 0
    while start < w:
        lanes = min(1 << ((w - start).bit_length() - 1), channels)
        each = r * lanes // channels
        block = packed[at : at + each]
        parts.append(
            jnp.concatenate([block[:, g * lanes : (g + 1) * lanes] for g in range(r // each)], axis=0)
        )
        start += lanes
        at += each
    return jnp.concatenate(parts, axis=1)


def gradient_kernel(me_ref, *refs, n1, n2, owned, near, far, frames):
    side_refs, column_refs = refs[:near], refs[near : 2 * near]
    weight_ref, mine_ref, packed_ref, own_ref = refs[2 * near : 2 * near + 4]
    out_refs, held = refs[2 * near + 4 : -1], refs[-1]
    start = n1 + n2
    rows = far * owned
    other = column_refs[near // 4][2 * rows :][:, : mine_ref.shape[1]]
    channels, seq = weight_ref.shape[1], packed_ref.shape[1]
    dp_count = (side_refs[0].shape[0] - start - 8) // (1 + frames)
    row = lax.broadcasted_iota(jnp.int32, (dp_count * frames, seq), 0)
    lane = lax.broadcasted_iota(jnp.int32, (dp_count * frames, seq), 1)
    block = (lax.div(lane, frames) + 1).astype(F32)
    same = lax.rem(lane, frames) == lax.rem(row, frames)
    shards = []
    for first_k in range(0, near, near // 2):
        picks, sent = [], []
        for k in range(first_k, first_k + near // 2):
            tail = side_refs[k][start:, :].astype(F32)
            ids = tail[8 : 8 + dp_count, :seq]
            ids = jnp.broadcast_to(ids[:, None, :], (dp_count, frames, seq)).reshape(dp_count * frames, seq)
            picks.append(jnp.where(jnp.logical_and(same, ids == block), 1.0, 0.0))
            rows_of = tail[8 + dp_count :]
            if first_k:
                rows_of = jnp.concatenate([rows_of[:, : channels // 2], rows_of[:, channels // 2 :]], axis=0)
            sent.append(rows_of.astype(BF))
        pick = jnp.concatenate(picks, axis=0).T.astype(BF)
        shards.append(dot(pick, jnp.concatenate(sent, axis=0)))
    packed_ref[...] = dot_nt(weight_ref[...], shards[0].astype(BF)).astype(BF)
    turn = (((0,), (1,)), ((), ()))
    partial = lax.dot_general(shards[0].astype(BF), mine_ref[...], turn, preferred_element_type=F32)
    theirs = lax.dot_general(shards[1].astype(BF), other, turn, preferred_element_type=F32)
    each = channels // dp_count
    depth = -(-(n1 + n2) // 128) * 128
    lane = lax.broadcasted_iota(jnp.int32, (rows, depth), 1)
    of_first, of_second, factors, sums = [], [], [], 0.0
    for k in range(near):
        at = k % 2 * rows
        side = column_refs[near // 2 * (k % 2) + k // 2][at : at + rows][:, :depth].astype(F32)
        of_first.append(jnp.where(lane < n1, side, 0.0).astype(BF))
        of_second.append(jnp.where(jnp.logical_and(lane >= n1, lane < start), side, 0.0).astype(BF))
        factors.append(side_refs[k][:depth, :])
        tail = side_refs[k][start : start + 16, :].astype(F32)
        sums += tail[0:4] + tail[4:8]
    factors = jnp.concatenate(factors, axis=0)
    first = dot(jnp.concatenate(of_first, axis=1), factors)
    second = dot(jnp.concatenate(of_second, axis=1), factors)
    high = sums.astype(BF).astype(F32)
    each = channels // dp_count
    for z in range(far):
        low_rows = partial[2 * z * each : (2 * z + 1) * each]
        high_rows = partial[(2 * z + 1) * each : (2 * z + 2) * each]
        held[z] = jnp.concatenate(
            [
                first[z * owned : (z + 1) * owned],
                second[z * owned : (z + 1) * owned],
                high,
                sums - high,
                pack(
                    jnp.where(me_ref[3] == 0, low_rows, high_rows) + theirs[z * each : (z + 1) * each], channels
                ),
            ],
            axis=0,
        )
    own_ref[...] = held[me_ref[2]]
    for f in range(1, far):
        out_refs[f - 1][...] = held[me_ref[2] ^ f].astype(BF)


def norm_back(grad, slope_ref, hat_ref, scale, gain):
    pre = grad * slope_ref[...]
    hat = hat_ref[...]
    by_hat = pre * hat
    inner = pre * gain
    average = jnp.mean(inner, axis=-1, keepdims=True)
    along = jnp.mean(inner * hat, axis=-1, keepdims=True)
    back = (inner - average - hat * along) * scale
    return (
        back.astype(BF),
        jnp.sum(by_hat, axis=0, keepdims=True),
        jnp.sum(pre, axis=0, keepdims=True),
    )


def back_kernel(slots_ref, got_ref, state_ref, weight_ref, out_ref, half_ref, *, frames):
    channels = weight_ref.shape[2]
    slope1_ref, slope2_ref, hat1_ref, hat2_ref, aux_ref, gain_ref = state_views(state_ref)
    slots = slots_ref[...]
    lanes = channels // 4
    scale1 = jnp.concatenate([aux_ref[:, 0:1], aux_ref[:, lanes : lanes + 1]], axis=0)
    scale2 = aux_ref[:, 2 * lanes : 2 * lanes + 1]
    n2 = aux_ref.shape[0]
    place = lax.broadcasted_iota(jnp.int32, (n2, slots.shape[0]), 1).astype(F32)
    pick = jnp.where(place == aux_ref[:, 3 * lanes : 3 * lanes + 1], 1.0, 0.0).astype(BF)
    grads = dot(pick, slots)
    second, gain2, shift2 = norm_back(grads, slope2_ref, hat2_ref, scale2, gain_ref[1:2, :])
    hidden = jnp.concatenate(
        [
            dot_nt(second, weight_ref[1, :channels, :]),
            dot_nt(second, weight_ref[1, channels:, :]),
        ],
        axis=0,
    )
    hidden = hidden.astype(BF).astype(F32)
    first, gain1, shift1 = norm_back(hidden, slope1_ref, hat1_ref, scale1, gain_ref[0:1, :])
    sums = jnp.concatenate([gain1, shift1, gain2, shift2], axis=0)
    high = sums.astype(BF).astype(F32)
    ids = got_ref[...].astype(F32)
    slots32 = slots.astype(F32)
    rows = [high, sums - high, jnp.concatenate([ids] * (channels // ids.shape[1]), axis=1)]
    sent = jnp.concatenate(
        [
            slots32[(2 * d + 1) * frames : (2 * d + 2) * frames]
            for d in range(slots.shape[0] // (2 * frames))
        ],
        axis=0,
    )
    dp_count = ids.shape[0]
    each = channels // dp_count
    odd_here = lax.rem(lax.axis_index("dp"), 2) == 1
    half = jnp.concatenate(
        [
            jnp.where(
                odd_here,
                sent[:, 2 * z * each : (2 * z + 1) * each],
                sent[:, (2 * z + 1) * each : (2 * z + 2) * each],
            )
            for z in range(dp_count // 2)
        ],
        axis=1,
    )
    middle = half.shape[0] // 2
    half = jnp.concatenate([half[:middle], half[middle:]], axis=1)
    n1, n2 = first.shape[0], second.shape[0]
    out_ref[:n1, :] = first
    out_ref[n1 : n1 + n2, :] = second
    out_ref[n1 + n2 :, :] = jnp.concatenate(rows + [sent], axis=0).astype(BF)
    half_ref[:n1, :] = first
    half_ref[n1 : n1 + n2, :] = second
    half_ref[n1 + n2 :, :] = jnp.concatenate(rows + [half], axis=0).astype(BF)


def input_kernel(me_ref, grad_ref, weight_ref, out_ref, *, pairs, frames):
    channels = weight_ref.shape[2]
    n1 = 2 * pairs * frames
    first = grad_ref[:n1, :]
    rows = jnp.concatenate(
        [dot_nt(first, weight_ref[0, :channels, :]), dot_nt(first, weight_ref[0, channels:, :])],
        axis=0,
    ).astype(BF)
    row = lax.broadcasted_iota(jnp.int32, (1, 2 * n1), 1)
    source = source_of(row, me_ref, pairs, frames)
    place = lax.broadcasted_iota(jnp.int32, (out_ref.shape[0], 2 * n1), 0)
    pick = jnp.where(place == source, 1.0, 0.0).astype(BF)
    out_ref[...] = dot(pick, rows).astype(BF)


def last_kernel(me_ref, *refs, owned, far):
    conv_ref, norm_ref, proj_ref = refs[far:]
    total = refs[0][...]
    for f in range(1, far):
        total += refs[f][...].astype(F32)
    conv_ref[0] = total[:owned]
    conv_ref[1] = total[owned : 2 * owned]
    proj_ref[...] = unpack(total[2 * owned + 8 :], *proj_ref.shape)
    channels = total.shape[1]
    sums = total[2 * owned : 2 * owned + 4] + total[2 * owned + 4 : 2 * owned + 8]
    start = me_ref[0] * owned
    later = start >= channels
    lines = jnp.concatenate(
        [jnp.where(later, sums[2 * k + 1 : 2 * k + 2], sums[2 * k : 2 * k + 1]) for k in range(2)]
        + [jnp.zeros((6, channels), F32)],
        axis=0,
    )
    start = jnp.where(later, start - channels, start)
    lines = pltpu.roll(lines, lax.rem(channels - start, channels), 1)
    norm_ref[...] = lines[:2, :owned]


def local(
    features, lengths, dests, offsets, conv_weight, norm_gain, norm_shift, proj_weight, grad_packed
):
    utt_count, positions, channels = features.shape
    frames = positions // 4
    pairs = utt_count // 2
    dp_count = lax.axis_size("dp")
    mp_count = lax.axis_size("mp")
    seq = grad_packed.shape[0]
    width = grad_packed.shape[1]
    owned = 2 * channels // (dp_count * mp_count)
    n1, n2 = 2 * pairs * frames, pairs * frames
    near, far = 2 * mp_count, dp_count // 2
    everyone = ("dp", "mp")

    def swap(x, mask):
        return lax.ppermute(x, everyone, [(i, i ^ mask) for i in range(dp_count * mp_count)])

    bits = [1 << b for b in range(mp_count.bit_length() - 1)][::-1]
    me, index, grad_rows = call(
        functools.partial(start_kernel, pairs=pairs, frames=frames, mp_count=mp_count),
        [
            shape(4 + 6 * pairs, kind=jnp.int32),
            shape(dp_count, 128, kind=jnp.int32),
            shape(seq, channels),
        ],
        (proj_weight.T, grad_packed.T, lengths, dests, offsets),
        fetched=5,
        to_scalars=1,
        flops=2 * seq * width * channels,
        scratch=[
            pltpu.VMEM((width, channels), BF),
            pltpu.VMEM((width, seq), BF),
            pltpu.SMEM(lengths.shape, jnp.int32),
            pltpu.SMEM(dests.shape, jnp.int32),
            pltpu.SMEM(offsets.shape, jnp.int32),
            pltpu.SemaphoreType.DMA((5,)),
        ],
        mebibytes=56,
    )
    feat = features.reshape(utt_count * positions, channels)
    got_index = lax.all_to_all(index, "dp", split_axis=0, concat_axis=0, tiled=True)

    wide = max(-(-(n1 + n2) // 128) * 128, seq)
    cotangent = grad_packed.T
    tall = (2 * channels, channels)
    made = call(
        functools.partial(
            forward_kernel, pairs=pairs, frames=frames, far=far, near=near, owned=owned
        ),
        [
            shape(*me.shape, kind=jnp.int32),
            shape(dp_count * frames, channels),
            shape(7 * n2 + 8, channels, kind=F32),
        ]
        + [
            shape(2 * far * owned + (width if 2 * k == mp_count else 0), wide)
            for k in range(near // 2)
        ],
        (me, feat, norm_gain, norm_shift, conv_weight, cotangent),
        scalars=1,
        fetched=5,
        to_scalars=1,
        flops=10**10,
        scratch=[
            pltpu.VMEM(feat.shape, BF),
            pltpu.VMEM(norm_gain.shape, F32),
            pltpu.VMEM(norm_shift.shape, F32),
            pltpu.VMEM(tall, BF),
            pltpu.VMEM(tall, BF),
            pltpu.VMEM((2 * channels, wide), F32),
            pltpu.SemaphoreType.DMA((6,)),
        ],
        mebibytes=56,
    )
    me, pair_frames, state = made[:3]
    in_sides = [swap(side, 2 * k) if k else side for k, side in enumerate(made[3:])]

    for mask in bits[:0:-1]:
        grad_rows = (grad_rows.astype(F32) + swap(grad_rows, mask).astype(F32)).astype(BF)
    other_rows = swap(grad_rows, bits[0])

    sent = call(
        functools.partial(send_kernel, frames=frames),
        shape(dp_count, 2 * frames, channels),
        (got_index, grad_rows, other_rows, pair_frames),
        scalars=1,
        scratch=[pltpu.VMEM((seq, channels), F32)],
    )
    slots = lax.all_to_all(sent, "dp", split_axis=0, concat_axis=0, tiled=True)

    rows_sent = n1 + n2 + 8 + dp_count * (1 + frames)
    grads, half_grads = call(
        functools.partial(back_kernel, frames=frames),
        [shape(rows_sent, channels), shape(rows_sent - dp_count * frames // 2, channels)],
        (slots.reshape(-1, channels), got_index, state, conv_weight),
        flops=2 * n2 * 2 * channels * channels,
    )
    by_mask = {0: grads}
    for mask in range(2, near, 2):
        leaving = grads if mask < mp_count else half_grads
        if mask == mp_count:
            leaving, *in_sides[1 : near // 2] = lax.optimization_barrier(
                (leaving, *in_sides[1 : near // 2])
            )
        by_mask[mask] = swap(leaving, mask)
    in_sides += [swap(side, 1) for side in in_sides]
    for mask in range(0, near, 2):
        by_mask[mask + 1] = swap(by_mask[mask], 1)

    per_dp = channels // dp_count
    packed_rows = per_dp * width // channels
    sides = tuple(by_mask[k] for k in range(near))
    rows_out = 2 * owned + 8 + packed_rows
    packed, *parts = call(
        functools.partial(
            gradient_kernel, n1=n1, n2=n2, owned=owned, near=near, far=far, frames=frames
        ),
        [shape(width, seq), shape(rows_out, channels, kind=F32)]
        + [shape(rows_out, channels)] * (far - 1),
        (me, *sides, *in_sides, proj_weight.T, cotangent),
        scalars=1,
        flops=2 * (n1 + n2) * 2 * channels * channels,
        scratch=[pltpu.VMEM((far, rows_out, channels), F32)],
    )

    grad_features = call(
        functools.partial(input_kernel, pairs=pairs, frames=frames),
        shape(utt_count * positions, channels),
        (me, grads, conv_weight),
        scalars=1,
        flops=2 * n1 * 2 * channels * channels,
    ).reshape(utt_count, positions, channels)

    got = [swap(part, near * f) if f else part for f, part in enumerate(parts)]
    grad_conv, grad_norm, grad_proj = call(
        functools.partial(last_kernel, owned=owned, far=far),
        [
            shape(2, owned, channels, kind=F32),
            shape(2, owned, kind=F32),
            shape(per_dp, width, kind=F32),
        ],
        (me, *got),
        scalars=1,
    )
    return (packed.T, grad_features, grad_conv, grad_norm, grad_proj)


def solution(mesh):
    return jax.shard_map(
        local,
        mesh=mesh,
        in_specs=(
            P(("dp", "mp"), None, None),
            P(("dp", "mp")),
            P(("dp", "mp")),
            P(("dp", "mp")),
            P(),
            P(),
            P(),
            P(None, "mp"),
            P("dp", "mp"),
        ),
        out_specs=(
            P("dp", "mp"),
            P(("dp", "mp"), None, None),
            P(None, ("dp", "mp"), None),
            P(None, ("dp", "mp")),
            P("dp", "mp"),
        ),
        check_vma=False,
    )
```
